512 devices in a mesh: group: 16 (over z_lo, y), resp: 32 (over z_hi, x, core).
Axes of the slice: x: 4, y: 4, z: 16 (z_hi: 4, z_lo: 4; z = z_hi * 4 + z_lo), core: 2. Of those that a mesh axis runs over, the one named last changes fastest.
Arguments:
- queries: bfloat16 [16, 32, 128, 2048], P('group', 'resp'), may hold values from -6 to 6
- response_keys: bfloat16 [16, 32, 128, 512], P('group', 'resp'), may hold values from -6 to 6
- response_values: bfloat16 [16, 32, 128, 512], P('group', 'resp'), may hold values from -6 to 6
- prompt_key_rows: bfloat16 [16, 512, 512], P('group', 'resp'), may hold values from -6 to 6
- prompt_value_rows: bfloat16 [16, 512, 512], P('group', 'resp'), may hold values from -6 to 6
- upstream: bfloat16 [16, 32, 128, 2048], P('group', 'resp'), may hold values from -6 to 6
- rewards: float32 [16, 32], P('group', 'resp'), may hold values from 0 to 1
- lengths: int32 [16, 32], P('group', 'resp'), may hold values from 16 to 128
Outputs:
- grad_queries: bfloat16 [16, 32, 128, 2048], P('group', 'resp')
- grad_own_keys: bfloat16 [16, 32, 128, 512], P('group', 'resp')
- grad_own_values: bfloat16 [16, 32, 128, 512], P('group', 'resp')
- grad_prompt_keys: float32 [16, 512, 512], P('group', 'resp')
- grad_prompt_values: float32 [16, 512, 512], P('group', 'resp')
The draws below stay inside these ranges and needn't reach their ends.
All inputs are finite; a program needn't handle non-finite values.
Results may differ from the reference program's by a relative error of at most 0.012.
The reference program's roundings to bfloat16 on the way count: a program that leaves them out, or rounds other values in their place, can miss the bound.
Values may be sent and summed in bfloat16 or wider, within the bound.
A program may use at most 64 MiB of HBM per device.

```python
import jax
import jax.numpy as jnp
from jax import lax

QUERY_HEADS = 16
KEY_HEADS = 4
HEAD_SIZE = 128
RESPONSE_SLOTS = 128
QUERY_PER_KV = 4
PROMPT_TOKENS = 512
RESPONSE_COUNT = 32
PROMPT_GROUPS = 16


def draw_queries(key, part):
    key = jax.random.fold_in(key, 11)
    base_key = jax.random.fold_in(key, 0)
    array_shape = (PROMPT_GROUPS, RESPONSE_COUNT, RESPONSE_SLOTS, QUERY_HEADS * HEAD_SIZE)
    return jax.random.truncated_normal(base_key, -6.0, 6.0, array_shape, jnp.float32).astype(jnp.bfloat16)


def draw_prompt_key_rows(key, part):
    key = jax.random.fold_in(key, 23)
    array_shape = (PROMPT_GROUPS, PROMPT_TOKENS, KEY_HEADS * HEAD_SIZE)
    return jax.random.truncated_normal(key, -6.0, 6.0, array_shape, jnp.float32).astype(jnp.bfloat16)


def touch_ends(result, key, smallest, top_value):
    spot = [jax.random.randint(jax.random.fold_in(key, axis), (), 0, length) for axis, length in enumerate(result.shape)]
    main_axis = result.shape.index(max(result.shape))
    neighbour = spot[:main_axis] + [(spot[main_axis] + 1) % result.shape[main_axis]] + spot[main_axis + 1:]
    return result.at[tuple(spot)].set(smallest).at[tuple(neighbour)].set(top_value)


def block_levels(stream_key, shape, cuts, low, high):
    loudness = 1.0
    for axis_at, parts in cuts:
        draws = jax.random.uniform(jax.random.fold_in(jax.random.fold_in(stream_key, 6), axis_at), (parts,), jnp.float32, low / len(cuts), high / len(cuts))
        loudness = loudness * jnp.repeat(jnp.exp(draws), shape[axis_at] // parts).reshape((-1,) + (1,) * (len(shape) - 1 - axis_at))
    return loudness


def centred(stream_key, dims, scale, limit, cuts=(), dtype=jnp.bfloat16):
    drawn = scale * jax.random.normal(stream_key, dims, jnp.float32)
    if cuts:
        drawn = drawn * block_levels(stream_key, dims, cuts, -0.22, 0.18)
    return jnp.clip(drawn, -limit, limit).astype(dtype)


def setup_inputs(seed: int = 0) -> dict:
    key_list = jax.random.split(jax.random.key(seed), 9)
    return {
        "queries": draw_queries(jax.random.fold_in(key_list[8], 71), 0),
        "response_keys": centred(key_list[1], (PROMPT_GROUPS, RESPONSE_COUNT, RESPONSE_SLOTS, KEY_HEADS * HEAD_SIZE), 1.0, 6.0, ((0, 16), (1, 32))),
        "response_values": centred(key_list[2], (PROMPT_GROUPS, RESPONSE_COUNT, RESPONSE_SLOTS, KEY_HEADS * HEAD_SIZE), 1.0, 6.0, ((0, 16), (1, 32))),
        "prompt_key_rows": draw_prompt_key_rows(jax.random.fold_in(key_list[8], 71), 0),
        "prompt_value_rows": centred(key_list[4], (PROMPT_GROUPS, PROMPT_TOKENS, KEY_HEADS * HEAD_SIZE), 1.0, 6.0, ((0, 16), (1, 32))),
        "upstream": centred(key_list[5], (PROMPT_GROUPS, RESPONSE_COUNT, RESPONSE_SLOTS, QUERY_HEADS * HEAD_SIZE), 1.0, 6.0, ((0, 16), (1, 32))),
        "rewards": jnp.clip(1.0 * jax.random.uniform(key_list[6], (PROMPT_GROUPS, RESPONSE_COUNT), jnp.float32) ** block_levels(key_list[6], (PROMPT_GROUPS, RESPONSE_COUNT), ((0, 16), (1, 32)), -0.2, 0.2), 0.0, 1.0),
        "lengths": touch_ends(jax.random.randint(key_list[7], (PROMPT_GROUPS, RESPONSE_COUNT), RESPONSE_SLOTS // 8, RESPONSE_SLOTS + 1), jax.random.fold_in(key_list[7], 1), RESPONSE_SLOTS // 8, RESPONSE_SLOTS).astype(jnp.int32),
    }


def attend_group(items):
    queries, response_keys, response_values, prompt_key_rows, prompt_value_rows, upstream, coef = items
    score_scale = HEAD_SIZE ** -0.5
    joined_keys = PROMPT_TOKENS + RESPONSE_SLOTS
    query_wide = queries.astype(jnp.float32).reshape(RESPONSE_COUNT, RESPONSE_SLOTS, KEY_HEADS, QUERY_PER_KV, HEAD_SIZE)
    keys_wide = jnp.concatenate([jnp.broadcast_to(prompt_key_rows[None], (RESPONSE_COUNT, PROMPT_TOKENS, KEY_HEADS * HEAD_SIZE)), response_keys], axis=1)
    keys_wide = keys_wide.astype(jnp.float32).reshape(RESPONSE_COUNT, joined_keys, KEY_HEADS, HEAD_SIZE)
    values_wide = jnp.concatenate([jnp.broadcast_to(prompt_value_rows[None], (RESPONSE_COUNT, PROMPT_TOKENS, KEY_HEADS * HEAD_SIZE)), response_values], axis=1)
    values_wide = values_wide.astype(jnp.float32).reshape(RESPONSE_COUNT, joined_keys, KEY_HEADS, HEAD_SIZE)
    scores = jnp.einsum('rtgqd,rkgd->rgqtk', query_wide, keys_wide) * score_scale
    key_index = jnp.arange(joined_keys)
    step_index = jnp.arange(RESPONSE_SLOTS)
    allowed = (key_index[None, :] < PROMPT_TOKENS) | ((key_index[None, :] - PROMPT_TOKENS) <= step_index[:, None])
    scores = jnp.where(allowed, scores, -1e30)
    top = jnp.max(scores, axis=-1)
    lse = top + jnp.log(jnp.sum(jnp.exp(scores - top[..., None]), axis=-1))
    probs = jnp.exp(scores - lse[..., None])
    probability_narrow = probs.astype(jnp.bfloat16).astype(jnp.float32)
    output_gradient = (upstream.astype(jnp.float32) * coef[:, :, None]).astype(jnp.bfloat16)
    output_gradient_wide = output_gradient.astype(jnp.float32).reshape(RESPONSE_COUNT, RESPONSE_SLOTS, KEY_HEADS, QUERY_PER_KV, HEAD_SIZE)
    out = jnp.einsum('rgqtk,rkgd->rtgqd', probability_narrow, values_wide)
    delta = jnp.transpose(jnp.sum(output_gradient_wide * out, axis=-1), (0, 2, 3, 1))
    grad_probs = jnp.einsum('rtgqd,rkgd->rgqtk', output_gradient_wide, values_wide)
    score_gradient = (probs * (grad_probs - delta[..., None])).astype(jnp.bfloat16).astype(jnp.float32)
    grad_queries = (score_scale * jnp.einsum('rgqtk,rkgd->rtgqd', score_gradient, keys_wide)).reshape(RESPONSE_COUNT, RESPONSE_SLOTS, QUERY_HEADS * HEAD_SIZE).astype(jnp.bfloat16)
    key_gradient = (score_scale * jnp.einsum('wilcm,wcils->wmis', score_gradient, query_wide)).reshape(RESPONSE_COUNT, joined_keys, KEY_HEADS * HEAD_SIZE)
    value_gradient = jnp.einsum('wilcm,wcils->wmis', probability_narrow, output_gradient_wide).reshape(RESPONSE_COUNT, joined_keys, KEY_HEADS * HEAD_SIZE)
    return (grad_queries,
            key_gradient[:, PROMPT_TOKENS:].astype(jnp.bfloat16),
            value_gradient[:, PROMPT_TOKENS:].astype(jnp.bfloat16),
            jnp.sum(key_gradient[:, :PROMPT_TOKENS], axis=0),
            jnp.sum(value_gradient[:, :PROMPT_TOKENS], axis=0))


def reference(queries, response_keys, response_values, prompt_key_rows, prompt_value_rows, upstream, rewards, lengths):
    advantage = rewards - jnp.sum(rewards, axis=1, keepdims=True) / RESPONSE_COUNT
    total = jnp.sum(lengths).astype(jnp.float32)
    live = (jnp.arange(RESPONSE_SLOTS)[None, None, :] < lengths[:, :, None]).astype(jnp.float32)
    coef = advantage[:, :, None] * live / total
    return lax.map(attend_group, (queries, response_keys, response_values, prompt_key_rows, prompt_value_rows, upstream, coef))
```

```python
import functools

import jax
import jax.numpy as jnp
from jax import lax
from jax.experimental import pallas as pl
from jax.experimental.pallas import tpu as pltpu
from jax.sharding import PartitionSpec as P

MESH = pl.DeviceIdType.MESH
KEY_HEADS = 4
QUERY_PER_KV = 4
HEAD = 128
TOKENS = 128
SCALE = HEAD ** (-0.5)
LOG2E = 1.4426950408889634
F32 = jnp.float32
BF16 = jnp.bfloat16


def dot(a, b, a_dim, b_dim):
    return lax.dot_general(
        a, b, (((a_dim,), (b_dim,)), ((), ())), preferred_element_type=F32
    )


def kernel(
    dims,
    q_hbm,
    ok_hbm,
    ov_hbm,
    pk_hbm,
    pv_hbm,
    up_hbm,
    reward_ref,
    length_ref,
    gq_hbm,
    gok_hbm,
    gov_hbm,
    gpk_hbm,
    gpv_hbm,
    q_v,
    up_v,
    own_v,
    kv,
    stat,
    stat_y,
    stat_l,
    stat_z,
    stat_x,
    stat_c,
    so_ref,
    s_ref,
    p_ref,
    dp_ref,
    pb_ref,
    ds_ref,
    acc,
    rc,
    xs,
    rx,
    zacc,
    zs,
    rz,
    gq_v,
    go_v,
    gp_v,
    in_sem,
    pin_sem,
    out_sem,
    gz_s,
    gz_r,
    gx_s,
    gx_r,
    gc_s,
    gc_r,
    sc_s,
    sc_r,
    sx_s,
    sx_r,
    sz_s,
    sz_r,
    ty_s,
    ty_r,
    tl_s,
    tl_r,
    tz_s,
    tz_r,
    tx_s,
    tx_r,
    tc_s,
    tc_r,
):
    nl, ny, nz, nx = dims
    prompt = nz * nx * 2 * 16
    rows = QUERY_PER_KV * TOKENS
    gi, ri = lax.axis_index("group"), lax.axis_index("resp")
    mc = lax.rem(ri, 2)
    mx = lax.rem(lax.div(ri, 2), nx)
    mz = lax.div(ri, 2 * nx)
    my = lax.rem(gi, ny)
    ml = lax.div(gi, ny)

    def device(c=mc, x=mx, z=mz, y=my, l=ml):
        return (l * ny + y, (z * nx + x) * 2 + c)

    def ahead(me, d, n):
        return lax.rem(me + d, n)

    def remote(src, dst, send, recv, to):
        return pltpu.make_async_remote_copy(
            src_ref=src,
            dst_ref=dst,
            send_sem=send,
            recv_sem=recv,
            device_id=to,
            device_id_type=MESH,
        )

    def head_cols(g):
        return slice(g * HEAD, (g + 1) * HEAD)

    shard_in = []
    for g in range(KEY_HEADS):
        pair = []
        for i, src in enumerate((pk_hbm, pv_hbm)):
            pair.append(
                pltpu.make_async_copy(
                    src.at[:, head_cols(g)],
                    kv.at[g, i, mc, mx, mz],
                    pin_sem.at[g, i],
                )
            )
            pair[-1].start()
        shard_in.append(pair)
    loads = [
        pltpu.make_async_copy(src, dst, in_sem.at[i])
        for i, (src, dst) in enumerate(
            (
                (q_hbm, q_v),
                (ok_hbm, own_v.at[0]),
                (ov_hbm, own_v.at[1]),
                (up_hbm, up_v),
            )
        )
    ]
    for load in loads:
        load.start()

    reward = reward_ref[0, 0]
    length = length_ref[0, 0]
    stat[0, 0:8] = jnp.full((8, 128), reward, F32)
    stat[0, 8:16] = jnp.full((8, 128), length.astype(F32), F32)

    partners = [device(c=1 - mc)]
    partners += [device(x=ahead(mx, d, nx)) for d in range(1, nx)]
    partners += [device(z=ahead(mz, d, nz)) for d in range(1, nz)]
    partners += [device(y=ahead(my, d, ny)) for d in range(1, ny)]
    partners += [device(l=ahead(ml, d, nl)) for d in range(1, nl)]
    barrier = pltpu.get_barrier_semaphore()
    for partner in partners:
        pl.semaphore_signal(barrier, inc=1, device_id=partner, device_id_type=MESH)
    pl.semaphore_wait(barrier, len(partners))

    sent = []

    def send(copies):
        for copy in copies:
            copy.start()
        sent.extend(copies)
        return copies

    def arrive(copies):
        for copy in copies:
            copy.wait_recv()

    def stat_send(step, into, s_sem, r_sem, name, me, n):
        return send(
            [
                remote(
                    stat.at[step],
                    into.at[d - 1],
                    s_sem.at[d - 1],
                    r_sem.at[d - 1],
                    device(**{name: ahead(me, d, n)}),
                )
                for d in range(1, n)
            ]
        )

    def stat_sum(step, copies, into, n, both):
        arrive(copies)
        block = stat[step]
        total = block[8:16]
        wins = block[0:8]
        for d in range(n - 1):
            total = total + into[d, 8:16]
            if both:
                wins = wins + into[d, 0:8]
        stat[step + 1, 0:8] = wins
        stat[step + 1, 8:16] = total

    def gather_z(g):
        mine = kv.at[g, :, mc, mx, mz]
        return send(
            [
                remote(
                    mine,
                    mine,
                    gz_s.at[g, d - 1],
                    gz_r.at[g, d - 1],
                    device(z=ahead(mz, d, nz)),
                )
                for d in range(1, nz)
            ]
        )

    def gather_x(g):
        mine = kv.at[g, :, mc, mx]
        return send(
            [
                remote(
                    mine,
                    mine,
                    gx_s.at[g, d - 1],
                    gx_r.at[g, d - 1],
                    device(x=ahead(mx, d, nx)),
                )
                for d in range(1, nx)
            ]
        )

    def gather_c(g):
        mine = kv.at[g, :, mc]
        return send(
            [remote(mine, mine, gc_s.at[g], gc_r.at[g], device(c=1 - mc))]
        )

    def reduce_c(g):
        return send(
            [
                remote(
                    acc.at[g, :, 1 - mc],
                    rc.at[g],
                    sc_s.at[g],
                    sc_r.at[g],
                    device(c=1 - mc),
                )
            ]
        )

    def reduce_x(g, copies):
        arrive(copies)
        xs[g] = (acc[g, :, mc] + rc[g]).astype(BF16)
        return send(
            [
                remote(
                    xs.at[g, :, ahead(mx, d, nx)],
                    rx.at[g, d - 1],
                    sx_s.at[g, d - 1],
                    sx_r.at[g, d - 1],
                    device(x=ahead(mx, d, nx)),
                )
                for d in range(1, nx)
            ]
        )

    def reduce_z(g, copies):
        arrive(copies)
        part = acc[g, :, mc, mx] + rc[g, :, mx]
        for d in range(nx - 1):
            part = part + rx[g, d].astype(F32)
        zacc[g] = part
        zs[g] = part.astype(BF16)
        return send(
            [
                remote(
                    zs.at[g, :, ahead(mz, d, nz)],
                    rz.at[g, d - 1],
                    sz_s.at[g, d - 1],
                    sz_r.at[g, d - 1],
                    device(z=ahead(mz, d, nz)),
                )
                for d in range(1, nz)
            ]
        )

    def reduce_end(g, copies):
        arrive(copies)
        part = zacc[g, :, mz]
        for d in range(nz - 1):
            part = part + rz[g, d].astype(F32)
        gp_v[0, :, head_cols(g)] = part[0]
        gp_v[1, :, head_cols(g)] = part[1]

    def query_cols(g, j):
        lower = (g * QUERY_PER_KV + j) * HEAD
        return slice(lower, lower + HEAD)

    def queries_of(g):
        return jnp.concatenate(
            [q_v[:, query_cols(g, j)] for j in range(QUERY_PER_KV)], axis=0
        )

    def own_scores(g):
        key = lax.broadcasted_iota(jnp.int32, (TOKENS, rows), 0)
        step = lax.broadcasted_iota(jnp.int32, (TOKENS, rows), 1) & (TOKENS - 1)
        scores = dot(own_v[0, :, head_cols(g)], queries_of(g), 1, 1)
        so_ref[g] = jnp.where(key <= step, scores, -1e30)

    def forward(g):
        s_ref[...] = dot(kv[g, 0].reshape(prompt, HEAD), queries_of(g), 1, 1)
        top = jnp.maximum(
            jnp.max(s_ref[...], axis=0, keepdims=True),
            jnp.max(so_ref[g], axis=0, keepdims=True),
        )
        p_ref[0:prompt] = jnp.exp2((s_ref[...] - top) * (SCALE * LOG2E))
        p_ref[prompt:] = jnp.exp2((so_ref[g] - top) * (SCALE * LOG2E))
        inverse = 1.0 / jnp.sum(p_ref[...], axis=0, keepdims=True)
        probs = p_ref[...] * inverse
        p_ref[...] = probs
        pb_ref[...] = probs.astype(BF16)

    def backward(g, coef):
        q_g = queries_of(g)
        keys = kv[g, 0].reshape(prompt, HEAD)
        own_keys = own_v[0, :, head_cols(g)]
        grad_out = jnp.concatenate(
            [
                (up_v[:, query_cols(g, j)].astype(F32) * coef).astype(BF16)
                for j in range(QUERY_PER_KV)
            ],
            axis=0,
        )
        dp_ref[0:prompt] = dot(kv[g, 1].reshape(prompt, HEAD), grad_out, 1, 1)
        dp_ref[prompt:] = dot(own_v[1, :, head_cols(g)], grad_out, 1, 1)
        grad_values = dot(pb_ref[...], grad_out, 1, 0)
        acc[g, 1] = grad_values[0:prompt].reshape(2, nx, nz, 16, HEAD)
        go_v[1, :, head_cols(g)] = grad_values[prompt:].astype(BF16)
        delta = jnp.sum(pb_ref[...].astype(F32) * dp_ref[...], axis=0, keepdims=True)
        ds_ref[...] = (p_ref[...] * (dp_ref[...] - delta)).astype(BF16)
        grad_keys = SCALE * dot(ds_ref[...], q_g, 1, 0)
        acc[g, 0] = grad_keys[0:prompt].reshape(2, nx, nz, 16, HEAD)
        go_v[0, :, head_cols(g)] = grad_keys[prompt:].astype(BF16)

    def query_gradient(g):
        keys = kv[g, 0].reshape(prompt, HEAD)
        own_keys = own_v[0, :, head_cols(g)]
        turned = SCALE * (
            dot(keys, ds_ref[0:prompt], 0, 0) + dot(own_keys, ds_ref[prompt:], 0, 0)
        )
        for j in range(QUERY_PER_KV):
            block = turned[:, j * TOKENS : (j + 1) * TOKENS]
            gq_v[:, query_cols(g, j)] = block.T.astype(BF16)

    t_y = stat_send(0, stat_y, ty_s, ty_r, "y", my, ny)
    on_z, on_x, on_c = [], [], []
    for g in range(KEY_HEADS):
        for copy in shard_in[g]:
            copy.wait()
        on_z.append(gather_z(g))
    for load in loads[0:3]:
        load.wait()
    for g in range(KEY_HEADS):
        own_scores(g)
    stat_sum(0, t_y, stat_y, ny, False)
    t_l = stat_send(1, stat_l, tl_s, tl_r, "l", ml, nl)
    arrive(on_z[0])
    on_x.append(gather_x(0))
    stat_sum(1, t_l, stat_l, nl, False)
    t_z = stat_send(2, stat_z, tz_s, tz_r, "z", mz, nz)
    arrive(on_z[1])
    on_x.append(gather_x(1))
    arrive(on_x[0])
    on_c.append(gather_c(0))
    stat_sum(2, t_z, stat_z, nz, True)
    t_x = stat_send(3, stat_x, tx_s, tx_r, "x", mx, nx)
    arrive(on_z[2])
    on_x.append(gather_x(2))
    arrive(on_x[1])
    on_c.append(gather_c(1))
    stat_sum(3, t_x, stat_x, nx, True)
    t_c = stat_send(4, stat_c, tc_s, tc_r, "c", mc, 2)
    arrive(on_z[3])
    on_x.append(gather_x(3))
    arrive(on_c[0])
    forward(0)
    arrive(on_x[2])
    on_c.append(gather_c(2))
    stat_sum(4, t_c, stat_c, 2, True)

    advantage = reward - stat[5, 0:1] / (nz * nx * 2)
    weight = jnp.broadcast_to(advantage / stat[5, 8:9], (TOKENS, HEAD))
    step = lax.broadcasted_iota(jnp.int32, (TOKENS, HEAD), 0)
    coef = jnp.where(step < length, weight, 0.0)
    loads[3].wait()

    backward(0, coef)
    off_c = [reduce_c(0)]
    arrive(on_x[3])
    on_c.append(gather_c(3))
    query_gradient(0)
    arrive(on_c[1])
    forward(1)
    off_x = [reduce_x(0, off_c[0])]
    backward(1, coef)
    off_c.append(reduce_c(1))
    query_gradient(1)
    off_z = [reduce_z(0, off_x[0])]
    arrive(on_c[2])
    forward(2)
    off_x.append(reduce_x(1, off_c[1]))
    backward(2, coef)
    off_c.append(reduce_c(2))
    query_gradient(2)
    off_z.append(reduce_z(1, off_x[1]))
    arrive(on_c[3])
    forward(3)
    off_x.append(reduce_x(2, off_c[2]))
    backward(3, coef)
    off_c.append(reduce_c(3))
    stores = [
        pltpu.make_async_copy(src, dst, out_sem.at[i])
        for i, (src, dst) in enumerate(
            (
                (go_v.at[0], gok_hbm),
                (go_v.at[1], gov_hbm),
                (gq_v, gq_hbm),
                (gp_v.at[0], gpk_hbm),
                (gp_v.at[1], gpv_hbm),
            )
        )
    ]
    stores[0].start()
    stores[1].start()
    off_z.append(reduce_z(2, off_x[2]))
    off_x.append(reduce_x(3, off_c[3]))
    query_gradient(3)
    stores[2].start()
    reduce_end(0, off_z[0])
    reduce_end(1, off_z[1])
    off_z.append(reduce_z(3, off_x[3]))
    reduce_end(2, off_z[2])
    reduce_end(3, off_z[3])
    stores[3].start()
    stores[4].start()
    for copy in sent:
        copy.wait_send()
    for store in stores:
        store.wait()


def on_device(
    dims,
    queries,
    response_keys,
    response_values,
    prompt_key_rows,
    prompt_value_rows,
    upstream,
    rewards,
    lengths,
):
    nl, ny, nz, nx = dims
    kvh, rows = KEY_HEADS, QUERY_PER_KV * TOKENS
    prompt = nz * nx * 2 * 16
    joined = prompt + TOKENS
    wide, narrow = queries.shape[3], response_keys.shape[3]
    shard = prompt_key_rows.shape[1]
    vmem, sem = pltpu.VMEM, pltpu.SemaphoreType.DMA
    anywhere = pl.BlockSpec(memory_space=pl.ANY)
    scalar = pl.BlockSpec(memory_space=pltpu.SMEM)
    results = pl.pallas_call(
        functools.partial(kernel, dims),
        out_shape=(
            jax.ShapeDtypeStruct((TOKENS, wide), BF16),
            jax.ShapeDtypeStruct((TOKENS, narrow), BF16),
            jax.ShapeDtypeStruct((TOKENS, narrow), BF16),
            jax.ShapeDtypeStruct((shard, narrow), F32),
            jax.ShapeDtypeStruct((shard, narrow), F32),
        ),
        in_specs=[anywhere] * 6 + [scalar] * 2,
        out_specs=[anywhere] * 5,
        scratch_shapes=[
            vmem((TOKENS, wide), BF16),
            vmem((TOKENS, wide), BF16),
            vmem((2, TOKENS, narrow), BF16),
            vmem((kvh, 2, 2, nx, nz, 16, HEAD), BF16),
            vmem((6, 16, 128), F32),
            vmem((max(ny - 1, 1), 16, 128), F32),
            vmem((max(nl - 1, 1), 16, 128), F32),
            vmem((max(nz - 1, 1), 16, 128), F32),
            vmem((max(nx - 1, 1), 16, 128), F32),
            vmem((1, 16, 128), F32),
            vmem((kvh, TOKENS, rows), F32),
            vmem((prompt, rows), F32),
            vmem((joined, rows), F32),
            vmem((joined, rows), F32),
            vmem((joined, rows), BF16),
            vmem((joined, rows), BF16),
            vmem((kvh, 2, 2, nx, nz, 16, HEAD), F32),
            vmem((kvh, 2, nx, nz, 16, HEAD), F32),
            vmem((kvh, 2, nx, nz, 16, HEAD), BF16),
            vmem((kvh, nx - 1, 2, nz, 16, HEAD), BF16),
            vmem((kvh, 2, nz, 16, HEAD), F32),
            vmem((kvh, 2, nz, 16, HEAD), BF16),
            vmem((kvh, nz - 1, 2, 16, HEAD), BF16),
            vmem((TOKENS, wide), BF16),
            vmem((2, TOKENS, narrow), BF16),
            vmem((2, shard, narrow), F32),
            sem((4,)),
            sem((kvh, 2)),
            sem((5,)),
            sem((kvh, nz - 1)),
            sem((kvh, nz - 1)),
            sem((kvh, nx - 1)),
            sem((kvh, nx - 1)),
            sem((kvh,)),
            sem((kvh,)),
            sem((kvh,)),
            sem((kvh,)),
            sem((kvh, nx - 1)),
            sem((kvh, nx - 1)),
            sem((kvh, nz - 1)),
            sem((kvh, nz - 1)),
            sem((max(ny - 1, 1),)),
            sem((max(ny - 1, 1),)),
            sem((max(nl - 1, 1),)),
            sem((max(nl - 1, 1),)),
            sem((nz - 1,)),
            sem((nz - 1,)),
            sem((nx - 1,)),
            sem((nx - 1,)),
            sem((1,)),
            sem((1,)),
        ],
        compiler_params=pltpu.CompilerParams(
            collective_id=0,
            has_side_effects=True,
            vmem_limit_bytes=56 * 1024 * 1024,
        ),
        cost_estimate=pl.CostEstimate(
            flops=1_400_000_000, bytes_accessed=3_000_000, transcendentals=1_400_000
        ),
    )(
        queries[0, 0],
        response_keys[0, 0],
        response_values[0, 0],
        prompt_key_rows[0],
        prompt_value_rows[0],
        upstream[0, 0],
        rewards,
        lengths,
    )
    gq, gok, gov, gpk, gpv = results
    return gq[None, None], gok[None, None], gov[None, None], gpk[None], gpv[None]


def solution(mesh, dims=(4, 4, 4, 4)):
    four = P("group", "resp", None, None)
    three = P("group", "resp", None)
    two = P("group", "resp")
    return jax.shard_map(
        functools.partial(on_device, dims),
        mesh=mesh,
        in_specs=(four, four, four, three, three, four, two, two),
        out_specs=(four, four, four, three, three),
        check_vma=False,
    )
```

```python
import functools

import jax
import jax.numpy as jnp
from jax import lax
from jax.experimental import pallas as pl
from jax.experimental.pallas import tpu as pltpu
from jax.sharding import PartitionSpec as P

MESH = pl.DeviceIdType.MESH
KEY_HEADS = 4
QUERY_PER_KV = 4
HEAD = 128
TOKENS = 128
SCALE = HEAD ** (-0.5)
LOG2E = 1.4426950408889634
F32 = jnp.float32
BF16 = jnp.bfloat16
VMEM_LIMIT = 56 * 1024 * 1024


def dot(a, b, a_dim, b_dim):
    return lax.dot_general(
        a, b, (((a_dim,), (b_dim,)), ((), ())), preferred_element_type=F32
    )


def kernel(
    dims,
    q_hbm,
    ok_hbm,
    ov_hbm,
    pk_hbm,
    pv_hbm,
    up_hbm,
    reward_ref,
    length_ref,
    gq_hbm,
    gok_hbm,
    gov_hbm,
    gpk_hbm,
    gpv_hbm,
    gq_v,
    gok_v,
    gov_v,
    gpk_v,
    gpv_v,
    q_v,
    up_v,
    own_v,
    kv,
    stat,
    stat_y,
    stat_l,
    stat_z,
    stat_x,
    stat_c,
    weight_ref,
    so_ref,
    dpo_ref,
    s_ref,
    e_ref,
    dp_ref,
    pb_ref,
    ds_ref,
    acc,
    rc,
    xs,
    rx,
    zacc,
    zs,
    rz,
    in_sem,
    pin_sem,
    out_sem,
    gz_s,
    gz_r,
    gx_s,
    gx_r,
    gc_s,
    gc_r,
    sc_s,
    sc_r,
    sx_s,
    sx_r,
    sz_s,
    sz_r,
    ty_s,
    ty_r,
    tl_s,
    tl_r,
    tz_s,
    tz_r,
    tx_s,
    tx_r,
    tc_s,
    tc_r,
):
    nl, ny, nz, nx = dims
    prompt = nz * nx * 2 * 16
    rows = QUERY_PER_KV * TOKENS
    gi, ri = lax.axis_index("group"), lax.axis_index("resp")
    mc = lax.rem(ri, 2)
    mx = lax.rem(lax.div(ri, 2), nx)
    mz = lax.div(ri, 2 * nx)
    my = lax.rem(gi, ny)
    ml = lax.div(gi, ny)

    def device(c=mc, x=mx, z=mz, y=my, l=ml):
        return (l * ny + y, (z * nx + x) * 2 + c)

    def ahead(me, d, n):
        return lax.rem(me + d, n)

    def remote(src, dst, send, recv, to):
        return pltpu.make_async_remote_copy(
            src_ref=src,
            dst_ref=dst,
            send_sem=send,
            recv_sem=recv,
            device_id=to,
            device_id_type=MESH,
        )

    shard_in = []
    for g in range(KEY_HEADS):
        for i, src in enumerate((pk_hbm, pv_hbm)):
            shard_in.append(
                pltpu.make_async_copy(
                    src.at[:, g * HEAD : (g + 1) * HEAD],
                    kv.at[g, i, mc, mx, mz],
                    pin_sem.at[g, i],
                )
            )
            shard_in[-1].start()
    loads = [
        pltpu.make_async_copy(src, dst, in_sem.at[i])
        for i, (src, dst) in enumerate(
            (
                (q_hbm, q_v),
                (ok_hbm, own_v.at[0]),
                (ov_hbm, own_v.at[1]),
                (up_hbm, up_v),
            )
        )
    ]
    for load in loads:
        load.start()

    reward = reward_ref[0, 0]
    length = length_ref[0, 0]
    stat[0, 0:8] = jnp.full((8, 128), reward, F32)
    stat[0, 8:16] = jnp.full((8, 128), length.astype(F32), F32)

    partners = [device(c=1 - mc)]
    partners += [device(x=ahead(mx, d, nx)) for d in range(1, nx)]
    partners += [device(z=ahead(mz, d, nz)) for d in range(1, nz)]
    partners += [device(y=ahead(my, d, ny)) for d in range(1, ny)]
    partners += [device(l=ahead(ml, d, nl)) for d in range(1, nl)]
    barrier = pltpu.get_barrier_semaphore()
    for partner in partners:
        pl.semaphore_signal(barrier, inc=1, device_id=partner, device_id_type=MESH)
    pl.semaphore_wait(barrier, len(partners))

    def start(copies):
        for copy in copies:
            copy.start()

    def arrive(copies):
        for copy in copies:
            copy.wait_recv()

    def drain(copies):
        for copy in copies:
            copy.wait_send()

    stages = (
        ("y", my, ny, stat_y, ty_s, ty_r, False),
        ("l", ml, nl, stat_l, tl_s, tl_r, False),
        ("z", mz, nz, stat_z, tz_s, tz_r, True),
        ("x", mx, nx, stat_x, tx_s, tx_r, True),
        ("c", mc, 2, stat_c, tc_s, tc_r, True),
    )

    def stat_copies(step):
        name, me, n, into, s_sem, r_sem, _ = stages[step]
        return [
            remote(
                stat.at[step],
                into.at[d - 1],
                s_sem.at[d - 1],
                r_sem.at[d - 1],
                device(**{name: ahead(me, d, n)}),
            )
            for d in range(1, n)
        ]

    def stat_sum(step):
        arrive(stat_copies(step))
        _, _, n, into, _, _, both = stages[step]
        wins = stat[step, 0:8]
        total = stat[step, 8:16]
        for d in range(n - 1):
            total = total + into[d, 8:16]
            if both:
                wins = wins + into[d, 0:8]
        stat[step + 1, 0:8] = wins
        stat[step + 1, 8:16] = total

    def gather_z(g):
        mine = kv.at[g, :, mc, mx, mz]
        return [
            remote(
                mine,
                mine,
                gz_s.at[g, d - 1],
                gz_r.at[g, d - 1],
                device(z=ahead(mz, d, nz)),
            )
            for d in range(1, nz)
        ]

    def gather_x(g):
        mine = kv.at[g, :, mc, mx]
        return [
            remote(
                mine,
                mine,
                gx_s.at[g, d - 1],
                gx_r.at[g, d - 1],
                device(x=ahead(mx, d, nx)),
            )
            for d in range(1, nx)
        ]

    def gather_c(g):
        mine = kv.at[g, :, mc]
        return [remote(mine, mine, gc_s.at[g], gc_r.at[g], device(c=1 - mc))]

    def reduce_c(g):
        return [
            remote(
                acc.at[g, :, 1 - mc],
                rc.at[g],
                sc_s.at[g],
                sc_r.at[g],
                device(c=1 - mc),
            )
        ]

    def reduce_x(g):
        return [
            remote(
                xs.at[g, :, ahead(mx, d, nx)],
                rx.at[g, d - 1],
                sx_s.at[g, d - 1],
                sx_r.at[g, d - 1],
                device(x=ahead(mx, d, nx)),
            )
            for d in range(1, nx)
        ]

    def reduce_z(g):
        return [
            remote(
                zs.at[g, :, ahead(mz, d, nz)],
                rz.at[g, d - 1],
                sz_s.at[g, d - 1],
                sz_r.at[g, d - 1],
                device(z=ahead(mz, d, nz)),
            )
            for d in range(1, nz)
        ]

    def after_c(g):
        arrive(reduce_c(g))
        xs[g] = (acc[g, :, mc] + rc[g]).astype(BF16)
        start(reduce_x(g))

    def after_x(g):
        arrive(reduce_x(g))
        part = acc[g, :, mc, mx] + rc[g, :, mx]
        for d in range(nx - 1):
            part = part + rx[g, d].astype(F32)
        zacc[g] = part
        zs[g] = part.astype(BF16)
        start(reduce_z(g))

    def after_z(g):
        arrive(reduce_z(g))
        part = zacc[g, :, mz]
        for d in range(nz - 1):
            part = part + rz[g, d].astype(F32)
        gpk_v[:, g * HEAD : (g + 1) * HEAD] = part[0]
        gpv_v[:, g * HEAD : (g + 1) * HEAD] = part[1]

    def head_cols(g):
        return pl.ds(pl.multiple_of(g * HEAD, HEAD), HEAD)

    def query_cols(g, j):
        return pl.ds(pl.multiple_of((g * QUERY_PER_KV + j) * HEAD, HEAD), HEAD)

    def stacked(ref, g):
        return jnp.concatenate(
            [ref[:, query_cols(g, j)] for j in range(QUERY_PER_KV)], axis=0
        )

    def own_part(g, carry):
        key = lax.broadcasted_iota(jnp.int32, (TOKENS, rows), 0)
        step = lax.broadcasted_iota(jnp.int32, (TOKENS, rows), 1) & (TOKENS - 1)
        scores = dot(own_v[0, :, head_cols(g)], stacked(q_v, g), 1, 1)
        so_ref[g] = jnp.where(key <= step, scores, -1e30)
        step = lax.broadcasted_iota(jnp.int32, (TOKENS, HEAD), 0)
        live = jnp.where(step < length, 1.0, 0.0)
        for j in range(QUERY_PER_KV):
            cols = query_cols(g, j)
            up_v[:, cols] = (up_v[:, cols].astype(F32) * live).astype(BF16)
        dpo_ref[g] = dot(own_v[1, :, head_cols(g)], stacked(up_v, g), 1, 1)
        return carry

    def forward(g):
        s_ref[...] = dot(kv[g, 0].reshape(prompt, HEAD), stacked(q_v, g), 1, 1)
        top = jnp.maximum(
            jnp.max(s_ref[...], axis=0, keepdims=True),
            jnp.max(so_ref[g], axis=0, keepdims=True),
        )
        e_ref[0:prompt] = jnp.exp2((s_ref[...] - top) * (SCALE * LOG2E))
        e_ref[prompt:] = jnp.exp2((so_ref[g] - top) * (SCALE * LOG2E))
        inverse = 1.0 / jnp.sum(e_ref[...], axis=0, keepdims=True)
        pb_ref[...] = (e_ref[...] * inverse).astype(BF16)
        return inverse

    def backward(g, inverse):
        grad_out = stacked(up_v, g)
        dp_ref[0:prompt] = dot(kv[g, 1].reshape(prompt, HEAD), grad_out, 1, 1)
        dp_ref[prompt:] = dpo_ref[g]
        weight = weight_ref[0:1]
        grad_values = weight * dot(pb_ref[...], grad_out, 1, 0)
        acc[g, 1] = grad_values[0:prompt].reshape(2, nx, nz, 16, HEAD)
        gov_v[:, head_cols(g)] = grad_values[prompt:].astype(BF16)
        delta = jnp.sum(pb_ref[...].astype(F32) * dp_ref[...], axis=0, keepdims=True)
        ds_ref[...] = ((e_ref[...] * inverse) * (dp_ref[...] - delta)).astype(BF16)
        grad_keys = (weight * SCALE) * dot(ds_ref[...], stacked(q_v, g), 1, 0)
        acc[g, 0] = grad_keys[0:prompt].reshape(2, nx, nz, 16, HEAD)
        gok_v[:, head_cols(g)] = grad_keys[prompt:].astype(BF16)

    def query_gradient(g):
        keys = kv[g, 0].reshape(prompt, HEAD)
        turned = dot(keys, ds_ref[0:prompt], 0, 0) + dot(
            own_v[0, :, head_cols(g)], ds_ref[prompt:], 0, 0
        )
        weight = weight_ref[0:1] * SCALE
        for j in range(QUERY_PER_KV):
            block = turned[:, j * TOKENS : (j + 1) * TOKENS]
            gq_v[:, query_cols(g, j)] = (block.T * weight).astype(BF16)

    start(stat_copies(0))
    for copy in shard_in[0:2]:
        copy.wait()
    start(gather_z(0))
    for g in range(1, KEY_HEADS):
        for copy in shard_in[2 * g : 2 * g + 2]:
            copy.wait()
        start(gather_z(g))
    for load in loads:
        load.wait()
    lax.fori_loop(0, KEY_HEADS, own_part, 0)
    stat_sum(0)
    start(stat_copies(1))
    arrive(gather_z(0))
    start(gather_x(0))
    arrive(gather_z(1))
    start(gather_x(1))
    stat_sum(1)
    start(stat_copies(2))
    arrive(gather_x(0))
    start(gather_c(0))
    stat_sum(2)
    start(stat_copies(3))

    def head(g, carry):
        arrive(gather_c(g))
        inverse = forward(g)

        @pl.when(g + 2 < KEY_HEADS)
        def _():
            arrive(gather_z(g + 2))
            start(gather_x(g + 2))

        @pl.when(g + 1 < KEY_HEADS)
        def _():
            arrive(gather_x(g + 1))
            start(gather_c(g + 1))

        @pl.when(g == 0)
        def _():
            stat_sum(3)
            start(stat_copies(4))
            stat_sum(4)
            advantage = reward - stat[5, 0:8] / (nz * nx * 2)
            weight_ref[...] = advantage / stat[5, 8:16]

        @pl.when(g > 0)
        def _():
            after_c(g - 1)

        backward(g, inverse)
        start(reduce_c(g))

        @pl.when(g > 0)
        def _():
            after_x(g - 1)

        query_gradient(g)
        return carry

    lax.fori_loop(0, KEY_HEADS, head, 0)
    stores = [
        pltpu.make_async_copy(src, dst, out_sem.at[i])
        for i, (src, dst) in enumerate(
            (
                (gq_v, gq_hbm),
                (gok_v, gok_hbm),
                (gov_v, gov_hbm),
                (gpk_v, gpk_hbm),
                (gpv_v, gpv_hbm),
            )
        )
    ]
    last = KEY_HEADS - 1
    after_c(last)
    start(stores[0:3])
    for g in range(last):
        after_z(g)
    after_x(last)
    after_z(last)
    start(stores[3:5])
    for step in range(len(stages)):
        drain(stat_copies(step))
    for g in range(KEY_HEADS):
        for copies in (gather_z, gather_x, gather_c, reduce_c, reduce_x, reduce_z):
            drain(copies(g))
    for store in stores:
        store.wait()


def store_kernel(*refs):
    count = len(refs) // 2
    sem = refs[-1]
    copies = [
        pltpu.make_async_copy(refs[i], refs[count + i], sem.at[i])
        for i in range(count)
    ]
    for copy in copies:
        copy.start()
    for copy in copies:
        copy.wait()


def on_device(
    dims,
    queries,
    response_keys,
    response_values,
    prompt_key_rows,
    prompt_value_rows,
    upstream,
    rewards,
    lengths,
):
    nl, ny, nz, nx = dims
    kvh, rows = KEY_HEADS, QUERY_PER_KV * TOKENS
    prompt = nz * nx * 2 * 16
    joined = prompt + TOKENS
    wide, narrow = queries.shape[3], response_keys.shape[3]
    shard = prompt_key_rows.shape[1]
    vmem, sem = pltpu.VMEM, pltpu.SemaphoreType.DMA
    anywhere = pl.BlockSpec(memory_space=pl.ANY)
    scalar = pl.BlockSpec(memory_space=pltpu.SMEM)
    shapes = (
        jax.ShapeDtypeStruct((TOKENS, wide), BF16),
        jax.ShapeDtypeStruct((TOKENS, narrow), BF16),
        jax.ShapeDtypeStruct((TOKENS, narrow), BF16),
        jax.ShapeDtypeStruct((shard, narrow), F32),
        jax.ShapeDtypeStruct((shard, narrow), F32),
    )
    results = pl.pallas_call(
        functools.partial(kernel, dims),
        out_shape=shapes,
        in_specs=[anywhere] * 6 + [scalar] * 2,
        out_specs=[anywhere] * 5,
        scratch_shapes=[
            vmem((TOKENS, wide), BF16),
            vmem((TOKENS, narrow), BF16),
            vmem((TOKENS, narrow), BF16),
            vmem((shard, narrow), F32),
            vmem((shard, narrow), F32),
            vmem((TOKENS, wide), BF16),
            vmem((TOKENS, wide), BF16),
            vmem((2, TOKENS, narrow), BF16),
            vmem((kvh, 2, 2, nx, nz, 16, HEAD), BF16),
            vmem((6, 16, 128), F32),
            vmem((max(ny - 1, 1), 16, 128), F32),
            vmem((max(nl - 1, 1), 16, 128), F32),
            vmem((max(nz - 1, 1), 16, 128), F32),
            vmem((max(nx - 1, 1), 16, 128), F32),
            vmem((1, 16, 128), F32),
            vmem((8, 128), F32),
            vmem((kvh, TOKENS, rows), F32),
            vmem((kvh, TOKENS, rows), F32),
            vmem((prompt, rows), F32),
            vmem((joined, rows), F32),
            vmem((joined, rows), F32),
            vmem((joined, rows), BF16),
            vmem((joined, rows), BF16),
            vmem((kvh, 2, 2, nx, nz, 16, HEAD), F32),
            vmem((kvh, 2, nx, nz, 16, HEAD), F32),
            vmem((kvh, 2, nx, nz, 16, HEAD), BF16),
            vmem((kvh, nx - 1, 2, nz, 16, HEAD), BF16),
            vmem((kvh, 2, nz, 16, HEAD), F32),
            vmem((kvh, 2, nz, 16, HEAD), BF16),
            vmem((kvh, nz - 1, 2, 16, HEAD), BF16),
            sem((4,)),
            sem((kvh, 2)),
            sem((5,)),
            sem((kvh, nz - 1)),
            sem((kvh, nz - 1)),
            sem((kvh, nx - 1)),
            sem((kvh, nx - 1)),
            sem((kvh,)),
            sem((kvh,)),
            sem((kvh,)),
            sem((kvh,)),
            sem((kvh, nx - 1)),
            sem((kvh, nx - 1)),
            sem((kvh, nz - 1)),
            sem((kvh, nz - 1)),
            sem((max(ny - 1, 1),)),
            sem((max(ny - 1, 1),)),
            sem((max(nl - 1, 1),)),
            sem((max(nl - 1, 1),)),
            sem((nz - 1,)),
            sem((nz - 1,)),
            sem((nx - 1,)),
            sem((nx - 1,)),
            sem((1,)),
            sem((1,)),
        ],
        compiler_params=pltpu.CompilerParams(
            collective_id=0,
            has_side_effects=True,
            vmem_limit_bytes=VMEM_LIMIT,
        ),
        cost_estimate=pl.CostEstimate(
            flops=1_400_000_000, bytes_accessed=3_000_000, transcendentals=1_400_000
        ),
    )(
        queries[0, 0],
        response_keys[0, 0],
        response_values[0, 0],
        prompt_key_rows[0],
        prompt_value_rows[0],
        upstream[0, 0],
        rewards,
        lengths,
    )
    gq, gok, gov, gpk, gpv = pl.pallas_call(
        store_kernel,
        out_shape=shapes,
        in_specs=[anywhere] * 5,
        out_specs=[anywhere] * 5,
        scratch_shapes=[sem((5,))],
        compiler_params=pltpu.CompilerParams(vmem_limit_bytes=VMEM_LIMIT),
    )(*results)
    return gq[None, None], gok[None, None], gov[None, None], gpk[None], gpv[None]


def solution(mesh, dims=(4, 4, 4, 4)):
    four = P("group", "resp", None, None)
    three = P("group", "resp", None)
    two = P("group", "resp")
    return jax.shard_map(
        functools.partial(on_device, dims),
        mesh=mesh,
        in_specs=(four, four, four, three, three, four, two, two),
        out_specs=(four, four, four, three, three),
        check_vma=False,
    )
```

```python
import functools

import jax
import jax.numpy as jnp
from jax import lax
from jax.experimental import pallas as pl
from jax.experimental.pallas import tpu as pltpu
from jax.sharding import PartitionSpec as P

MESH = pl.DeviceIdType.MESH
KEY_HEADS = 4
QUERY_PER_KV = 4
HEAD = 128
TOKENS = 128
SCALE = HEAD ** (-0.5)
LOG2E = 1.4426950408889634
F32 = jnp.float32
BF16 = jnp.bfloat16
VMEM_LIMIT = 56 * 1024 * 1024


def dot(a, b, a_dim, b_dim):
    return lax.dot_general(
        a, b, (((a_dim,), (b_dim,)), ((), ())), preferred_element_type=F32
    )


def kernel(
    dims,
    q_hbm,
    ok_hbm,
    ov_hbm,
    pk_hbm,
    pv_hbm,
    up_hbm,
    reward_ref,
    length_ref,
    gq_hbm,
    gok_hbm,
    gov_hbm,
    gpk_hbm,
    gpv_hbm,
    gq_v,
    go_v,
    gp_v,
    q_v,
    up_v,
    own_v,
    shard_v,
    kv,
    stat,
    stat_in,
    own_grad,
    so_ref,
    dpo_ref,
    s_ref,
    e_ref,
    dp_ref,
    pb_ref,
    ds_ref,
    acc,
    cs,
    rc,
    part,
    xs,
    rx,
    zs,
    rz,
    in_sem,
    out_sem,
    gz_s,
    gz_r,
    gx_s,
    gx_r,
    gc_s,
    gc_r,
    sc_s,
    sc_r,
    sx_s,
    sx_r,
    sz_s,
    sz_r,
    t_s,
    t_r,
):
    nl, ny, nz, nx = dims
    prompt = nz * nx * 2 * 16
    rows = QUERY_PER_KV * TOKENS
    gi, ri = lax.axis_index("group"), lax.axis_index("resp")
    mc = lax.rem(ri, 2)
    mx = lax.rem(lax.div(ri, 2), nx)
    mz = lax.div(ri, 2 * nx)
    my = lax.rem(gi, ny)
    ml = lax.div(gi, ny)

    def device(c=mc, x=mx, z=mz, y=my, l=ml):
        return (l * ny + y, (z * nx + x) * 2 + c)

    def ahead(me, d, n):
        return lax.rem(me + d, n)

    def remote(src, dst, send, recv, to):
        return pltpu.make_async_remote_copy(
            src_ref=src,
            dst_ref=dst,
            send_sem=send,
            recv_sem=recv,
            device_id=to,
            device_id_type=MESH,
        )

    on_core = device(c=1 - mc)
    on_x = [device(x=ahead(mx, d, nx)) for d in range(1, nx)]
    on_z = [device(z=ahead(mz, d, nz)) for d in range(1, nz)]
    on_y = [device(y=ahead(my, d, ny)) for d in range(1, ny)]
    on_l = [device(l=ahead(ml, d, nl)) for d in range(1, nl)]
    partners = [on_core] + on_x + on_z + on_y + on_l
    barrier = pltpu.get_barrier_semaphore()
    for partner in partners:
        pl.semaphore_signal(barrier, inc=1, device_id=partner, device_id_type=MESH)

    loads = [
        pltpu.make_async_copy(src, dst, in_sem.at[i])
        for i, (src, dst) in enumerate(
            (
                (pk_hbm, shard_v.at[0]),
                (pv_hbm, shard_v.at[1]),
                (q_hbm, q_v),
                (ok_hbm, own_v.at[0]),
                (ov_hbm, own_v.at[1]),
                (up_hbm, up_v),
            )
        )
    ]
    for load in loads:
        load.start()

    reward = reward_ref[0, 0]
    length = length_ref[0, 0]
    stat[0, 0:8] = jnp.full((8, 128), reward, F32)
    stat[0, 8:16] = jnp.full((8, 128), length.astype(F32), F32)

    def start(copies):
        for copy in copies:
            copy.start()

    def arrive(copies):
        for copy in copies:
            copy.wait_recv()

    def drain(copies):
        for copy in copies:
            copy.wait_send()

    stages = (on_z, on_x, [on_core], on_y, on_l)

    def stat_copies(step):
        return [
            remote(
                stat.at[step],
                stat_in.at[step, d],
                t_s.at[step, d],
                t_r.at[step, d],
                to,
            )
            for d, to in enumerate(stages[step])
        ]

    def stat_sum(step):
        arrive(stat_copies(step))
        total = stat[step]
        for d in range(len(stages[step])):
            total = total + stat_in[step, d]
        stat[step + 1] = total

    def gather_z():
        mine = kv.at[:, mc, mx, mz]
        return [
            remote(mine, mine, gz_s.at[d], gz_r.at[d], to) for d, to in enumerate(on_z)
        ]

    def gather_x(half):
        mine = kv.at[2 * half : 2 * half + 2, mc, mx]
        return [
            remote(mine, mine, gx_s.at[half, d], gx_r.at[half, d], to)
            for d, to in enumerate(on_x)
        ]

    def gather_c(half):
        mine = kv.at[2 * half : 2 * half + 2, mc]
        return [remote(mine, mine, gc_s.at[half], gc_r.at[half], on_core)]

    chunks = (slice(0, 2), slice(2, 3), slice(3, 4))

    def reduce_c(n):
        return [
            remote(cs.at[chunks[n]], rc.at[chunks[n]], sc_s.at[n], sc_r.at[n], on_core)
        ]

    def reduce_x(n):
        return [
            remote(
                xs.at[chunks[n], ahead(mx, d + 1, nx)],
                rx.at[d, chunks[n]],
                sx_s.at[n, d],
                sx_r.at[n, d],
                to,
            )
            for d, to in enumerate(on_x)
        ]

    def reduce_z(n):
        return [
            remote(
                zs.at[chunks[n], ahead(mz, d + 1, nz)],
                rz.at[d, chunks[n]],
                sz_s.at[n, d],
                sz_r.at[n, d],
                to,
            )
            for d, to in enumerate(on_z)
        ]

    def before_c(n):
        cs[chunks[n]] = acc[chunks[n], 1 - mc].astype(BF16)
        start(reduce_c(n))

    def after_c(n):
        arrive(reduce_c(n))
        both = acc[chunks[n], mc] + rc[chunks[n]].astype(F32)
        part[chunks[n]] = both
        xs[chunks[n]] = both.astype(BF16)
        start(reduce_x(n))

    def after_x(n):
        arrive(reduce_x(n))
        both = part[chunks[n], mx]
        for d in range(nx - 1):
            both = both + rx[d, chunks[n]].astype(F32)
        part[chunks[n], 0] = both
        zs[chunks[n]] = both.astype(BF16)
        start(reduce_z(n))

    def after_z(n, scale):
        arrive(reduce_z(n))
        both = part[chunks[n], 0, mz]
        for d in range(nz - 1):
            both = both + rz[d, chunks[n]].astype(F32)
        for i, g in enumerate(range(chunks[n].start, chunks[n].stop)):
            gp_v[0, :, head_cols(g)] = both[i, 0] * scale
            gp_v[1, :, head_cols(g)] = both[i, 1] * scale

    def head_cols(g):
        return slice(g * HEAD, (g + 1) * HEAD)

    def query_cols(g, j):
        lower = (g * QUERY_PER_KV + j) * HEAD
        return slice(lower, lower + HEAD)

    def stacked(ref, g):
        return jnp.concatenate(
            [ref[:, query_cols(g, j)] for j in range(QUERY_PER_KV)], axis=0
        )

    def prompt_rows(g, i):
        return kv[g, :, :, :, i].reshape(prompt, HEAD)

    def own_part(g):
        key = lax.broadcasted_iota(jnp.int32, (TOKENS, rows), 0)
        step = lax.broadcasted_iota(jnp.int32, (TOKENS, rows), 1) & (TOKENS - 1)
        scores = dot(own_v[0, :, head_cols(g)], stacked(q_v, g), 1, 1)
        so_ref[g] = jnp.where(key <= step, scores, -1e30)
        step = lax.broadcasted_iota(jnp.int32, (TOKENS, HEAD), 0)
        live = jnp.where(step < length, 1.0, 0.0)
        for j in range(QUERY_PER_KV):
            cols = query_cols(g, j)
            up_v[:, cols] = (up_v[:, cols].astype(F32) * live).astype(BF16)
        dpo_ref[g] = dot(own_v[1, :, head_cols(g)], stacked(up_v, g), 1, 1)

    def attend(g, advantage):
        q_g, grad_out = stacked(q_v, g), stacked(up_v, g)
        s_ref[...] = dot(prompt_rows(g, 0), q_g, 1, 1)
        dp_ref[0:prompt] = dot(prompt_rows(g, 1), grad_out, 1, 1)
        dp_ref[prompt:] = dpo_ref[g]
        top = jnp.maximum(
            jnp.max(s_ref[...], axis=0, keepdims=True),
            jnp.max(so_ref[g], axis=0, keepdims=True),
        )
        e_ref[0:prompt] = jnp.exp2((s_ref[...] - top) * (SCALE * LOG2E))
        e_ref[prompt:] = jnp.exp2((so_ref[g] - top) * (SCALE * LOG2E))
        inverse = 1.0 / jnp.sum(e_ref[...], axis=0, keepdims=True)
        pb_ref[...] = (e_ref[...] * inverse).astype(BF16)
        grad_values = advantage * dot(pb_ref[...], grad_out, 1, 0)
        acc[g, :, :, :, 1] = grad_values[0:prompt].reshape(2, nx, nz, 16, HEAD)
        own_grad[1, :, head_cols(g)] = grad_values[prompt:]
        delta = jnp.sum(pb_ref[...].astype(F32) * dp_ref[...], axis=0, keepdims=True)
        ds_ref[g] = ((e_ref[...] * inverse) * (dp_ref[...] - delta)).astype(BF16)
        grad_keys = (advantage * SCALE) * dot(ds_ref[g], q_g, 1, 0)
        acc[g, :, :, :, 0] = grad_keys[0:prompt].reshape(2, nx, nz, 16, HEAD)
        own_grad[0, :, head_cols(g)] = grad_keys[prompt:]

    def query_gradient(g, weight):
        turned = dot(prompt_rows(g, 0), ds_ref[g, 0:prompt], 0, 0) + dot(
            own_v[0, :, head_cols(g)], ds_ref[g, prompt:], 0, 0
        )
        for j in range(QUERY_PER_KV):
            block = turned[:, j * TOKENS : (j + 1) * TOKENS]
            gq_v[:, query_cols(g, j)] = (block.T * weight).astype(BF16)

    loads[0].wait()
    loads[1].wait()
    for g in range(KEY_HEADS):
        kv[g, mc, mx, mz, 0] = shard_v[0, :, head_cols(g)]
        kv[g, mc, mx, mz, 1] = shard_v[1, :, head_cols(g)]
    pl.semaphore_wait(barrier, len(partners))
    start(gather_z())
    start(stat_copies(0))
    for load in loads[2:]:
        load.wait()
    own_part(0)
    own_part(1)
    arrive(gather_z())
    start(gather_x(0))
    start(gather_x(1))
    stat_sum(0)
    start(stat_copies(1))
    own_part(2)
    own_part(3)
    arrive(gather_x(0))
    start(gather_c(0))
    stat_sum(1)
    start(stat_copies(2))
    arrive(gather_x(1))
    start(gather_c(1))
    stat_sum(2)
    start(stat_copies(3))
    advantage = reward - stat[3, 0:1] / (nz * nx * 2)
    arrive(gather_c(0))
    attend(0, advantage)
    attend(1, advantage)
    before_c(0)
    arrive(gather_c(1))
    attend(2, advantage)
    before_c(1)
    after_c(0)
    stat_sum(3)
    start(stat_copies(4))
    attend(3, advantage)
    before_c(2)
    after_c(1)
    after_x(0)
    after_c(2)
    stat_sum(4)
    unit = 1.0 / stat[5, 8:9]
    weight = advantage * SCALE * unit
    query_gradient(0, weight)
    after_x(1)
    query_gradient(1, weight)
    after_x(2)
    query_gradient(2, weight)
    query_gradient(3, weight)
    for g in range(KEY_HEADS):
        for i in range(2):
            go_v[i, :, head_cols(g)] = (own_grad[i, :, head_cols(g)] * unit).astype(BF16)
    stores = [
        pltpu.make_async_copy(src, dst, out_sem.at[i])
        for i, (src, dst) in enumerate(
            (
                (gq_v, gq_hbm),
                (go_v.at[0], gok_hbm),
                (go_v.at[1], gov_hbm),
                (gp_v.at[0], gpk_hbm),
                (gp_v.at[1], gpv_hbm),
            )
        )
    ]
    start(stores[0:3])
    after_z(0, unit)
    after_z(1, unit)
    after_z(2, unit)
    start(stores[3:5])
    for step in range(len(stages)):
        drain(stat_copies(step))
    drain(gather_z())
    for half in range(2):
        drain(gather_x(half))
        drain(gather_c(half))
    for n in range(len(chunks)):
        drain(reduce_c(n))
        drain(reduce_x(n))
        drain(reduce_z(n))
    for store in stores:
        store.wait()


def store_kernel(*refs):
    sources, targets, holds = refs[0:5], refs[5:10], refs[10:15]
    in_sem, out_sem = refs[15:17]
    ins = [
        pltpu.make_async_copy(sources[i], holds[i], in_sem.at[i]) for i in range(5)
    ]
    outs = [
        pltpu.make_async_copy(holds[i], targets[i], out_sem.at[i]) for i in range(5)
    ]
    for copy in ins:
        copy.start()
    for i in (1, 2, 3, 4, 0):
        ins[i].wait()
        outs[i].start()
    for copy in outs:
        copy.wait()


def on_device(
    dims,
    queries,
    response_keys,
    response_values,
    prompt_key_rows,
    prompt_value_rows,
    upstream,
    rewards,
    lengths,
):
    nl, ny, nz, nx = dims
    kvh, rows = KEY_HEADS, QUERY_PER_KV * TOKENS
    prompt = nz * nx * 2 * 16
    joined = prompt + TOKENS
    wide, narrow = queries.shape[3], response_keys.shape[3]
    shard = prompt_key_rows.shape[1]
    most = max(dims) - 1
    vmem, sem = pltpu.VMEM, pltpu.SemaphoreType.DMA
    anywhere = pl.BlockSpec(memory_space=pl.ANY)
    scalar = pl.BlockSpec(memory_space=pltpu.SMEM)
    shapes = (
        jax.ShapeDtypeStruct((TOKENS, wide), BF16),
        jax.ShapeDtypeStruct((TOKENS, narrow), BF16),
        jax.ShapeDtypeStruct((TOKENS, narrow), BF16),
        jax.ShapeDtypeStruct((shard, narrow), F32),
        jax.ShapeDtypeStruct((shard, narrow), F32),
    )
    results = pl.pallas_call(
        functools.partial(kernel, dims),
        out_shape=shapes,
        in_specs=[anywhere] * 6 + [scalar] * 2,
        out_specs=[anywhere] * 5,
        scratch_shapes=[
            vmem((TOKENS, wide), BF16),
            vmem((2, TOKENS, narrow), BF16),
            vmem((2, shard, narrow), F32),
            vmem((TOKENS, wide), BF16),
            vmem((TOKENS, wide), BF16),
            vmem((2, TOKENS, narrow), BF16),
            vmem((2, shard, narrow), BF16),
            vmem((kvh, 2, nx, nz, 2, 16, HEAD), BF16),
            vmem((6, 16, 128), F32),
            vmem((5, most, 16, 128), F32),
            vmem((2, TOKENS, narrow), F32),
            vmem((kvh, TOKENS, rows), F32),
            vmem((kvh, TOKENS, rows), F32),
            vmem((prompt, rows), F32),
            vmem((joined, rows), F32),
            vmem((joined, rows), F32),
            vmem((joined, rows), BF16),
            vmem((kvh, joined, rows), BF16),
            vmem((kvh, 2, nx, nz, 2, 16, HEAD), F32),
            vmem((kvh, nx, nz, 2, 16, HEAD), BF16),
            vmem((kvh, nx, nz, 2, 16, HEAD), BF16),
            vmem((kvh, nx, nz, 2, 16, HEAD), F32),
            vmem((kvh, nx, nz, 2, 16, HEAD), BF16),
            vmem((nx - 1, kvh, nz, 2, 16, HEAD), BF16),
            vmem((kvh, nz, 2, 16, HEAD), BF16),
            vmem((nz - 1, kvh, 2, 16, HEAD), BF16),
            sem((6,)),
            sem((5,)),
            sem((nz - 1,)),
            sem((nz - 1,)),
            sem((2, nx - 1)),
            sem((2, nx - 1)),
            sem((2,)),
            sem((2,)),
            sem((3,)),
            sem((3,)),
            sem((3, nx - 1)),
            sem((3, nx - 1)),
            sem((3, nz - 1)),
            sem((3, nz - 1)),
            sem((5, most)),
            sem((5, most)),
        ],
        compiler_params=pltpu.CompilerParams(
            collective_id=0,
            has_side_effects=True,
            vmem_limit_bytes=VMEM_LIMIT,
        ),
        cost_estimate=pl.CostEstimate(
            flops=1_400_000_000, bytes_accessed=3_000_000, transcendentals=1_400_000
        ),
    )(
        queries[0, 0],
        response_keys[0, 0],
        response_values[0, 0],
        prompt_key_rows[0],
        prompt_value_rows[0],
        upstream[0, 0],
        rewards,
        lengths,
    )
    gq, gok, gov, gpk, gpv = pl.pallas_call(
        store_kernel,
        out_shape=shapes,
        in_specs=[anywhere] * 5,
        out_specs=[anywhere] * 5,
        scratch_shapes=[vmem(x.shape, x.dtype) for x in shapes] + [sem((5,)), sem((5,))],
        compiler_params=pltpu.CompilerParams(vmem_limit_bytes=VMEM_LIMIT),
    )(*results)
    return gq[None, None], gok[None, None], gov[None, None], gpk[None], gpv[None]


def solution(mesh, dims=(4, 4, 4, 4)):
    four = P("group", "resp", None, None)
    three = P("group", "resp", None)
    two = P("group", "resp")
    return jax.shard_map(
        functools.partial(on_device, dims),
        mesh=mesh,
        in_specs=(four, four, four, three, three, four, two, two),
        out_specs=(four, four, four, three, three),
        check_vma=False,
    )
```

```python
import functools

import jax
import jax.numpy as jnp
from jax import lax
from jax.experimental import pallas as pl
from jax.experimental.pallas import tpu as pltpu
from jax.sharding import PartitionSpec as P

MESH = pl.DeviceIdType.MESH
KEY_HEADS = 4
QUERY_PER_KV = 4
HEAD = 128
TOKENS = 128
SCALE = HEAD ** (-0.5)
LOG2E = 1.4426950408889634
F32 = jnp.float32
BF16 = jnp.bfloat16
VMEM_LIMIT = 56 * 1024 * 1024


def dot(a, b, a_dim, b_dim):
    return lax.dot_general(
        a, b, (((a_dim,), (b_dim,)), ((), ())), preferred_element_type=F32
    )


def kernel(
    dims,
    q_hbm,
    ok_hbm,
    ov_hbm,
    pk_hbm,
    pv_hbm,
    up_hbm,
    reward_ref,
    length_ref,
    gq_hbm,
    gok_hbm,
    gov_hbm,
    gpk_hbm,
    gpv_hbm,
    gq_v,
    go_v,
    gp_v,
    q_v,
    up_v,
    own_v,
    shard_v,
    kv,
    stat,
    stat_in,
    own_grad,
    so_ref,
    dpo_ref,
    s_ref,
    e_ref,
    dp_ref,
    pb_ref,
    ds_ref,
    acc,
    cs,
    rc,
    part,
    xs,
    rx,
    zs,
    rz,
    in_sem,
    out_sem,
    gz_s,
    gz_r,
    hz_s,
    hz_r,
    gx_s,
    gx_r,
    hx_s,
    hx_r,
    gc_s,
    gc_r,
    sc_s,
    sc_r,
    sx_s,
    sx_r,
    sz_s,
    sz_r,
    t_s,
    t_r,
):
    nl, ny, nz, nx = dims
    prompt = nz * nx * 2 * 16
    rows = QUERY_PER_KV * TOKENS
    gi, ri = lax.axis_index("group"), lax.axis_index("resp")
    mc = lax.rem(ri, 2)
    mx = lax.rem(lax.div(ri, 2), nx)
    mz = lax.div(ri, 2 * nx)
    my = lax.rem(gi, ny)
    ml = lax.div(gi, ny)

    def device(c=mc, x=mx, z=mz, y=my, l=ml):
        return (l * ny + y, (z * nx + x) * 2 + c)

    def ahead(me, d, n):
        return lax.rem(me + d, n)

    def remote(src, dst, send, recv, to):
        return pltpu.make_async_remote_copy(
            src_ref=src,
            dst_ref=dst,
            send_sem=send,
            recv_sem=recv,
            device_id=to,
            device_id_type=MESH,
        )

    def ring(me, n):
        return [lax.rem(me + 1, n)] + ([lax.rem(me + n - 1, n)] if n > 2 else [])

    def pairs(me, n):
        flip = [me + 1 - 2 * lax.rem(me, 2)] if n > 1 else []
        return flip + ([n - 1 - me] if n > 2 else [])

    near_z, near_x = ring(mz, nz), ring(mx, nx)
    on_core = device(c=1 - mc)
    next_z = [device(z=z) for z in near_z]
    next_x = [device(x=x) for x in near_x]
    pair_y = [device(y=y) for y in pairs(my, ny)]
    pair_l = [device(l=l) for l in pairs(ml, nl)]
    on_x = [device(x=ahead(mx, d, nx)) for d in range(1, nx)]
    on_z = [device(z=ahead(mz, d, nz)) for d in range(1, nz)]
    partners = [on_core] + next_x + next_z + pair_y + pair_l
    barrier = pltpu.get_barrier_semaphore()
    for partner in partners:
        pl.semaphore_signal(barrier, inc=1, device_id=partner, device_id_type=MESH)

    loads = [
        pltpu.make_async_copy(src, dst, in_sem.at[i])
        for i, (src, dst) in enumerate(
            (
                (pk_hbm, shard_v.at[0]),
                (pv_hbm, shard_v.at[1]),
                (q_hbm, q_v),
                (ok_hbm, own_v.at[0]),
                (ov_hbm, own_v.at[1]),
                (up_hbm, up_v),
            )
        )
    ]
    for load in loads:
        load.start()

    reward = reward_ref[0, 0]
    length = length_ref[0, 0]
    stat[0, 0:8] = jnp.full((8, 128), reward, F32)
    stat[0, 8:16] = jnp.full((8, 128), length.astype(F32), F32)

    def start(copies):
        for copy in copies:
            copy.start()

    def arrive(copies):
        for copy in copies:
            copy.wait_recv()

    def drain(copies):
        for copy in copies:
            copy.wait_send()

    stages = [device(z=z) for z in pairs(mz, nz)]
    stages += [device(x=x) for x in pairs(mx, nx)] + [on_core]
    in_group = len(stages)
    stages += pair_y + pair_l

    def stat_copy(step):
        return remote(
            stat.at[step], stat_in.at[step], t_s.at[step], t_r.at[step], stages[step]
        )

    def stat_next(step):
        if step < len(stages):
            stat_copy(step).wait_recv()
            stat[step + 1] = stat[step] + stat_in[step]
            if step + 1 < len(stages):
                stat_copy(step + 1).start()

    def gather_z():
        mine = kv.at[:, mc, mx, mz]
        return [
            remote(mine, mine, gz_s.at[d], gz_r.at[d], to)
            for d, to in enumerate(next_z)
        ]

    def relay_z():
        if nz == 2:
            return []
        parts = [kv.at[0:2, mc, mx, near_z[1]], kv.at[2:4, mc, mx, near_z[0]]]
        return [
            remote(block, block, hz_s.at[d], hz_r.at[d], next_z[d])
            for d, block in enumerate(parts)
        ]

    def gather_x(half):
        mine = kv.at[2 * half : 2 * half + 2, mc, mx]
        return [
            remote(mine, mine, gx_s.at[half, d], gx_r.at[half, d], to)
            for d, to in enumerate(next_x)
        ]

    def relay_x(half):
        if nx == 2:
            return []
        parts = [kv.at[2 * half, mc, near_x[1]], kv.at[2 * half + 1, mc, near_x[0]]]
        return [
            remote(block, block, hx_s.at[half, d], hx_r.at[half, d], next_x[d])
            for d, block in enumerate(parts)
        ]

    def pass_on(copies, relays):
        for d, copy in enumerate(copies):
            copy.wait_recv()
            start(relays[d : d + 1])

    def gather_c(half):
        mine = kv.at[2 * half : 2 * half + 2, mc]
        return [remote(mine, mine, gc_s.at[half], gc_r.at[half], on_core)]

    chunks = (slice(0, 2), slice(2, 3), slice(3, 4))

    def reduce_c(n):
        return [
            remote(cs.at[chunks[n]], rc.at[chunks[n]], sc_s.at[n], sc_r.at[n], on_core)
        ]

    def reduce_x(n):
        return [
            remote(
                xs.at[chunks[n], ahead(mx, d + 1, nx)],
                rx.at[d, chunks[n]],
                sx_s.at[n, d],
                sx_r.at[n, d],
                to,
            )
            for d, to in enumerate(on_x)
        ]

    def reduce_z(n):
        return [
            remote(
                zs.at[chunks[n], ahead(mz, d + 1, nz)],
                rz.at[d, chunks[n]],
                sz_s.at[n, d],
                sz_r.at[n, d],
                to,
            )
            for d, to in enumerate(on_z)
        ]

    def before_c(n, advantage):
        cs[chunks[n]] = (acc[chunks[n], 1 - mc] * advantage).astype(BF16)
        start(reduce_c(n))

    def after_c(n, advantage):
        arrive(reduce_c(n))
        both = acc[chunks[n], mc] * advantage + rc[chunks[n]].astype(F32)
        part[chunks[n]] = both
        xs[chunks[n]] = both.astype(BF16)
        start(reduce_x(n))

    def after_x(n):
        arrive(reduce_x(n))
        both = part[chunks[n], mx]
        for d in range(nx - 1):
            both = both + rx[d, chunks[n]].astype(F32)
        part[chunks[n], 0] = both
        zs[chunks[n]] = both.astype(BF16)
        start(reduce_z(n))

    def after_z(n, scale):
        arrive(reduce_z(n))
        both = part[chunks[n], 0, mz]
        for d in range(nz - 1):
            both = both + rz[d, chunks[n]].astype(F32)
        for i, g in enumerate(range(chunks[n].start, chunks[n].stop)):
            gp_v[0, :, head_cols(g)] = both[i, 0] * scale
            gp_v[1, :, head_cols(g)] = both[i, 1] * scale

    def head_cols(g):
        return slice(g * HEAD, (g + 1) * HEAD)

    def query_cols(g, j):
        lower = (g * QUERY_PER_KV + j) * HEAD
        return slice(lower, lower + HEAD)

    def stacked(ref, g):
        return jnp.concatenate(
            [ref[:, query_cols(g, j)] for j in range(QUERY_PER_KV)], axis=0
        )

    def prompt_rows(g, i):
        return kv[g, :, :, :, i].reshape(prompt, HEAD)

    def own_part(g):
        key = lax.broadcasted_iota(jnp.int32, (TOKENS, rows), 0)
        step = lax.broadcasted_iota(jnp.int32, (TOKENS, rows), 1) & (TOKENS - 1)
        scores = dot(own_v[0, :, head_cols(g)], stacked(q_v, g), 1, 1)
        so_ref[g] = jnp.where(key <= step, scores, -1e30)
        step = lax.broadcasted_iota(jnp.int32, (TOKENS, HEAD), 0)
        live = jnp.where(step < length, 1.0, 0.0)
        for j in range(QUERY_PER_KV):
            cols = query_cols(g, j)
            up_v[:, cols] = (up_v[:, cols].astype(F32) * live).astype(BF16)
        dpo_ref[g] = dot(own_v[1, :, head_cols(g)], stacked(up_v, g), 1, 1)

    def attend(g):
        q_g, grad_out = stacked(q_v, g), stacked(up_v, g)
        s_ref[...] = dot(prompt_rows(g, 0), q_g, 1, 1)
        dp_ref[0:prompt] = dot(prompt_rows(g, 1), grad_out, 1, 1)
        dp_ref[prompt:] = dpo_ref[g]
        top = jnp.maximum(
            jnp.max(s_ref[...], axis=0, keepdims=True),
            jnp.max(so_ref[g], axis=0, keepdims=True),
        )
        e_ref[0:prompt] = jnp.exp2((s_ref[...] - top) * (SCALE * LOG2E))
        e_ref[prompt:] = jnp.exp2((so_ref[g] - top) * (SCALE * LOG2E))
        inverse = 1.0 / jnp.sum(e_ref[...], axis=0, keepdims=True)
        pb_ref[...] = (e_ref[...] * inverse).astype(BF16)
        grad_values = dot(pb_ref[...], grad_out, 1, 0)
        acc[g, :, :, :, 1] = grad_values[0:prompt].reshape(2, nx, nz, 16, HEAD)
        own_grad[1, :, head_cols(g)] = grad_values[prompt:]
        delta = jnp.sum(pb_ref[...].astype(F32) * dp_ref[...], axis=0, keepdims=True)
        ds_ref[g] = ((e_ref[...] * inverse) * (dp_ref[...] - delta)).astype(BF16)
        grad_keys = SCALE * dot(ds_ref[g], q_g, 1, 0)
        acc[g, :, :, :, 0] = grad_keys[0:prompt].reshape(2, nx, nz, 16, HEAD)
        own_grad[0, :, head_cols(g)] = grad_keys[prompt:]

    def query_gradient(g, weight):
        turned = dot(prompt_rows(g, 0), ds_ref[g, 0:prompt], 0, 0) + dot(
            own_v[0, :, head_cols(g)], ds_ref[g, prompt:], 0, 0
        )
        for j in range(QUERY_PER_KV):
            block = turned[:, j * TOKENS : (j + 1) * TOKENS]
            gq_v[:, query_cols(g, j)] = (block.T * weight).astype(BF16)

    loads[0].wait()
    loads[1].wait()
    for g in range(KEY_HEADS):
        kv[g, mc, mx, mz, 0] = shard_v[0, :, head_cols(g)]
        kv[g, mc, mx, mz, 1] = shard_v[1, :, head_cols(g)]
    pl.semaphore_wait(barrier, len(partners))
    start(gather_z())
    stat_copy(0).start()
    pass_on(gather_z(), relay_z())
    stat_next(0)
    arrive(relay_z()[0:1])
    start(gather_x(0))
    arrive(relay_z()[1:2])
    start(gather_x(1))
    stat_next(1)
    for load in loads[2:]:
        load.wait()
    own_part(0)
    pass_on(gather_x(0), relay_x(0))
    stat_next(2)
    own_part(1)
    pass_on(gather_x(1), relay_x(1))
    arrive(relay_x(0))
    start(gather_c(0))
    stat_next(3)
    own_part(2)
    arrive(relay_x(1))
    start(gather_c(1))
    own_part(3)
    arrive(gather_c(0))
    attend(0)
    stat_next(4)
    attend(1)
    advantage = (reward - stat[in_group, 0:1] / (nz * nx * 2)).reshape(1, 1, 1, 1, 1, 128)
    before_c(0, advantage)
    arrive(gather_c(1))
    attend(2)
    before_c(1, advantage)
    after_c(0, advantage)
    stat_next(5)
    attend(3)
    before_c(2, advantage)
    after_c(1, advantage)
    after_x(0)
    stat_next(6)
    after_c(2, advantage)
    stat_next(7)
    after_x(1)
    stat_next(8)
    unit = 1.0 / stat[len(stages), 8:9]
    weight = (reward - stat[in_group, 0:1] / (nz * nx * 2)) * unit
    query_gradient(0, weight * SCALE)
    query_gradient(1, weight * SCALE)
    after_x(2)
    query_gradient(2, weight * SCALE)
    query_gradient(3, weight * SCALE)
    for g in range(KEY_HEADS):
        for i in range(2):
            go_v[i, :, head_cols(g)] = (own_grad[i, :, head_cols(g)] * weight).astype(BF16)
    stores = [
        pltpu.make_async_copy(src, dst, out_sem.at[i])
        for i, (src, dst) in enumerate(
            (
                (gq_v, gq_hbm),
                (go_v.at[0], gok_hbm),
                (go_v.at[1], gov_hbm),
                (gp_v.at[0], gpk_hbm),
                (gp_v.at[1], gpv_hbm),
            )
        )
    ]
    start(stores[0:3])
    after_z(0, unit)
    after_z(1, unit)
    after_z(2, unit)
    start(stores[3:5])
    for step in range(len(stages)):
        stat_copy(step).wait_send()
    drain(gather_z())
    drain(relay_z())
    for half in range(2):
        drain(gather_x(half))
        drain(relay_x(half))
        drain(gather_c(half))
    for n in range(len(chunks)):
        drain(reduce_c(n))
        drain(reduce_x(n))
        drain(reduce_z(n))
    for store in stores:
        store.wait()


def store_kernel(*refs):
    sources, targets, holds = refs[0:5], refs[5:10], refs[10:15]
    in_sem, out_sem = refs[15:17]
    ins = [
        pltpu.make_async_copy(sources[i], holds[i], in_sem.at[i]) for i in range(5)
    ]
    outs = [
        pltpu.make_async_copy(holds[i], targets[i], out_sem.at[i]) for i in range(5)
    ]
    for copy in ins:
        copy.start()
    for i in (1, 2, 3, 4, 0):
        ins[i].wait()
        outs[i].start()
    for copy in outs:
        copy.wait()


def on_device(
    dims,
    queries,
    response_keys,
    response_values,
    prompt_key_rows,
    prompt_value_rows,
    upstream,
    rewards,
    lengths,
):
    nl, ny, nz, nx = dims
    kvh, rows = KEY_HEADS, QUERY_PER_KV * TOKENS
    prompt = nz * nx * 2 * 16
    joined = prompt + TOKENS
    wide, narrow = queries.shape[3], response_keys.shape[3]
    shard = prompt_key_rows.shape[1]
    vmem, sem = pltpu.VMEM, pltpu.SemaphoreType.DMA
    anywhere = pl.BlockSpec(memory_space=pl.ANY)
    scalar = pl.BlockSpec(memory_space=pltpu.SMEM)
    shapes = (
        jax.ShapeDtypeStruct((TOKENS, wide), BF16),
        jax.ShapeDtypeStruct((TOKENS, narrow), BF16),
        jax.ShapeDtypeStruct((TOKENS, narrow), BF16),
        jax.ShapeDtypeStruct((shard, narrow), F32),
        jax.ShapeDtypeStruct((shard, narrow), F32),
    )
    results = pl.pallas_call(
        functools.partial(kernel, dims),
        out_shape=shapes,
        in_specs=[anywhere] * 6 + [scalar] * 2,
        out_specs=[anywhere] * 5,
        scratch_shapes=[
            vmem((TOKENS, wide), BF16),
            vmem((2, TOKENS, narrow), BF16),
            vmem((2, shard, narrow), F32),
            vmem((TOKENS, wide), BF16),
            vmem((TOKENS, wide), BF16),
            vmem((2, TOKENS, narrow), BF16),
            vmem((2, shard, narrow), BF16),
            vmem((kvh, 2, nx, nz, 2, 16, HEAD), BF16),
            vmem((10, 16, 128), F32),
            vmem((9, 16, 128), F32),
            vmem((2, TOKENS, narrow), F32),
            vmem((kvh, TOKENS, rows), F32),
            vmem((kvh, TOKENS, rows), F32),
            vmem((prompt, rows), F32),
            vmem((joined, rows), F32),
            vmem((joined, rows), F32),
            vmem((joined, rows), BF16),
            vmem((kvh, joined, rows), BF16),
            vmem((kvh, 2, nx, nz, 2, 16, HEAD), F32),
            vmem((kvh, nx, nz, 2, 16, HEAD), BF16),
            vmem((kvh, nx, nz, 2, 16, HEAD), BF16),
            vmem((kvh, nx, nz, 2, 16, HEAD), F32),
            vmem((kvh, nx, nz, 2, 16, HEAD), BF16),
            vmem((nx - 1, kvh, nz, 2, 16, HEAD), BF16),
            vmem((kvh, nz, 2, 16, HEAD), BF16),
            vmem((nz - 1, kvh, 2, 16, HEAD), BF16),
            sem((6,)),
            sem((5,)),
            sem((2,)),
            sem((2,)),
            sem((2,)),
            sem((2,)),
            sem((2, 2)),
            sem((2, 2)),
            sem((2, 2)),
            sem((2, 2)),
            sem((2,)),
            sem((2,)),
            sem((3,)),
            sem((3,)),
            sem((3, nx - 1)),
            sem((3, nx - 1)),
            sem((3, nz - 1)),
            sem((3, nz - 1)),
            sem((9,)),
            sem((9,)),
        ],
        compiler_params=pltpu.CompilerParams(
            collective_id=0,
            has_side_effects=True,
            vmem_limit_bytes=VMEM_LIMIT,
        ),
        cost_estimate=pl.CostEstimate(
            flops=1_400_000_000, bytes_accessed=3_000_000, transcendentals=1_400_000
        ),
    )(
        queries[0, 0],
        response_keys[0, 0],
        response_values[0, 0],
        prompt_key_rows[0],
        prompt_value_rows[0],
        upstream[0, 0],
        rewards,
        lengths,
    )
    gq, gok, gov, gpk, gpv = pl.pallas_call(
        store_kernel,
        out_shape=shapes,
        in_specs=[anywhere] * 5,
        out_specs=[anywhere] * 5,
        scratch_shapes=[vmem(x.shape, x.dtype) for x in shapes] + [sem((5,)), sem((5,))],
        compiler_params=pltpu.CompilerParams(vmem_limit_bytes=VMEM_LIMIT),
    )(*results)
    return gq[None, None], gok[None, None], gov[None, None], gpk[None], gpv[None]


def solution(mesh, dims=(4, 4, 4, 4)):
    four = P("group", "resp", None, None)
    three = P("group", "resp", None)
    two = P("group", "resp")
    return jax.shard_map(
        functools.partial(on_device, dims),
        mesh=mesh,
        in_specs=(four, four, four, three, three, four, two, two),
        out_specs=(four, four, four, three, three),
        check_vma=False,
    )
```

```python
import functools

import jax
import jax.numpy as jnp
from jax import lax
from jax.experimental import pallas as pl
from jax.experimental.pallas import tpu as pltpu
from jax.sharding import PartitionSpec as P

MESH = pl.DeviceIdType.MESH
KEY_HEADS = 4
QUERY_PER_KV = 4
HEAD = 128
TOKENS = 128
SCALE = HEAD ** (-0.5)
LOG2E = 1.4426950408889634
F32 = jnp.float32
BF16 = jnp.bfloat16
VMEM_LIMIT = 56 * 1024 * 1024


def dot(a, b, a_dim, b_dim):
    return lax.dot_general(
        a, b, (((a_dim,), (b_dim,)), ((), ())), preferred_element_type=F32
    )


def kernel(
    dims,
    q_hbm,
    ok_hbm,
    ov_hbm,
    pk_hbm,
    pv_hbm,
    up_hbm,
    reward_ref,
    length_ref,
    gq_hbm,
    gok_hbm,
    gov_hbm,
    gpk_hbm,
    gpv_hbm,
    gq_v,
    go_v,
    gp_v,
    q_v,
    up_v,
    own_v,
    shard_v,
    kv,
    stat,
    stat_in,
    own_grad,
    so_ref,
    dpo_ref,
    s_ref,
    e_ref,
    dp_ref,
    pb_ref,
    ds_ref,
    acc,
    cs,
    rc,
    part,
    xs,
    rx,
    zs,
    rz,
    in_sem,
    out_sem,
    gz_s,
    gz_r,
    gx_s,
    gx_r,
    gc_s,
    gc_r,
    sc_s,
    sc_r,
    sx_s,
    sx_r,
    sz_s,
    sz_r,
    t_s,
    t_r,
):
    nl, ny, nz, nx = dims
    prompt = nz * nx * 2 * 16
    rows = QUERY_PER_KV * TOKENS
    gi, ri = lax.axis_index("group"), lax.axis_index("resp")
    mc = lax.rem(ri, 2)
    mx = lax.rem(lax.div(ri, 2), nx)
    mz = lax.div(ri, 2 * nx)
    my = lax.rem(gi, ny)
    ml = lax.div(gi, ny)

    def device(c=mc, x=mx, z=mz, y=my, l=ml):
        return (l * ny + y, (z * nx + x) * 2 + c)

    def ahead(me, d, n):
        return lax.rem(me + d, n)

    def remote(src, dst, send, recv, to):
        return pltpu.make_async_remote_copy(
            src_ref=src,
            dst_ref=dst,
            send_sem=send,
            recv_sem=recv,
            device_id=to,
            device_id_type=MESH,
        )

    def pairs(me, n):
        flip = [me + 1 - 2 * lax.rem(me, 2)] if n > 1 else []
        return flip + ([n - 1 - me] if n > 2 else [])

    on_core = device(c=1 - mc)
    pair_y = [device(y=y) for y in pairs(my, ny)]
    pair_l = [device(l=l) for l in pairs(ml, nl)]
    on_x = [device(x=ahead(mx, d, nx)) for d in range(1, nx)]
    on_z = [device(z=ahead(mz, d, nz)) for d in range(1, nz)]
    partners = on_z + on_x + [on_core] + pair_y + pair_l
    barrier = pltpu.get_barrier_semaphore()
    for partner in partners:
        pl.semaphore_signal(barrier, inc=1, device_id=partner, device_id_type=MESH)

    loads = [
        pltpu.make_async_copy(src, dst, in_sem.at[i])
        for i, (src, dst) in enumerate(
            (
                (pk_hbm, shard_v.at[0]),
                (pv_hbm, shard_v.at[1]),
                (q_hbm, q_v),
                (ok_hbm, own_v.at[0]),
                (ov_hbm, own_v.at[1]),
                (up_hbm, up_v),
            )
        )
    ]
    for load in loads:
        load.start()

    reward = reward_ref[0, 0]
    length = length_ref[0, 0]
    stat[0, 0:8] = jnp.full((8, 128), reward, F32)
    stat[0, 8:16] = jnp.full((8, 128), length.astype(F32), F32)

    def start(copies):
        for copy in copies:
            copy.start()

    def arrive(copies):
        for copy in copies:
            copy.wait_recv()

    def drain(copies):
        for copy in copies:
            copy.wait_send()

    stages = [device(z=z) for z in pairs(mz, nz)]
    stages += [device(x=x) for x in pairs(mx, nx)] + [on_core]
    in_group = len(stages)
    stages += pair_y + pair_l

    def stat_copy(step):
        return remote(
            stat.at[step], stat_in.at[step], t_s.at[step], t_r.at[step], stages[step]
        )

    def stat_next(step):
        if step < len(stages):
            stat_copy(step).wait_recv()
            stat[step + 1] = stat[step] + stat_in[step]
            if step + 1 < len(stages):
                stat_copy(step + 1).start()

    pieces = (slice(0, 1), slice(1, 2), slice(2, 4))

    def gather_z(n):
        mine = kv.at[pieces[n], mc, mx, mz]
        return [
            remote(mine, mine, gz_s.at[n, d], gz_r.at[n, d], to)
            for d, to in enumerate(on_z)
        ]

    def gather_x(n):
        mine = kv.at[pieces[n], mc, mx]
        return [
            remote(mine, mine, gx_s.at[n, d], gx_r.at[n, d], to)
            for d, to in enumerate(on_x)
        ]

    def gather_c(n):
        mine = kv.at[pieces[n], mc]
        return [remote(mine, mine, gc_s.at[n], gc_r.at[n], on_core)]

    def z_to_x(n):
        arrive(gather_z(n))
        start(gather_x(n))

    def x_to_c(n):
        arrive(gather_x(n))
        start(gather_c(n))

    chunks = (slice(0, 2), slice(2, 3), slice(3, 4))

    def reduce_c(n):
        return [
            remote(cs.at[chunks[n]], rc.at[chunks[n]], sc_s.at[n], sc_r.at[n], on_core)
        ]

    def reduce_x(n):
        return [
            remote(
                xs.at[chunks[n], ahead(mx, d + 1, nx)],
                rx.at[d, chunks[n]],
                sx_s.at[n, d],
                sx_r.at[n, d],
                to,
            )
            for d, to in enumerate(on_x)
        ]

    def reduce_z(n):
        return [
            remote(
                zs.at[chunks[n], ahead(mz, d + 1, nz)],
                rz.at[d, chunks[n]],
                sz_s.at[n, d],
                sz_r.at[n, d],
                to,
            )
            for d, to in enumerate(on_z)
        ]

    def before_c(n, advantage):
        cs[chunks[n]] = (acc[chunks[n], 1 - mc] * advantage).astype(BF16)
        start(reduce_c(n))

    def after_c(n, advantage):
        arrive(reduce_c(n))
        both = acc[chunks[n], mc] * advantage + rc[chunks[n]].astype(F32)
        part[chunks[n]] = both
        xs[chunks[n]] = both.astype(BF16)
        start(reduce_x(n))

    def after_x(n):
        arrive(reduce_x(n))
        both = part[chunks[n], mx]
        for d in range(nx - 1):
            both = both + rx[d, chunks[n]].astype(F32)
        part[chunks[n], 0] = both
        zs[chunks[n]] = both.astype(BF16)
        start(reduce_z(n))

    def after_z(n, scale):
        arrive(reduce_z(n))
        both = part[chunks[n], 0, mz]
        for d in range(nz - 1):
            both = both + rz[d, chunks[n]].astype(F32)
        for i, g in enumerate(range(chunks[n].start, chunks[n].stop)):
            gp_v[0, :, head_cols(g)] = both[i, 0] * scale
            gp_v[1, :, head_cols(g)] = both[i, 1] * scale

    def head_cols(g):
        return slice(g * HEAD, (g + 1) * HEAD)

    def query_cols(g, j):
        lower = (g * QUERY_PER_KV + j) * HEAD
        return slice(lower, lower + HEAD)

    def stacked(ref, g):
        return jnp.concatenate(
            [ref[:, query_cols(g, j)] for j in range(QUERY_PER_KV)], axis=0
        )

    def prompt_rows(g, i):
        return kv[g, :, :, :, i].reshape(prompt, HEAD)

    def own_part(g):
        key = lax.broadcasted_iota(jnp.int32, (TOKENS, rows), 0)
        step = lax.broadcasted_iota(jnp.int32, (TOKENS, rows), 1) & (TOKENS - 1)
        scores = dot(own_v[0, :, head_cols(g)], stacked(q_v, g), 1, 1)
        so_ref[g] = jnp.where(key <= step, scores, -1e30)
        step = lax.broadcasted_iota(jnp.int32, (TOKENS, HEAD), 0)
        live = jnp.where(step < length, 1.0, 0.0)
        for j in range(QUERY_PER_KV):
            cols = query_cols(g, j)
            up_v[:, cols] = (up_v[:, cols].astype(F32) * live).astype(BF16)
        dpo_ref[g] = dot(own_v[1, :, head_cols(g)], stacked(up_v, g), 1, 1)

    def attend(g):
        q_g, grad_out = stacked(q_v, g), stacked(up_v, g)
        s_ref[...] = dot(prompt_rows(g, 0), q_g, 1, 1)
        dp_ref[0:prompt] = dot(prompt_rows(g, 1), grad_out, 1, 1)
        dp_ref[prompt:] = dpo_ref[g]
        top = jnp.maximum(
            jnp.max(s_ref[...], axis=0, keepdims=True),
            jnp.max(so_ref[g], axis=0, keepdims=True),
        )
        e_ref[0:prompt] = jnp.exp2((s_ref[...] - top) * (SCALE * LOG2E))
        e_ref[prompt:] = jnp.exp2((so_ref[g] - top) * (SCALE * LOG2E))
        inverse = 1.0 / jnp.sum(e_ref[...], axis=0, keepdims=True)
        pb_ref[...] = (e_ref[...] * inverse).astype(BF16)
        grad_values = dot(pb_ref[...], grad_out, 1, 0)
        acc[g, :, :, :, 1] = grad_values[0:prompt].reshape(2, nx, nz, 16, HEAD)
        own_grad[1, :, head_cols(g)] = grad_values[prompt:]
        delta = jnp.sum(pb_ref[...].astype(F32) * dp_ref[...], axis=0, keepdims=True)
        ds_ref[g] = ((e_ref[...] * inverse) * (dp_ref[...] - delta)).astype(BF16)
        grad_keys = SCALE * dot(ds_ref[g], q_g, 1, 0)
        acc[g, :, :, :, 0] = grad_keys[0:prompt].reshape(2, nx, nz, 16, HEAD)
        own_grad[0, :, head_cols(g)] = grad_keys[prompt:]

    def query_gradient(g, weight):
        turned = dot(prompt_rows(g, 0), ds_ref[g, 0:prompt], 0, 0) + dot(
            own_v[0, :, head_cols(g)], ds_ref[g, prompt:], 0, 0
        )
        for j in range(QUERY_PER_KV):
            block = turned[:, j * TOKENS : (j + 1) * TOKENS]
            gq_v[:, query_cols(g, j)] = (block.T * weight).astype(BF16)

    loads[0].wait()
    loads[1].wait()
    for g in range(KEY_HEADS):
        kv[g, mc, mx, mz, 0] = shard_v[0, :, head_cols(g)]
        kv[g, mc, mx, mz, 1] = shard_v[1, :, head_cols(g)]
    pl.semaphore_wait(barrier, len(partners))
    start(gather_z(0))
    start(gather_z(1))
    start(gather_z(2))
    stat_copy(0).start()
    z_to_x(0)
    stat_next(0)
    z_to_x(1)
    for load in loads[2:]:
        load.wait()
    own_part(0)
    x_to_c(0)
    z_to_x(2)
    stat_next(1)
    own_part(1)
    x_to_c(1)
    stat_next(2)
    own_part(2)
    stat_next(3)
    arrive(gather_c(0))
    attend(0)
    x_to_c(2)
    stat_next(4)
    own_part(3)
    arrive(gather_c(1))
    attend(1)
    advantage = (reward - stat[in_group, 0:1] / (nz * nx * 2)).reshape(1, 1, 1, 1, 1, 128)
    before_c(0, advantage)
    stat_next(5)
    arrive(gather_c(2))
    attend(2)
    before_c(1, advantage)
    after_c(0, advantage)
    stat_next(6)
    attend(3)
    before_c(2, advantage)
    after_c(1, advantage)
    after_x(0)
    stat_next(7)
    after_c(2, advantage)
    after_x(1)
    stat_next(8)
    unit = 1.0 / stat[len(stages), 8:9]
    weight = (reward - stat[in_group, 0:1] / (nz * nx * 2)) * unit
    query_gradient(0, weight * SCALE)
    query_gradient(1, weight * SCALE)
    after_x(2)
    query_gradient(2, weight * SCALE)
    query_gradient(3, weight * SCALE)
    for g in range(KEY_HEADS):
        for i in range(2):
            go_v[i, :, head_cols(g)] = (own_grad[i, :, head_cols(g)] * weight).astype(BF16)
    stores = [
        pltpu.make_async_copy(src, dst, out_sem.at[i])
        for i, (src, dst) in enumerate(
            (
                (gq_v, gq_hbm),
                (go_v.at[0], gok_hbm),
                (go_v.at[1], gov_hbm),
                (gp_v.at[0], gpk_hbm),
                (gp_v.at[1], gpv_hbm),
            )
        )
    ]
    start(stores[0:3])
    after_z(0, unit)
    after_z(1, unit)
    after_z(2, unit)
    start(stores[3:5])
    for step in range(len(stages)):
        stat_copy(step).wait_send()
    for n in range(len(pieces)):
        drain(gather_z(n))
        drain(gather_x(n))
        drain(gather_c(n))
    for n in range(len(chunks)):
        drain(reduce_c(n))
        drain(reduce_x(n))
        drain(reduce_z(n))
    for store in stores:
        store.wait()


def store_kernel(*refs):
    sources, targets, holds = refs[0:5], refs[5:10], refs[10:15]
    in_sem, out_sem = refs[15:17]
    ins = [
        pltpu.make_async_copy(sources[i], holds[i], in_sem.at[i]) for i in range(5)
    ]
    outs = [
        pltpu.make_async_copy(holds[i], targets[i], out_sem.at[i]) for i in range(5)
    ]
    for copy in ins:
        copy.start()
    for i in (1, 2, 3, 4, 0):
        ins[i].wait()
        outs[i].start()
    for copy in outs:
        copy.wait()


def on_device(
    dims,
    queries,
    response_keys,
    response_values,
    prompt_key_rows,
    prompt_value_rows,
    upstream,
    rewards,
    lengths,
):
    nl, ny, nz, nx = dims
    kvh, rows = KEY_HEADS, QUERY_PER_KV * TOKENS
    prompt = nz * nx * 2 * 16
    joined = prompt + TOKENS
    wide, narrow = queries.shape[3], response_keys.shape[3]
    shard = prompt_key_rows.shape[1]
    vmem, sem = pltpu.VMEM, pltpu.SemaphoreType.DMA
    anywhere = pl.BlockSpec(memory_space=pl.ANY)
    scalar = pl.BlockSpec(memory_space=pltpu.SMEM)
    shapes = (
        jax.ShapeDtypeStruct((TOKENS, wide), BF16),
        jax.ShapeDtypeStruct((TOKENS, narrow), BF16),
        jax.ShapeDtypeStruct((TOKENS, narrow), BF16),
        jax.ShapeDtypeStruct((shard, narrow), F32),
        jax.ShapeDtypeStruct((shard, narrow), F32),
    )
    results = pl.pallas_call(
        functools.partial(kernel, dims),
        out_shape=shapes,
        in_specs=[anywhere] * 6 + [scalar] * 2,
        out_specs=[anywhere] * 5,
        scratch_shapes=[
            vmem((TOKENS, wide), BF16),
            vmem((2, TOKENS, narrow), BF16),
            vmem((2, shard, narrow), F32),
            vmem((TOKENS, wide), BF16),
            vmem((TOKENS, wide), BF16),
            vmem((2, TOKENS, narrow), BF16),
            vmem((2, shard, narrow), BF16),
            vmem((kvh, 2, nx, nz, 2, 16, HEAD), BF16),
            vmem((10, 16, 128), F32),
            vmem((9, 16, 128), F32),
            vmem((2, TOKENS, narrow), F32),
            vmem((kvh, TOKENS, rows), F32),
            vmem((kvh, TOKENS, rows), F32),
            vmem((prompt, rows), F32),
            vmem((joined, rows), F32),
            vmem((joined, rows), F32),
            vmem((joined, rows), BF16),
            vmem((kvh, joined, rows), BF16),
            vmem((kvh, 2, nx, nz, 2, 16, HEAD), F32),
            vmem((kvh, nx, nz, 2, 16, HEAD), BF16),
            vmem((kvh, nx, nz, 2, 16, HEAD), BF16),
            vmem((kvh, nx, nz, 2, 16, HEAD), F32),
            vmem((kvh, nx, nz, 2, 16, HEAD), BF16),
            vmem((nx - 1, kvh, nz, 2, 16, HEAD), BF16),
            vmem((kvh, nz, 2, 16, HEAD), BF16),
            vmem((nz - 1, kvh, 2, 16, HEAD), BF16),
            sem((6,)),
            sem((5,)),
            sem((3, nz - 1)),
            sem((3, nz - 1)),
            sem((3, nx - 1)),
            sem((3, nx - 1)),
            sem((3,)),
            sem((3,)),
            sem((3,)),
            sem((3,)),
            sem((3, nx - 1)),
            sem((3, nx - 1)),
            sem((3, nz - 1)),
            sem((3, nz - 1)),
            sem((9,)),
            sem((9,)),
        ],
        compiler_params=pltpu.CompilerParams(
            collective_id=0,
            has_side_effects=True,
            vmem_limit_bytes=VMEM_LIMIT,
        ),
        cost_estimate=pl.CostEstimate(
            flops=1_400_000_000, bytes_accessed=3_000_000, transcendentals=1_400_000
        ),
    )(
        queries[0, 0],
        response_keys[0, 0],
        response_values[0, 0],
        prompt_key_rows[0],
        prompt_value_rows[0],
        upstream[0, 0],
        rewards,
        lengths,
    )
    gq, gok, gov, gpk, gpv = pl.pallas_call(
        store_kernel,
        out_shape=shapes,
        in_specs=[anywhere] * 5,
        out_specs=[anywhere] * 5,
        scratch_shapes=[vmem(x.shape, x.dtype) for x in shapes] + [sem((5,)), sem((5,))],
        compiler_params=pltpu.CompilerParams(vmem_limit_bytes=VMEM_LIMIT),
    )(*results)
    return gq[None, None], gok[None, None], gov[None, None], gpk[None], gpv[None]


def solution(mesh, dims=(4, 4, 4, 4)):
    four = P("group", "resp", None, None)
    three = P("group", "resp", None)
    two = P("group", "resp")
    return jax.shard_map(
        functools.partial(on_device, dims),
        mesh=mesh,
        in_specs=(four, four, four, three, three, four, two, two),
        out_specs=(four, four, four, three, three),
        check_vma=False,
    )
```

```python
import functools

import jax
import jax.numpy as jnp
from jax import lax
from jax.experimental import pallas as pl
from jax.experimental.pallas import tpu as pltpu
from jax.sharding import PartitionSpec as P

MESH = pl.DeviceIdType.MESH
KEY_HEADS = 4
QUERY_PER_KV = 4
HEAD = 128
TOKENS = 128
SCALE = HEAD ** (-0.5)
LOG2E = 1.4426950408889634
F32 = jnp.float32
BF16 = jnp.bfloat16
VMEM_LIMIT = 56 * 1024 * 1024


def dot(a, b, a_dim, b_dim):
    return lax.dot_general(
        a, b, (((a_dim,), (b_dim,)), ((), ())), preferred_element_type=F32
    )


def kernel(
    dims,
    q_hbm,
    ok_hbm,
    ov_hbm,
    pk_hbm,
    pv_hbm,
    up_hbm,
    reward_ref,
    length_ref,
    gq_hbm,
    gok_hbm,
    gov_hbm,
    gpk_hbm,
    gpv_hbm,
    gq_v,
    go_v,
    gp_v,
    q_v,
    up_v,
    own_v,
    shard_v,
    kv,
    stat,
    stat_in,
    own_grad,
    inverse_ref,
    so_ref,
    dpo_ref,
    s_ref,
    e_ref,
    dp_ref,
    pb_ref,
    ds_ref,
    acc,
    cs,
    rc,
    part,
    xs,
    rx,
    zs,
    rz,
    in_sem,
    out_sem,
    gz_s,
    gz_r,
    gx_s,
    gx_r,
    gc_s,
    gc_r,
    sc_s,
    sc_r,
    sx_s,
    sx_r,
    sz_s,
    sz_r,
    t_s,
    t_r,
):
    nl, ny, nz, nx = dims
    prompt = nz * nx * 2 * 16
    rows = QUERY_PER_KV * TOKENS
    gi, ri = lax.axis_index("group"), lax.axis_index("resp")
    mc = lax.rem(ri, 2)
    mx = lax.rem(lax.div(ri, 2), nx)
    mz = lax.div(ri, 2 * nx)
    my = lax.rem(gi, ny)
    ml = lax.div(gi, ny)

    def device(c=mc, x=mx, z=mz, y=my, l=ml):
        return (l * ny + y, (z * nx + x) * 2 + c)

    def ahead(me, d, n):
        return lax.rem(me + d, n)

    def remote(src, dst, send, recv, to):
        return pltpu.make_async_remote_copy(
            src_ref=src,
            dst_ref=dst,
            send_sem=send,
            recv_sem=recv,
            device_id=to,
            device_id_type=MESH,
        )

    def pairs(me, n):
        flip = [me + 1 - 2 * lax.rem(me, 2)] if n > 1 else []
        return flip + ([n - 1 - me] if n > 2 else [])

    on_core = device(c=1 - mc)
    pair_y = [device(y=y) for y in pairs(my, ny)]
    pair_l = [device(l=l) for l in pairs(ml, nl)]
    on_x = [device(x=ahead(mx, d, nx)) for d in range(1, nx)]
    on_z = [device(z=ahead(mz, d, nz)) for d in range(1, nz)]
    partners = on_z + on_x + [on_core] + pair_y + pair_l
    barrier = pltpu.get_barrier_semaphore()
    for partner in partners:
        pl.semaphore_signal(barrier, inc=1, device_id=partner, device_id_type=MESH)

    loads = [
        pltpu.make_async_copy(src, dst, in_sem.at[i])
        for i, (src, dst) in enumerate(
            (
                (pk_hbm, shard_v.at[0]),
                (pv_hbm, shard_v.at[1]),
                (q_hbm, q_v),
                (ok_hbm, own_v.at[0]),
                (ov_hbm, own_v.at[1]),
                (up_hbm, up_v),
            )
        )
    ]
    for load in loads:
        load.start()

    reward = reward_ref[0, 0]
    length = length_ref[0, 0]
    stat[0, 0:8] = jnp.full((8, 128), reward, F32)
    stat[0, 8:16] = jnp.full((8, 128), length.astype(F32), F32)

    def start(copies):
        for copy in copies:
            copy.start()

    def arrive(copies):
        for copy in copies:
            copy.wait_recv()

    def drain(copies):
        for copy in copies:
            copy.wait_send()

    stages = [on_z, on_x, [on_core]] + [[to] for to in pair_y + pair_l]
    in_group = 3

    def stat_copies(step):
        return [
            remote(
                stat.at[step],
                stat_in.at[step, d],
                t_s.at[step, d],
                t_r.at[step, d],
                to,
            )
            for d, to in enumerate(stages[step])
        ]

    def stat_next(step):
        if step < len(stages):
            arrive(stat_copies(step))
            total = stat[step]
            for d in range(len(stages[step])):
                total = total + stat_in[step, d]
            stat[step + 1] = total
            if step + 1 < len(stages):
                start(stat_copies(step + 1))

    pieces = (slice(0, 1), slice(1, 2), slice(2, 4))

    def gather_z(n):
        mine = kv.at[pieces[n], mc, mx, mz]
        return [
            remote(mine, mine, gz_s.at[n, d], gz_r.at[n, d], to)
            for d, to in enumerate(on_z)
        ]

    def gather_x(n):
        mine = kv.at[pieces[n], mc, mx]
        return [
            remote(mine, mine, gx_s.at[n, d], gx_r.at[n, d], to)
            for d, to in enumerate(on_x)
        ]

    def gather_c(n):
        mine = kv.at[pieces[n], mc]
        return [remote(mine, mine, gc_s.at[n], gc_r.at[n], on_core)]

    def z_to_x(n):
        arrive(gather_z(n))
        start(gather_x(n))

    def x_to_c(n):
        arrive(gather_x(n))
        start(gather_c(n))

    chunks = (slice(0, 2), slice(2, 3), slice(3, 4))

    def reduce_c(n):
        return [
            remote(cs.at[chunks[n]], rc.at[chunks[n]], sc_s.at[n], sc_r.at[n], on_core)
        ]

    def reduce_x(n):
        return [
            remote(
                xs.at[chunks[n], ahead(mx, d + 1, nx)],
                rx.at[d, chunks[n]],
                sx_s.at[n, d],
                sx_r.at[n, d],
                to,
            )
            for d, to in enumerate(on_x)
        ]

    def reduce_z(n):
        return [
            remote(
                zs.at[chunks[n], ahead(mz, d + 1, nz)],
                rz.at[d, chunks[n]],
                sz_s.at[n, d],
                sz_r.at[n, d],
                to,
            )
            for d, to in enumerate(on_z)
        ]

    def before_c(n, advantage):
        cs[chunks[n]] = (acc[chunks[n], 1 - mc] * advantage).astype(BF16)
        start(reduce_c(n))

    def after_c(n, advantage):
        arrive(reduce_c(n))
        both = acc[chunks[n], mc] * advantage + rc[chunks[n]].astype(F32)
        part[chunks[n]] = both
        xs[chunks[n]] = both.astype(BF16)
        start(reduce_x(n))

    def after_x(n):
        arrive(reduce_x(n))
        both = part[chunks[n], mx]
        for d in range(nx - 1):
            both = both + rx[d, chunks[n]].astype(F32)
        part[chunks[n], 0] = both
        zs[chunks[n]] = both.astype(BF16)
        start(reduce_z(n))

    def after_z(n, scale):
        arrive(reduce_z(n))
        both = part[chunks[n], 0, mz]
        for d in range(nz - 1):
            both = both + rz[d, chunks[n]].astype(F32)
        for i, g in enumerate(range(chunks[n].start, chunks[n].stop)):
            gp_v[0, :, head_cols(g)] = both[i, 0] * scale
            gp_v[1, :, head_cols(g)] = both[i, 1] * scale

    def head_cols(g):
        return slice(g * HEAD, (g + 1) * HEAD)

    def query_cols(g, j):
        lower = (g * QUERY_PER_KV + j) * HEAD
        return slice(lower, lower + HEAD)

    def stacked(ref, g):
        return jnp.concatenate(
            [ref[:, query_cols(g, j)] for j in range(QUERY_PER_KV)], axis=0
        )

    def prompt_rows(g, i):
        return kv[g, :, :, :, i].reshape(prompt, HEAD)

    def own_part(g):
        key = lax.broadcasted_iota(jnp.int32, (TOKENS, rows), 0)
        step = lax.broadcasted_iota(jnp.int32, (TOKENS, rows), 1) & (TOKENS - 1)
        scores = dot(own_v[0, :, head_cols(g)], stacked(q_v, g), 1, 1)
        so_ref[g] = jnp.where(key <= step, scores, -1e30)
        step = lax.broadcasted_iota(jnp.int32, (TOKENS, HEAD), 0)
        live = jnp.where(step < length, 1.0, 0.0)
        for j in range(QUERY_PER_KV):
            cols = query_cols(g, j)
            up_v[:, cols] = (up_v[:, cols].astype(F32) * live).astype(BF16)
        dpo_ref[g] = dot(own_v[1, :, head_cols(g)], stacked(up_v, g), 1, 1)

    def forward(g):
        q_g, grad_out = stacked(q_v, g), stacked(up_v, g)
        s_ref[...] = dot(prompt_rows(g, 0), q_g, 1, 1)
        dp_ref[0:prompt] = dot(prompt_rows(g, 1), grad_out, 1, 1)
        dp_ref[prompt:] = dpo_ref[g]
        top = jnp.maximum(
            jnp.max(s_ref[...], axis=0, keepdims=True),
            jnp.max(so_ref[g], axis=0, keepdims=True),
        )
        e_ref[0:prompt] = jnp.exp2((s_ref[...] - top) * (SCALE * LOG2E))
        e_ref[prompt:] = jnp.exp2((so_ref[g] - top) * (SCALE * LOG2E))
        inverse = 1.0 / jnp.sum(e_ref[...], axis=0, keepdims=True)
        pb_ref[...] = (e_ref[...] * inverse).astype(BF16)
        inverse_ref[...] = inverse

    def backward(g):
        q_g, grad_out = stacked(q_v, g), stacked(up_v, g)
        inverse = inverse_ref[...]
        grad_values = dot(pb_ref[...], grad_out, 1, 0)
        acc[g, :, :, :, 1] = grad_values[0:prompt].reshape(2, nx, nz, 16, HEAD)
        own_grad[1, :, head_cols(g)] = grad_values[prompt:]
        delta = jnp.sum(pb_ref[...].astype(F32) * dp_ref[...], axis=0, keepdims=True)
        ds_ref[g] = ((e_ref[...] * inverse) * (dp_ref[...] - delta)).astype(BF16)
        grad_keys = SCALE * dot(ds_ref[g], q_g, 1, 0)
        acc[g, :, :, :, 0] = grad_keys[0:prompt].reshape(2, nx, nz, 16, HEAD)
        own_grad[0, :, head_cols(g)] = grad_keys[prompt:]

    def query_gradient(g, weight):
        turned = dot(prompt_rows(g, 0), ds_ref[g, 0:prompt], 0, 0) + dot(
            own_v[0, :, head_cols(g)], ds_ref[g, prompt:], 0, 0
        )
        for j in range(QUERY_PER_KV):
            block = turned[:, j * TOKENS : (j + 1) * TOKENS]
            gq_v[:, query_cols(g, j)] = (block.T * weight).astype(BF16)

    loads[0].wait()
    loads[1].wait()
    for g in range(KEY_HEADS):
        kv[g, mc, mx, mz, 0] = shard_v[0, :, head_cols(g)]
        kv[g, mc, mx, mz, 1] = shard_v[1, :, head_cols(g)]
    pl.semaphore_wait(barrier, len(partners))
    start(gather_z(0))
    start(stat_copies(0))
    start(gather_z(1))
    start(gather_z(2))
    z_to_x(0)
    z_to_x(1)
    stat_next(0)
    for load in loads[2:]:
        load.wait()
    own_part(0)
    x_to_c(0)
    z_to_x(2)
    own_part(1)
    x_to_c(1)
    stat_next(1)
    own_part(2)
    arrive(gather_c(0))
    forward(0)
    x_to_c(2)
    backward(0)
    stat_next(2)
    own_part(3)
    arrive(gather_c(1))
    forward(1)
    backward(1)
    advantage = (reward - stat[in_group, 0:1] / (nz * nx * 2)).reshape(1, 1, 1, 1, 1, 128)
    before_c(0, advantage)
    stat_next(3)
    arrive(gather_c(2))
    forward(2)
    after_c(0, advantage)
    backward(2)
    before_c(1, advantage)
    stat_next(4)
    forward(3)
    after_c(1, advantage)
    after_x(0)
    backward(3)
    before_c(2, advantage)
    stat_next(5)
    after_x(1)
    after_c(2, advantage)
    stat_next(6)
    unit = 1.0 / stat[len(stages), 8:9]
    weight = (reward - stat[in_group, 0:1] / (nz * nx * 2)) * unit
    query_gradient(0, weight * SCALE)
    query_gradient(1, weight * SCALE)
    after_x(2)
    query_gradient(2, weight * SCALE)
    query_gradient(3, weight * SCALE)
    for g in range(KEY_HEADS):
        for i in range(2):
            go_v[i, :, head_cols(g)] = (own_grad[i, :, head_cols(g)] * weight).astype(BF16)
    stores = [
        pltpu.make_async_copy(src, dst, out_sem.at[i])
        for i, (src, dst) in enumerate(
            (
                (gq_v, gq_hbm),
                (go_v.at[0], gok_hbm),
                (go_v.at[1], gov_hbm),
                (gp_v.at[0], gpk_hbm),
                (gp_v.at[1], gpv_hbm),
            )
        )
    ]
    start(stores[0:3])
    for step in range(len(stages)):
        drain(stat_copies(step))
    for n in range(len(pieces)):
        drain(gather_z(n))
        drain(gather_x(n))
        drain(gather_c(n))
    after_z(0, unit)
    after_z(1, unit)
    for n in range(len(chunks)):
        drain(reduce_c(n))
        drain(reduce_x(n))
        if n + 1 < len(chunks):
            drain(reduce_z(n))
    after_z(2, unit)
    start(stores[3:5])
    drain(reduce_z(len(chunks) - 1))
    for store in stores:
        store.wait()


def store_kernel(*refs):
    sources, targets, holds = refs[0:5], refs[5:10], refs[10:15]
    in_sem, out_sem = refs[15:17]
    ins = [
        pltpu.make_async_copy(sources[i], holds[i], in_sem.at[i]) for i in range(5)
    ]
    outs = [
        pltpu.make_async_copy(holds[i], targets[i], out_sem.at[i]) for i in range(5)
    ]
    for copy in ins:
        copy.start()
    for i in (1, 2, 3, 4, 0):
        ins[i].wait()
        outs[i].start()
    for copy in outs:
        copy.wait()


def on_device(
    dims,
    queries,
    response_keys,
    response_values,
    prompt_key_rows,
    prompt_value_rows,
    upstream,
    rewards,
    lengths,
):
    nl, ny, nz, nx = dims
    kvh, rows = KEY_HEADS, QUERY_PER_KV * TOKENS
    prompt = nz * nx * 2 * 16
    joined = prompt + TOKENS
    wide, narrow = queries.shape[3], response_keys.shape[3]
    shard = prompt_key_rows.shape[1]
    vmem, sem = pltpu.VMEM, pltpu.SemaphoreType.DMA
    anywhere = pl.BlockSpec(memory_space=pl.ANY)
    scalar = pl.BlockSpec(memory_space=pltpu.SMEM)
    shapes = (
        jax.ShapeDtypeStruct((TOKENS, wide), BF16),
        jax.ShapeDtypeStruct((TOKENS, narrow), BF16),
        jax.ShapeDtypeStruct((TOKENS, narrow), BF16),
        jax.ShapeDtypeStruct((shard, narrow), F32),
        jax.ShapeDtypeStruct((shard, narrow), F32),
    )
    results = pl.pallas_call(
        functools.partial(kernel, dims),
        out_shape=shapes,
        in_specs=[anywhere] * 6 + [scalar] * 2,
        out_specs=[anywhere] * 5,
        scratch_shapes=[
            vmem((TOKENS, wide), BF16),
            vmem((2, TOKENS, narrow), BF16),
            vmem((2, shard, narrow), F32),
            vmem((TOKENS, wide), BF16),
            vmem((TOKENS, wide), BF16),
            vmem((2, TOKENS, narrow), BF16),
            vmem((2, shard, narrow), BF16),
            vmem((kvh, 2, nx, nz, 2, 16, HEAD), BF16),
            vmem((10, 16, 128), F32),
            vmem((7, 3, 16, 128), F32),
            vmem((2, TOKENS, narrow), F32),
            vmem((1, rows), F32),
            vmem((kvh, TOKENS, rows), F32),
            vmem((kvh, TOKENS, rows), F32),
            vmem((prompt, rows), F32),
            vmem((joined, rows), F32),
            vmem((joined, rows), F32),
            vmem((joined, rows), BF16),
            vmem((kvh, joined, rows), BF16),
            vmem((kvh, 2, nx, nz, 2, 16, HEAD), F32),
            vmem((kvh, nx, nz, 2, 16, HEAD), BF16),
            vmem((kvh, nx, nz, 2, 16, HEAD), BF16),
            vmem((kvh, nx, nz, 2, 16, HEAD), F32),
            vmem((kvh, nx, nz, 2, 16, HEAD), BF16),
            vmem((nx - 1, kvh, nz, 2, 16, HEAD), BF16),
            vmem((kvh, nz, 2, 16, HEAD), BF16),
            vmem((nz - 1, kvh, 2, 16, HEAD), BF16),
            sem((6,)),
            sem((5,)),
            sem((3, nz - 1)),
            sem((3, nz - 1)),
            sem((3, nx - 1)),
            sem((3, nx - 1)),
            sem((3,)),
            sem((3,)),
            sem((3,)),
            sem((3,)),
            sem((3, nx - 1)),
            sem((3, nx - 1)),
            sem((3, nz - 1)),
            sem((3, nz - 1)),
            sem((7, 3)),
            sem((7, 3)),
        ],
        compiler_params=pltpu.CompilerParams(
            collective_id=0,
            has_side_effects=True,
            vmem_limit_bytes=VMEM_LIMIT,
        ),
        cost_estimate=pl.CostEstimate(
            flops=1_400_000_000, bytes_accessed=3_000_000, transcendentals=1_400_000
        ),
    )(
        queries[0, 0],
        response_keys[0, 0],
        response_values[0, 0],
        prompt_key_rows[0],
        prompt_value_rows[0],
        upstream[0, 0],
        rewards,
        lengths,
    )
    gq, gok, gov, gpk, gpv = pl.pallas_call(
        store_kernel,
        out_shape=shapes,
        in_specs=[anywhere] * 5,
        out_specs=[anywhere] * 5,
        scratch_shapes=[vmem(x.shape, x.dtype) for x in shapes] + [sem((5,)), sem((5,))],
        compiler_params=pltpu.CompilerParams(vmem_limit_bytes=VMEM_LIMIT),
    )(*results)
    return gq[None, None], gok[None, None], gov[None, None], gpk[None], gpv[None]


def solution(mesh, dims=(4, 4, 4, 4)):
    four = P("group", "resp", None, None)
    three = P("group", "resp", None)
    two = P("group", "resp")
    return jax.shard_map(
        functools.partial(on_device, dims),
        mesh=mesh,
        in_specs=(four, four, four, three, three, four, two, two),
        out_specs=(four, four, four, three, three),
        check_vma=False,
    )
```

```python
import functools

import jax
import jax.numpy as jnp
from jax import lax
from jax.experimental import pallas as pl
from jax.experimental.pallas import tpu as pltpu
from jax.sharding import PartitionSpec as P

MESH = pl.DeviceIdType.MESH
KEY_HEADS = 4
QUERY_PER_KV = 4
HEAD = 128
TOKENS = 128
SCALE = HEAD ** (-0.5)
LOG2E = 1.4426950408889634
F32 = jnp.float32
BF16 = jnp.bfloat16
VMEM_LIMIT = 56 * 1024 * 1024


def dot(a, b, a_dim, b_dim):
    return lax.dot_general(
        a, b, (((a_dim,), (b_dim,)), ((), ())), preferred_element_type=F32
    )


def kernel(
    dims,
    q_hbm,
    ok_hbm,
    ov_hbm,
    pk_hbm,
    pv_hbm,
    up_hbm,
    reward_hbm,
    length_hbm,
    gq_hbm,
    gok_hbm,
    gov_hbm,
    gpk_hbm,
    gpv_hbm,
    gq_v,
    go_v,
    gp_v,
    q_v,
    up_v,
    own_v,
    shard_v,
    kv,
    stat,
    stat_in,
    own_grad,
    inverse_ref,
    reward_ref,
    length_ref,
    so_ref,
    dpo_ref,
    s_ref,
    e_ref,
    dp_ref,
    pb_ref,
    ds_ref,
    acc,
    cs,
    rc,
    part,
    xs,
    rx,
    zs,
    rz,
    in_sem,
    out_sem,
    gz_s,
    gz_r,
    gx_s,
    gx_r,
    gc_s,
    gc_r,
    sc_s,
    sc_r,
    sx_s,
    sx_r,
    sz_s,
    sz_r,
    t_s,
    t_r,
):
    nl, ny, nz, nx = dims
    prompt = nz * nx * 2 * 16
    rows = QUERY_PER_KV * TOKENS
    gi, ri = lax.axis_index("group"), lax.axis_index("resp")
    mc = lax.rem(ri, 2)
    mx = lax.rem(lax.div(ri, 2), nx)
    mz = lax.div(ri, 2 * nx)
    my = lax.rem(gi, ny)
    ml = lax.div(gi, ny)

    def device(c=mc, x=mx, z=mz, y=my, l=ml):
        return (l * ny + y, (z * nx + x) * 2 + c)

    def ahead(me, d, n):
        return lax.rem(me + d, n)

    def remote(src, dst, send, recv, to):
        return pltpu.make_async_remote_copy(
            src_ref=src,
            dst_ref=dst,
            send_sem=send,
            recv_sem=recv,
            device_id=to,
            device_id_type=MESH,
        )

    def pairs(me, n):
        flip = [me + 1 - 2 * lax.rem(me, 2)] if n > 1 else []
        return flip + ([n - 1 - me] if n > 2 else [])

    on_core = device(c=1 - mc)
    pair_y = [device(y=y) for y in pairs(my, ny)]
    pair_l = [device(l=l) for l in pairs(ml, nl)]
    on_x = [device(x=ahead(mx, d, nx)) for d in range(1, nx)]
    on_z = [device(z=ahead(mz, d, nz)) for d in range(1, nz)]
    partners = on_z + on_x + [on_core] + pair_y + pair_l
    barrier = pltpu.get_barrier_semaphore()
    for partner in partners:
        pl.semaphore_signal(barrier, inc=1, device_id=partner, device_id_type=MESH)

    loads = [
        pltpu.make_async_copy(src, dst, in_sem.at[i])
        for i, (src, dst) in enumerate(
            (
                (pk_hbm, shard_v.at[0]),
                (pv_hbm, shard_v.at[1]),
                (reward_hbm, reward_ref),
                (length_hbm, length_ref),
                (q_hbm, q_v),
                (ok_hbm, own_v.at[0]),
                (ov_hbm, own_v.at[1]),
                (up_hbm, up_v),
            )
        )
    ]
    for load in loads:
        load.start()

    loads[2].wait()
    loads[3].wait()
    reward = reward_ref[0, 0]
    length = length_ref[0, 0]
    stat[0, 0:8] = jnp.full((8, 128), reward, F32)
    stat[0, 8:16] = jnp.full((8, 128), length.astype(F32), F32)

    def start(copies):
        for copy in copies:
            copy.start()

    def arrive(copies):
        for copy in copies:
            copy.wait_recv()

    def drain(copies):
        for copy in copies:
            copy.wait_send()

    stages = [on_z, on_x, [on_core]] + [[to] for to in pair_y + pair_l]
    in_group = 3

    def stat_copies(step):
        return [
            remote(
                stat.at[step],
                stat_in.at[step, d],
                t_s.at[step, d],
                t_r.at[step, d],
                to,
            )
            for d, to in enumerate(stages[step])
        ]

    def stat_next(step):
        if step < len(stages):
            arrive(stat_copies(step))
            total = stat[step]
            for d in range(len(stages[step])):
                total = total + stat_in[step, d]
            stat[step + 1] = total
            if step + 1 < len(stages):
                start(stat_copies(step + 1))

    pieces = (slice(0, 2), slice(2, 4))

    def gather_z():
        mine = kv.at[:, mc, mx, mz]
        return [
            remote(mine, mine, gz_s.at[d], gz_r.at[d], to) for d, to in enumerate(on_z)
        ]

    def gather_x(n):
        mine = kv.at[pieces[n], mc, mx]
        return [
            remote(mine, mine, gx_s.at[n, d], gx_r.at[n, d], to)
            for d, to in enumerate(on_x)
        ]

    def gather_c(n):
        mine = kv.at[pieces[n], mc]
        return [remote(mine, mine, gc_s.at[n], gc_r.at[n], on_core)]

    def x_to_c(n):
        arrive(gather_x(n))
        start(gather_c(n))

    chunks = (slice(0, 2), slice(2, 3), slice(3, 4))

    def reduce_c(n):
        return [
            remote(cs.at[chunks[n]], rc.at[chunks[n]], sc_s.at[n], sc_r.at[n], on_core)
        ]

    def reduce_x(n):
        return [
            remote(
                xs.at[chunks[n], ahead(mx, d + 1, nx)],
                rx.at[d, chunks[n]],
                sx_s.at[n, d],
                sx_r.at[n, d],
                to,
            )
            for d, to in enumerate(on_x)
        ]

    def reduce_z(n):
        return [
            remote(
                zs.at[chunks[n], ahead(mz, d + 1, nz)],
                rz.at[d, chunks[n]],
                sz_s.at[n, d],
                sz_r.at[n, d],
                to,
            )
            for d, to in enumerate(on_z)
        ]

    def before_c(n, advantage):
        cs[chunks[n]] = (acc[chunks[n], 1 - mc] * advantage).astype(BF16)
        start(reduce_c(n))

    def after_c(n, advantage):
        arrive(reduce_c(n))
        both = acc[chunks[n], mc] * advantage + rc[chunks[n]].astype(F32)
        part[chunks[n]] = both
        xs[chunks[n]] = both.astype(BF16)
        start(reduce_x(n))

    def after_x(n):
        arrive(reduce_x(n))
        both = part[chunks[n], mx]
        for d in range(nx - 1):
            both = both + rx[d, chunks[n]].astype(F32)
        part[chunks[n], 0] = both
        zs[chunks[n]] = both.astype(BF16)
        start(reduce_z(n))

    def after_z(n, scale):
        arrive(reduce_z(n))
        both = part[chunks[n], 0, mz]
        for d in range(nz - 1):
            both = both + rz[d, chunks[n]].astype(F32)
        for i, g in enumerate(range(chunks[n].start, chunks[n].stop)):
            gp_v[0, :, head_cols(g)] = both[i, 0] * scale
            gp_v[1, :, head_cols(g)] = both[i, 1] * scale

    def head_cols(g):
        if isinstance(g, int):
            return slice(g * HEAD, (g + 1) * HEAD)
        return pl.ds(pl.multiple_of(g * HEAD, HEAD), HEAD)

    def query_cols(g, j):
        return head_cols(g * QUERY_PER_KV + j)

    def each(lower, upper, body):
        def step(i, carry):
            body(i)
            return carry

        lax.fori_loop(lower, upper, step, 0)

    def stacked(ref, g):
        return jnp.concatenate(
            [ref[:, query_cols(g, j)] for j in range(QUERY_PER_KV)], axis=0
        )

    def prompt_rows(g, i):
        return kv[g, :, :, :, i].reshape(prompt, HEAD)

    def own_part(g):
        key = lax.broadcasted_iota(jnp.int32, (TOKENS, rows), 0)
        step = lax.broadcasted_iota(jnp.int32, (TOKENS, rows), 1) & (TOKENS - 1)
        scores = dot(own_v[0, :, head_cols(g)], stacked(q_v, g), 1, 1)
        so_ref[g] = jnp.where(key <= step, scores, -1e30)
        step = lax.broadcasted_iota(jnp.int32, (TOKENS, HEAD), 0)
        live = jnp.where(step < length, 1.0, 0.0)
        for j in range(QUERY_PER_KV):
            cols = query_cols(g, j)
            up_v[:, cols] = (up_v[:, cols].astype(F32) * live).astype(BF16)
        dpo_ref[g] = dot(own_v[1, :, head_cols(g)], stacked(up_v, g), 1, 1)

    def key_rows(i):
        return pl.ds(pl.multiple_of(i * TOKENS, TOKENS), TOKENS)

    tiles = prompt // TOKENS

    def column(x):
        return x.reshape(TOKENS // 8, 8, rows)

    def forward(g):
        q_g, grad_out = stacked(q_v, g), stacked(up_v, g)
        s_ref[0:prompt] = dot(prompt_rows(g, 0), q_g, 1, 1)
        s_ref[prompt:] = so_ref[g]
        dp_ref[0:prompt] = dot(prompt_rows(g, 1), grad_out, 1, 1)
        dp_ref[prompt:] = dpo_ref[g]

        def highest(i, top):
            return jnp.maximum(top, jnp.max(column(s_ref[key_rows(i)]), axis=0))

        top = lax.fori_loop(0, tiles + 1, highest, jnp.full((8, rows), -1e30, F32))
        top = jnp.max(top, axis=0, keepdims=True)

        def exponents(i, total):
            e = jnp.exp2((s_ref[key_rows(i)] - top) * (SCALE * LOG2E))
            e_ref[key_rows(i)] = e
            return total + jnp.sum(column(e), axis=0)

        total = lax.fori_loop(0, tiles + 1, exponents, jnp.zeros((8, rows), F32))
        inverse_ref[...] = 1.0 / jnp.sum(total, axis=0, keepdims=True)

    def backward(g):
        q_g, grad_out = stacked(q_v, g), stacked(up_v, g)
        inverse = inverse_ref[...]

        def narrow(i, delta):
            probs = e_ref[key_rows(i)] * inverse
            e_ref[key_rows(i)] = probs
            probs_b = probs.astype(BF16)
            pb_ref[key_rows(i)] = probs_b
            return delta + jnp.sum(
                column(probs_b.astype(F32) * dp_ref[key_rows(i)]), axis=0
            )

        delta = lax.fori_loop(0, tiles + 1, narrow, jnp.zeros((8, rows), F32))
        delta = jnp.sum(delta, axis=0, keepdims=True)

        def scores(i):
            ds_ref[g, key_rows(i)] = (
                e_ref[key_rows(i)] * (dp_ref[key_rows(i)] - delta)
            ).astype(BF16)

        each(0, tiles + 1, scores)
        grad_values = dot(pb_ref[...], grad_out, 1, 0)
        acc[g, :, :, :, 1] = grad_values[0:prompt].reshape(2, nx, nz, 16, HEAD)
        own_grad[1, :, head_cols(g)] = grad_values[prompt:]
        grad_keys = SCALE * dot(ds_ref[g], q_g, 1, 0)
        acc[g, :, :, :, 0] = grad_keys[0:prompt].reshape(2, nx, nz, 16, HEAD)
        own_grad[0, :, head_cols(g)] = grad_keys[prompt:]

    def query_gradient(g, weight):
        turned = dot(prompt_rows(g, 0), ds_ref[g, 0:prompt], 0, 0) + dot(
            own_v[0, :, head_cols(g)], ds_ref[g, prompt:], 0, 0
        )
        for j in range(QUERY_PER_KV):
            block = turned[:, j * TOKENS : (j + 1) * TOKENS]
            gq_v[:, query_cols(g, j)] = (block.T * weight).astype(BF16)

    loads[0].wait()
    loads[1].wait()
    for g in range(KEY_HEADS):
        kv[g, mc, mx, mz, 0] = shard_v[0, :, head_cols(g)]
        kv[g, mc, mx, mz, 1] = shard_v[1, :, head_cols(g)]
    pl.semaphore_wait(barrier, len(partners))
    start(gather_z())
    start(stat_copies(0))
    for load in loads[4:]:
        load.wait()
    arrive(gather_z())
    start(gather_x(0))
    start(gather_x(1))
    stat_next(0)
    each(0, 2, own_part)
    x_to_c(0)
    x_to_c(1)
    stat_next(1)
    each(2, 4, own_part)
    arrive(gather_c(0))
    forward(0)
    backward(0)
    stat_next(2)
    forward(1)
    backward(1)
    advantage = (reward - stat[in_group, 0:1] / (nz * nx * 2)).reshape(1, 1, 1, 1, 1, 128)
    before_c(0, advantage)
    stat_next(3)
    arrive(gather_c(1))
    forward(2)
    after_c(0, advantage)
    backward(2)
    before_c(1, advantage)
    stat_next(4)
    forward(3)
    after_c(1, advantage)
    after_x(0)
    backward(3)
    before_c(2, advantage)
    stat_next(5)
    after_x(1)
    after_c(2, advantage)
    stat_next(6)
    unit = 1.0 / stat[len(stages), 8:9]
    weight = (reward - stat[in_group, 0:1] / (nz * nx * 2)) * unit
    each(0, 2, lambda g: query_gradient(g, weight * SCALE))
    after_x(2)
    each(2, 4, lambda g: query_gradient(g, weight * SCALE))
    for g in range(KEY_HEADS):
        for i in range(2):
            go_v[i, :, head_cols(g)] = (own_grad[i, :, head_cols(g)] * weight).astype(BF16)
    stores = [
        pltpu.make_async_copy(src, dst, out_sem.at[i])
        for i, (src, dst) in enumerate(
            (
                (gq_v, gq_hbm),
                (go_v.at[0], gok_hbm),
                (go_v.at[1], gov_hbm),
                (gp_v.at[0], gpk_hbm),
                (gp_v.at[1], gpv_hbm),
            )
        )
    ]
    start(stores[0:3])
    for step in range(len(stages)):
        drain(stat_copies(step))
    drain(gather_z())
    for n in range(len(pieces)):
        drain(gather_x(n))
        drain(gather_c(n))
    after_z(0, unit)
    after_z(1, unit)
    for n in range(len(chunks)):
        drain(reduce_c(n))
        drain(reduce_x(n))
        if n + 1 < len(chunks):
            drain(reduce_z(n))
    after_z(2, unit)
    start(stores[3:5])
    drain(reduce_z(len(chunks) - 1))
    for store in stores:
        store.wait()


def store_kernel(*refs):
    sources, targets, holds = refs[0:5], refs[5:10], refs[10:15]
    in_sem, out_sem = refs[15:17]
    ins = [
        pltpu.make_async_copy(sources[i], holds[i], in_sem.at[i]) for i in range(5)
    ]
    outs = [
        pltpu.make_async_copy(holds[i], targets[i], out_sem.at[i]) for i in range(5)
    ]
    for copy in ins:
        copy.start()
    for i in (1, 2, 3, 4, 0):
        ins[i].wait()
        outs[i].start()
    for copy in outs:
        copy.wait()


def on_device(
    dims,
    queries,
    response_keys,
    response_values,
    prompt_key_rows,
    prompt_value_rows,
    upstream,
    rewards,
    lengths,
):
    nl, ny, nz, nx = dims
    kvh, rows = KEY_HEADS, QUERY_PER_KV * TOKENS
    prompt = nz * nx * 2 * 16
    joined = prompt + TOKENS
    wide, narrow = queries.shape[3], response_keys.shape[3]
    shard = prompt_key_rows.shape[1]
    vmem, sem = pltpu.VMEM, pltpu.SemaphoreType.DMA
    anywhere = pl.BlockSpec(memory_space=pl.ANY)
    shapes = (
        jax.ShapeDtypeStruct((TOKENS, wide), BF16),
        jax.ShapeDtypeStruct((TOKENS, narrow), BF16),
        jax.ShapeDtypeStruct((TOKENS, narrow), BF16),
        jax.ShapeDtypeStruct((shard, narrow), F32),
        jax.ShapeDtypeStruct((shard, narrow), F32),
    )
    results = pl.pallas_call(
        functools.partial(kernel, dims),
        out_shape=shapes,
        in_specs=[anywhere] * 8,
        out_specs=[anywhere] * 5,
        scratch_shapes=[
            vmem((TOKENS, wide), BF16),
            vmem((2, TOKENS, narrow), BF16),
            vmem((2, shard, narrow), F32),
            vmem((TOKENS, wide), BF16),
            vmem((TOKENS, wide), BF16),
            vmem((2, TOKENS, narrow), BF16),
            vmem((2, shard, narrow), BF16),
            vmem((kvh, 2, nx, nz, 2, 16, HEAD), BF16),
            vmem((10, 16, 128), F32),
            vmem((7, 3, 16, 128), F32),
            vmem((2, TOKENS, narrow), F32),
            vmem((1, rows), F32),
            pltpu.SMEM((1, 1), F32),
            pltpu.SMEM((1, 1), jnp.int32),
            vmem((kvh, TOKENS, rows), F32),
            vmem((kvh, TOKENS, rows), F32),
            vmem((joined, rows), F32),
            vmem((joined, rows), F32),
            vmem((joined, rows), F32),
            vmem((joined, rows), BF16),
            vmem((kvh, joined, rows), BF16),
            vmem((kvh, 2, nx, nz, 2, 16, HEAD), F32),
            vmem((kvh, nx, nz, 2, 16, HEAD), BF16),
            vmem((kvh, nx, nz, 2, 16, HEAD), BF16),
            vmem((kvh, nx, nz, 2, 16, HEAD), F32),
            vmem((kvh, nx, nz, 2, 16, HEAD), BF16),
            vmem((nx - 1, kvh, nz, 2, 16, HEAD), BF16),
            vmem((kvh, nz, 2, 16, HEAD), BF16),
            vmem((nz - 1, kvh, 2, 16, HEAD), BF16),
            sem((8,)),
            sem((5,)),
            sem((nz - 1,)),
            sem((nz - 1,)),
            sem((2, nx - 1)),
            sem((2, nx - 1)),
            sem((2,)),
            sem((2,)),
            sem((3,)),
            sem((3,)),
            sem((3, nx - 1)),
            sem((3, nx - 1)),
            sem((3, nz - 1)),
            sem((3, nz - 1)),
            sem((7, 3)),
            sem((7, 3)),
        ],
        compiler_params=pltpu.CompilerParams(
            collective_id=0,
            has_side_effects=True,
            vmem_limit_bytes=VMEM_LIMIT,
        ),
        cost_estimate=pl.CostEstimate(
            flops=1_400_000_000, bytes_accessed=3_000_000, transcendentals=1_400_000
        ),
    )(
        queries[0, 0],
        response_keys[0, 0],
        response_values[0, 0],
        prompt_key_rows[0],
        prompt_value_rows[0],
        upstream[0, 0],
        rewards,
        lengths,
    )
    gq, gok, gov, gpk, gpv = pl.pallas_call(
        store_kernel,
        out_shape=shapes,
        in_specs=[anywhere] * 5,
        out_specs=[anywhere] * 5,
        scratch_shapes=[vmem(x.shape, x.dtype) for x in shapes] + [sem((5,)), sem((5,))],
        compiler_params=pltpu.CompilerParams(vmem_limit_bytes=VMEM_LIMIT),
    )(*results)
    return gq[None, None], gok[None, None], gov[None, None], gpk[None], gpv[None]


def solution(mesh, dims=(4, 4, 4, 4)):
    four = P("group", "resp", None, None)
    three = P("group", "resp", None)
    two = P("group", "resp")
    return jax.shard_map(
        functools.partial(on_device, dims),
        mesh=mesh,
        in_specs=(four, four, four, three, three, four, two, two),
        out_specs=(four, four, four, three, three),
        check_vma=False,
    )
```

```python
import functools

import jax
import jax.numpy as jnp
from jax import lax
from jax.experimental import pallas as pl
from jax.experimental.pallas import tpu as pltpu
from jax.sharding import PartitionSpec as P

MESH = pl.DeviceIdType.MESH
KEY_HEADS = 4
QUERY_PER_KV = 4
HEAD = 128
TOKENS = 128
SCALE = HEAD ** (-0.5)
F32 = jnp.float32
BF16 = jnp.bfloat16
VMEM_LIMIT = 56 * 1024 * 1024


def dot(a, b, a_dim, b_dim):
    return lax.dot_general(
        a, b, (((a_dim,), (b_dim,)), ((), ())), preferred_element_type=F32
    )


def kernel(
    dims,
    q_hbm,
    ok_hbm,
    ov_hbm,
    pk_hbm,
    pv_hbm,
    up_hbm,
    reward_hbm,
    length_hbm,
    gq_hbm,
    gok_hbm,
    gov_hbm,
    gpk_hbm,
    gpv_hbm,
    gq_v,
    go_v,
    gp_v,
    q_v,
    up_v,
    own_v,
    shard_v,
    kv,
    stat,
    stat_in,
    own_grad,
    inverse_ref,
    reward_ref,
    length_ref,
    so_ref,
    dpo_ref,
    s_ref,
    e_ref,
    dp_ref,
    pb_ref,
    ds_ref,
    acc,
    cs,
    rc,
    part,
    xs,
    rx,
    zs,
    rz,
    in_sem,
    out_sem,
    gz_s,
    gz_r,
    gx_s,
    gx_r,
    gc_s,
    gc_r,
    sc_s,
    sc_r,
    sx_s,
    sx_r,
    sz_s,
    sz_r,
    t_s,
    t_r,
):
    nl, ny, nz, nx = dims
    prompt = nz * nx * 2 * 16
    rows = QUERY_PER_KV * TOKENS
    gi, ri = lax.axis_index("group"), lax.axis_index("resp")
    mc = lax.rem(ri, 2)
    mx = lax.rem(lax.div(ri, 2), nx)
    mz = lax.div(ri, 2 * nx)
    my = lax.rem(gi, ny)
    ml = lax.div(gi, ny)

    def device(c=mc, x=mx, z=mz, y=my, l=ml):
        return (l * ny + y, (z * nx + x) * 2 + c)

    def ahead(me, d, n):
        return lax.rem(me + d, n)

    def remote(src, dst, send, recv, to):
        return pltpu.make_async_remote_copy(
            src_ref=src,
            dst_ref=dst,
            send_sem=send,
            recv_sem=recv,
            device_id=to,
            device_id_type=MESH,
        )

    on_core = device(c=1 - mc)
    on_y = [device(y=ahead(my, d, ny)) for d in range(1, ny)]
    on_l = [device(l=ahead(ml, d, nl)) for d in range(1, nl)]
    on_x = [device(x=ahead(mx, d, nx)) for d in range(1, nx)]
    on_z = [device(z=ahead(mz, d, nz)) for d in range(1, nz)]
    partners = on_z + on_x + [on_core] + on_y + on_l
    barrier = pltpu.get_barrier_semaphore()
    for partner in partners:
        pl.semaphore_signal(barrier, inc=1, device_id=partner, device_id_type=MESH)

    loads = [
        pltpu.make_async_copy(src, dst, in_sem.at[i])
        for i, (src, dst) in enumerate(
            (
                (pk_hbm, shard_v.at[0]),
                (pv_hbm, shard_v.at[1]),
                (reward_hbm, reward_ref),
                (length_hbm, length_ref),
                (q_hbm, q_v),
                (ok_hbm, own_v.at[0]),
                (ov_hbm, own_v.at[1]),
                (up_hbm, up_v),
            )
        )
    ]
    for load in loads:
        load.start()

    loads[2].wait()
    loads[3].wait()
    reward = reward_ref[0, 0]
    length = length_ref[0, 0]
    stat[0, 0:8] = jnp.full((8, 128), reward, F32)
    stat[0, 8:16] = jnp.full((8, 128), length.astype(F32), F32)

    def start(copies):
        for copy in copies:
            copy.start()

    def arrive(copies):
        for copy in copies:
            copy.wait_recv()

    def drain(copies):
        for copy in copies:
            copy.wait_send()

    stages = [on_z, on_x, [on_core], on_y, on_l]
    in_group = 3

    def stat_copies(step):
        return [
            remote(
                stat.at[step],
                stat_in.at[step, d],
                t_s.at[step, d],
                t_r.at[step, d],
                to,
            )
            for d, to in enumerate(stages[step])
        ]

    def stat_next(step):
        if step < len(stages):
            arrive(stat_copies(step))
            total = stat[step]
            for d in range(len(stages[step])):
                total = total + stat_in[step, d]
            stat[step + 1] = total
            if step + 1 < len(stages):
                start(stat_copies(step + 1))

    pieces = (slice(0, 2), slice(2, 4))

    def gather_z():
        mine = kv.at[:, mc, mx, mz]
        return [
            remote(mine, mine, gz_s.at[d], gz_r.at[d], to) for d, to in enumerate(on_z)
        ]

    def gather_x(n):
        mine = kv.at[pieces[n], mc, mx]
        return [
            remote(mine, mine, gx_s.at[n, d], gx_r.at[n, d], to)
            for d, to in enumerate(on_x)
        ]

    def gather_c(n):
        mine = kv.at[pieces[n], mc]
        return [remote(mine, mine, gc_s.at[n], gc_r.at[n], on_core)]

    def x_to_c(n):
        arrive(gather_x(n))
        start(gather_c(n))

    chunks = (slice(0, 2), slice(2, 3), slice(3, 4))

    def reduce_c(n):
        return [
            remote(cs.at[chunks[n]], rc.at[chunks[n]], sc_s.at[n], sc_r.at[n], on_core)
        ]

    def reduce_x(n):
        return [
            remote(
                xs.at[chunks[n], ahead(mx, d + 1, nx)],
                rx.at[d, chunks[n]],
                sx_s.at[n, d],
                sx_r.at[n, d],
                to,
            )
            for d, to in enumerate(on_x)
        ]

    def reduce_z(n):
        return [
            remote(
                zs.at[chunks[n], ahead(mz, d + 1, nz)],
                rz.at[d, chunks[n]],
                sz_s.at[n, d],
                sz_r.at[n, d],
                to,
            )
            for d, to in enumerate(on_z)
        ]

    def before_c(n, advantage):
        cs[chunks[n]] = (acc[chunks[n], 1 - mc] * advantage).astype(BF16)
        start(reduce_c(n))

    def after_c(n, advantage):
        arrive(reduce_c(n))
        both = acc[chunks[n], mc] * advantage + rc[chunks[n]].astype(F32)
        part[chunks[n]] = both
        xs[chunks[n]] = both.astype(BF16)
        start(reduce_x(n))

    def after_x(n):
        arrive(reduce_x(n))
        both = part[chunks[n], mx]
        for d in range(nx - 1):
            both = both + rx[d, chunks[n]].astype(F32)
        part[chunks[n], 0] = both
        zs[chunks[n]] = both.astype(BF16)
        start(reduce_z(n))

    def after_z(n, scale):
        arrive(reduce_z(n))
        both = part[chunks[n], 0, mz]
        for d in range(nz - 1):
            both = both + rz[d, chunks[n]].astype(F32)
        for i, g in enumerate(range(chunks[n].start, chunks[n].stop)):
            gp_v[0, :, head_cols(g)] = both[i, 0] * scale
            gp_v[1, :, head_cols(g)] = both[i, 1] * scale

    def head_cols(g):
        return slice(g * HEAD, (g + 1) * HEAD)

    def query_cols(g, j):
        lower = (g * QUERY_PER_KV + j) * HEAD
        return slice(lower, lower + HEAD)

    def stacked(ref, g):
        return jnp.concatenate(
            [ref[:, query_cols(g, j)] for j in range(QUERY_PER_KV)], axis=0
        )

    def prompt_rows(g, i):
        return kv[g, :, :, :, i].reshape(prompt, HEAD)

    def own_part(g):
        key = lax.broadcasted_iota(jnp.int32, (TOKENS, rows), 0)
        step = lax.broadcasted_iota(jnp.int32, (TOKENS, rows), 1) & (TOKENS - 1)
        scores = dot(own_v[0, :, head_cols(g)], stacked(q_v, g), 1, 1)
        so_ref[g] = jnp.where(key <= step, scores, -1e30)
        step = lax.broadcasted_iota(jnp.int32, (TOKENS, HEAD), 0)
        live = jnp.where(step < length, 1.0, 0.0)
        for j in range(QUERY_PER_KV):
            cols = query_cols(g, j)
            up_v[:, cols] = (up_v[:, cols].astype(F32) * live).astype(BF16)
        dpo_ref[g] = dot(own_v[1, :, head_cols(g)], stacked(up_v, g), 1, 1)

    def forward(g):
        q_g, grad_out = stacked(q_v, g), stacked(up_v, g)
        s_ref[...] = dot(prompt_rows(g, 0), q_g, 1, 1)
        dp_ref[0:prompt] = dot(prompt_rows(g, 1), grad_out, 1, 1)
        dp_ref[prompt:] = dpo_ref[g]
        top = jnp.maximum(
            jnp.max(s_ref[...], axis=0, keepdims=True),
            jnp.max(so_ref[g], axis=0, keepdims=True),
        )
        e_ref[0:prompt] = jnp.exp((s_ref[...] - top) * SCALE)
        e_ref[prompt:] = jnp.exp((so_ref[g] - top) * SCALE)
        inverse = 1.0 / jnp.sum(e_ref[...], axis=0, keepdims=True)
        pb_ref[...] = (e_ref[...] * inverse).astype(BF16)
        inverse_ref[...] = inverse

    def backward(g):
        q_g, grad_out = stacked(q_v, g), stacked(up_v, g)
        inverse = inverse_ref[...]
        grad_values = dot(pb_ref[...], grad_out, 1, 0)
        acc[g, :, :, :, 1] = grad_values[0:prompt].reshape(2, nx, nz, 16, HEAD)
        own_grad[1, :, head_cols(g)] = grad_values[prompt:]
        delta = jnp.sum(pb_ref[...].astype(F32) * dp_ref[...], axis=0, keepdims=True)
        ds_ref[g] = ((e_ref[...] * inverse) * (dp_ref[...] - delta)).astype(BF16)
        grad_keys = SCALE * dot(ds_ref[g], q_g, 1, 0)
        acc[g, :, :, :, 0] = grad_keys[0:prompt].reshape(2, nx, nz, 16, HEAD)
        own_grad[0, :, head_cols(g)] = grad_keys[prompt:]

    def query_gradient(g, weight):
        turned = dot(prompt_rows(g, 0), ds_ref[g, 0:prompt], 0, 0) + dot(
            own_v[0, :, head_cols(g)], ds_ref[g, prompt:], 0, 0
        )
        for j in range(QUERY_PER_KV):
            block = turned[:, j * TOKENS : (j + 1) * TOKENS]
            gq_v[:, query_cols(g, j)] = (block.T * weight).astype(BF16)

    loads[0].wait()
    loads[1].wait()
    for g in range(KEY_HEADS):
        kv[g, mc, mx, mz, 0] = shard_v[0, :, head_cols(g)]
        kv[g, mc, mx, mz, 1] = shard_v[1, :, head_cols(g)]
    pl.semaphore_wait(barrier, len(partners))
    start(gather_z())
    start(stat_copies(0))
    for load in loads[4:]:
        load.wait()
    own_part(0)
    own_part(1)
    arrive(gather_z())
    start(gather_x(0))
    start(gather_x(1))
    stat_next(0)
    own_part(2)
    x_to_c(0)
    own_part(3)
    stat_next(1)
    arrive(gather_c(0))
    forward(0)
    x_to_c(1)
    backward(0)
    stat_next(2)
    forward(1)
    backward(1)
    advantage = (reward - stat[in_group, 0:1] / (nz * nx * 2)).reshape(1, 1, 1, 1, 1, 128)
    before_c(0, advantage)
    arrive(gather_c(1))
    forward(2)
    stat_next(3)
    after_c(0, advantage)
    backward(2)
    before_c(1, advantage)
    forward(3)
    stat_next(4)
    after_c(1, advantage)
    after_x(0)
    backward(3)
    before_c(2, advantage)
    unit = 1.0 / stat[len(stages), 8:9]
    weight = (reward - stat[in_group, 0:1] / (nz * nx * 2)) * unit
    query_gradient(0, weight * SCALE)
    after_c(2, advantage)
    after_x(1)
    query_gradient(1, weight * SCALE)
    query_gradient(2, weight * SCALE)
    after_x(2)
    query_gradient(3, weight * SCALE)
    for g in range(KEY_HEADS):
        for i in range(2):
            go_v[i, :, head_cols(g)] = (own_grad[i, :, head_cols(g)] * weight).astype(BF16)
    stores = [
        pltpu.make_async_copy(src, dst, out_sem.at[i])
        for i, (src, dst) in enumerate(
            (
                (gq_v, gq_hbm),
                (go_v.at[0], gok_hbm),
                (go_v.at[1], gov_hbm),
                (gp_v.at[0], gpk_hbm),
                (gp_v.at[1], gpv_hbm),
            )
        )
    ]
    start(stores[0:3])
    for step in range(len(stages)):
        drain(stat_copies(step))
    drain(gather_z())
    for n in range(len(pieces)):
        drain(gather_x(n))
        drain(gather_c(n))
    after_z(0, unit)
    after_z(1, unit)
    for n in range(len(chunks)):
        drain(reduce_c(n))
        drain(reduce_x(n))
        if n + 1 < len(chunks):
            drain(reduce_z(n))
    after_z(2, unit)
    start(stores[3:5])
    drain(reduce_z(len(chunks) - 1))
    for store in stores:
        store.wait()


def store_kernel(*refs):
    sources, targets, holds = refs[0:5], refs[5:10], refs[10:15]
    in_sem, out_sem = refs[15:17]
    ins = [
        pltpu.make_async_copy(sources[i], holds[i], in_sem.at[i]) for i in range(5)
    ]
    outs = [
        pltpu.make_async_copy(holds[i], targets[i], out_sem.at[i]) for i in range(5)
    ]
    for copy in ins:
        copy.start()
    for i in (1, 2, 3, 4, 0):
        ins[i].wait()
        outs[i].start()
    for copy in outs:
        copy.wait()


def on_device(
    dims,
    queries,
    response_keys,
    response_values,
    prompt_key_rows,
    prompt_value_rows,
    upstream,
    rewards,
    lengths,
):
    nl, ny, nz, nx = dims
    kvh, rows = KEY_HEADS, QUERY_PER_KV * TOKENS
    prompt = nz * nx * 2 * 16
    joined = prompt + TOKENS
    wide, narrow = queries.shape[3], response_keys.shape[3]
    shard = prompt_key_rows.shape[1]
    vmem, sem = pltpu.VMEM, pltpu.SemaphoreType.DMA
    anywhere = pl.BlockSpec(memory_space=pl.ANY)
    shapes = (
        jax.ShapeDtypeStruct((TOKENS, wide), BF16),
        jax.ShapeDtypeStruct((TOKENS, narrow), BF16),
        jax.ShapeDtypeStruct((TOKENS, narrow), BF16),
        jax.ShapeDtypeStruct((shard, narrow), F32),
        jax.ShapeDtypeStruct((shard, narrow), F32),
    )
    results = pl.pallas_call(
        functools.partial(kernel, dims),
        out_shape=shapes,
        in_specs=[anywhere] * 8,
        out_specs=[anywhere] * 5,
        scratch_shapes=[
            vmem((TOKENS, wide), BF16),
            vmem((2, TOKENS, narrow), BF16),
            vmem((2, shard, narrow), F32),
            vmem((TOKENS, wide), BF16),
            vmem((TOKENS, wide), BF16),
            vmem((2, TOKENS, narrow), BF16),
            vmem((2, shard, narrow), BF16),
            vmem((kvh, 2, nx, nz, 2, 16, HEAD), BF16),
            vmem((10, 16, 128), F32),
            vmem((5, 3, 16, 128), F32),
            vmem((2, TOKENS, narrow), F32),
            vmem((1, rows), F32),
            pltpu.SMEM((1, 1), F32),
            pltpu.SMEM((1, 1), jnp.int32),
            vmem((kvh, TOKENS, rows), F32),
            vmem((kvh, TOKENS, rows), F32),
            vmem((prompt, rows), F32),
            vmem((joined, rows), F32),
            vmem((joined, rows), F32),
            vmem((joined, rows), BF16),
            vmem((kvh, joined, rows), BF16),
            vmem((kvh, 2, nx, nz, 2, 16, HEAD), F32),
            vmem((kvh, nx, nz, 2, 16, HEAD), BF16),
            vmem((kvh, nx, nz, 2, 16, HEAD), BF16),
            vmem((kvh, nx, nz, 2, 16, HEAD), F32),
            vmem((kvh, nx, nz, 2, 16, HEAD), BF16),
            vmem((nx - 1, kvh, nz, 2, 16, HEAD), BF16),
            vmem((kvh, nz, 2, 16, HEAD), BF16),
            vmem((nz - 1, kvh, 2, 16, HEAD), BF16),
            sem((8,)),
            sem((5,)),
            sem((nz - 1,)),
            sem((nz - 1,)),
            sem((2, nx - 1)),
            sem((2, nx - 1)),
            sem((2,)),
            sem((2,)),
            sem((3,)),
            sem((3,)),
            sem((3, nx - 1)),
            sem((3, nx - 1)),
            sem((3, nz - 1)),
            sem((3, nz - 1)),
            sem((5, 3)),
            sem((5, 3)),
        ],
        compiler_params=pltpu.CompilerParams(
            collective_id=0,
            has_side_effects=True,
            vmem_limit_bytes=VMEM_LIMIT,
        ),
        cost_estimate=pl.CostEstimate(
            flops=1_400_000_000, bytes_accessed=3_000_000, transcendentals=1_400_000
        ),
    )(
        queries[0, 0],
        response_keys[0, 0],
        response_values[0, 0],
        prompt_key_rows[0],
        prompt_value_rows[0],
        upstream[0, 0],
        rewards,
        lengths,
    )
    gq, gok, gov, gpk, gpv = pl.pallas_call(
        store_kernel,
        out_shape=shapes,
        in_specs=[anywhere] * 5,
        out_specs=[anywhere] * 5,
        scratch_shapes=[vmem(x.shape, x.dtype) for x in shapes] + [sem((5,)), sem((5,))],
        compiler_params=pltpu.CompilerParams(vmem_limit_bytes=VMEM_LIMIT),
    )(*results)
    return gq[None, None], gok[None, None], gov[None, None], gpk[None], gpv[None]


def solution(mesh, dims=(4, 4, 4, 4)):
    four = P("group", "resp", None, None)
    three = P("group", "resp", None)
    two = P("group", "resp")
    return jax.shard_map(
        functools.partial(on_device, dims),
        mesh=mesh,
        in_specs=(four, four, four, three, three, four, two, two),
        out_specs=(four, four, four, three, three),
        check_vma=False,
    )
```

```python
import functools

import jax
import jax.numpy as jnp
from jax import lax
from jax.experimental import pallas as pl
from jax.experimental.pallas import tpu as pltpu
from jax.sharding import PartitionSpec as P

MESH = pl.DeviceIdType.MESH
KEY_HEADS = 4
QUERY_PER_KV = 4
HEAD = 128
TOKENS = 128
SCALE = HEAD ** (-0.5)
F32 = jnp.float32
BF16 = jnp.bfloat16
VMEM_LIMIT = 56 * 1024 * 1024


def dot(a, b, a_dim, b_dim):
    return lax.dot_general(
        a, b, (((a_dim,), (b_dim,)), ((), ())), preferred_element_type=F32
    )


def kernel(
    dims,
    q_hbm,
    ok_hbm,
    ov_hbm,
    pk_hbm,
    pv_hbm,
    up_hbm,
    reward_ref,
    length_ref,
    gq_hbm,
    gok_hbm,
    gov_hbm,
    gpk_hbm,
    gpv_hbm,
    gq_v,
    go_v,
    gp_v,
    q_v,
    up_v,
    own_v,
    shard_v,
    kv,
    stat,
    stat_in,
    own_grad,
    inverse_ref,
    so_ref,
    dpo_ref,
    s_ref,
    e_ref,
    dp_ref,
    pb_ref,
    ds_ref,
    acc,
    cs,
    rc,
    part,
    xs,
    rx,
    zs,
    rz,
    in_sem,
    out_sem,
    gz_s,
    gz_r,
    gx_s,
    gx_r,
    gc_s,
    gc_r,
    sc_s,
    sc_r,
    sx_s,
    sx_r,
    sz_s,
    sz_r,
    t_s,
    t_r,
):
    nl, ny, nz, nx = dims
    prompt = nz * nx * 2 * 16
    rows = QUERY_PER_KV * TOKENS
    gi, ri = lax.axis_index("group"), lax.axis_index("resp")
    mc = lax.rem(ri, 2)
    mx = lax.rem(lax.div(ri, 2), nx)
    mz = lax.div(ri, 2 * nx)
    my = lax.rem(gi, ny)
    ml = lax.div(gi, ny)

    def device(c=mc, x=mx, z=mz, y=my, l=ml):
        return (l * ny + y, (z * nx + x) * 2 + c)

    def ahead(me, d, n):
        return lax.rem(me + d, n)

    def remote(src, dst, send, recv, to):
        return pltpu.make_async_remote_copy(
            src_ref=src,
            dst_ref=dst,
            send_sem=send,
            recv_sem=recv,
            device_id=to,
            device_id_type=MESH,
        )

    on_core = device(c=1 - mc)
    on_y = [device(y=ahead(my, d, ny)) for d in range(1, ny)]
    on_l = [device(l=ahead(ml, d, nl)) for d in range(1, nl)]
    on_x = [device(x=ahead(mx, d, nx)) for d in range(1, nx)]
    on_z = [device(z=ahead(mz, d, nz)) for d in range(1, nz)]
    partners = on_z + on_x + [on_core] + on_y + on_l
    barrier = pltpu.get_barrier_semaphore()
    for partner in partners:
        pl.semaphore_signal(barrier, inc=1, device_id=partner, device_id_type=MESH)

    loads = [
        pltpu.make_async_copy(src, dst, in_sem.at[i])
        for i, (src, dst) in enumerate(
            (
                (pk_hbm, shard_v.at[0]),
                (pv_hbm, shard_v.at[1]),
                (q_hbm, q_v),
                (ok_hbm, own_v.at[0]),
                (ov_hbm, own_v.at[1]),
                (up_hbm, up_v),
            )
        )
    ]
    for load in loads:
        load.start()

    reward = reward_ref[0, 0]
    length = length_ref[0, 0]
    stat[0, 0:8] = jnp.full((8, 128), reward, F32)
    stat[0, 8:16] = jnp.full((8, 128), length.astype(F32), F32)

    def start(copies):
        for copy in copies:
            copy.start()

    def arrive(copies):
        for copy in copies:
            copy.wait_recv()

    def drain(copies):
        for copy in copies:
            copy.wait_send()

    stages = [on_z, on_x, [on_core], on_y, on_l]
    in_group = 3

    def stat_copies(step):
        return [
            remote(
                stat.at[step],
                stat_in.at[step, d],
                t_s.at[step, d],
                t_r.at[step, d],
                to,
            )
            for d, to in enumerate(stages[step])
        ]

    def stat_next(step):
        if step < len(stages):
            arrive(stat_copies(step))
            total = stat[step]
            for d in range(len(stages[step])):
                total = total + stat_in[step, d]
            stat[step + 1] = total
            if step + 1 < len(stages):
                start(stat_copies(step + 1))

    pieces = (slice(0, 2), slice(2, 4))

    def gather_z():
        mine = kv.at[:, mc, mx, mz]
        return [
            remote(mine, mine, gz_s.at[d], gz_r.at[d], to) for d, to in enumerate(on_z)
        ]

    def gather_x(n):
        mine = kv.at[pieces[n], mc, mx]
        return [
            remote(mine, mine, gx_s.at[n, d], gx_r.at[n, d], to)
            for d, to in enumerate(on_x)
        ]

    def gather_c(n):
        mine = kv.at[pieces[n], mc]
        return [remote(mine, mine, gc_s.at[n], gc_r.at[n], on_core)]

    def x_to_c(n):
        arrive(gather_x(n))
        start(gather_c(n))

    chunks = (slice(0, 2), slice(2, 3), slice(3, 4))

    def reduce_c(n):
        return [
            remote(cs.at[chunks[n]], rc.at[chunks[n]], sc_s.at[n], sc_r.at[n], on_core)
        ]

    def reduce_x(n):
        return [
            remote(
                xs.at[chunks[n], ahead(mx, d + 1, nx)],
                rx.at[d, chunks[n]],
                sx_s.at[n, d],
                sx_r.at[n, d],
                to,
            )
            for d, to in enumerate(on_x)
        ]

    def reduce_z(n):
        return [
            remote(
                zs.at[chunks[n], ahead(mz, d + 1, nz)],
                rz.at[d, chunks[n]],
                sz_s.at[n, d],
                sz_r.at[n, d],
                to,
            )
            for d, to in enumerate(on_z)
        ]

    def before_c(n, advantage):
        cs[chunks[n]] = (acc[chunks[n], 1 - mc] * advantage).astype(BF16)
        start(reduce_c(n))

    def after_c(n, advantage):
        arrive(reduce_c(n))
        both = acc[chunks[n], mc] * advantage + rc[chunks[n]].astype(F32)
        part[chunks[n]] = both
        xs[chunks[n]] = both.astype(BF16)
        start(reduce_x(n))

    def after_x(n):
        arrive(reduce_x(n))
        both = part[chunks[n], mx]
        for d in range(nx - 1):
            both = both + rx[d, chunks[n]].astype(F32)
        part[chunks[n], 0] = both
        zs[chunks[n]] = both.astype(BF16)
        start(reduce_z(n))

    def after_z(n, scale):
        arrive(reduce_z(n))
        both = part[chunks[n], 0, mz]
        for d in range(nz - 1):
            both = both + rz[d, chunks[n]].astype(F32)
        for i, g in enumerate(range(chunks[n].start, chunks[n].stop)):
            gp_v[0, :, head_cols(g)] = both[i, 0] * scale
            gp_v[1, :, head_cols(g)] = both[i, 1] * scale

    def head_cols(g):
        return slice(g * HEAD, (g + 1) * HEAD)

    def query_cols(g, j):
        lower = (g * QUERY_PER_KV + j) * HEAD
        return slice(lower, lower + HEAD)

    def stacked(ref, g):
        return jnp.concatenate(
            [ref[:, query_cols(g, j)] for j in range(QUERY_PER_KV)], axis=0
        )

    def prompt_rows(g, i):
        return kv[g, :, :, :, i].reshape(prompt, HEAD)

    def own_part(g):
        key = lax.broadcasted_iota(jnp.int32, (TOKENS, rows), 0)
        step = lax.broadcasted_iota(jnp.int32, (TOKENS, rows), 1) & (TOKENS - 1)
        scores = dot(own_v[0, :, head_cols(g)], stacked(q_v, g), 1, 1)
        so_ref[g] = jnp.where(key <= step, scores, -1e30)
        step = lax.broadcasted_iota(jnp.int32, (TOKENS, HEAD), 0)
        live = jnp.where(step < length, 1.0, 0.0)
        for j in range(QUERY_PER_KV):
            cols = query_cols(g, j)
            up_v[:, cols] = (up_v[:, cols].astype(F32) * live).astype(BF16)
        dpo_ref[g] = dot(own_v[1, :, head_cols(g)], stacked(up_v, g), 1, 1)

    def forward(g):
        q_g, grad_out = stacked(q_v, g), stacked(up_v, g)
        s_ref[...] = dot(prompt_rows(g, 0), q_g, 1, 1)
        dp_ref[0:prompt] = dot(prompt_rows(g, 1), grad_out, 1, 1)
        dp_ref[prompt:] = dpo_ref[g]
        top = jnp.maximum(
            jnp.max(s_ref[...], axis=0, keepdims=True),
            jnp.max(so_ref[g], axis=0, keepdims=True),
        )
        e_ref[0:prompt] = jnp.exp((s_ref[...] - top) * SCALE)
        e_ref[prompt:] = jnp.exp((so_ref[g] - top) * SCALE)
        inverse = 1.0 / jnp.sum(e_ref[...], axis=0, keepdims=True)
        pb_ref[...] = (e_ref[...] * inverse).astype(BF16)
        inverse_ref[...] = inverse

    def backward(g):
        q_g, grad_out = stacked(q_v, g), stacked(up_v, g)
        inverse = inverse_ref[...]
        grad_values = dot(pb_ref[...], grad_out, 1, 0)
        acc[g, :, :, :, 1] = grad_values[0:prompt].reshape(2, nx, nz, 16, HEAD)
        own_grad[1, :, head_cols(g)] = grad_values[prompt:]
        delta = jnp.sum(pb_ref[...].astype(F32) * dp_ref[...], axis=0, keepdims=True)
        ds_ref[g] = ((e_ref[...] * inverse) * (dp_ref[...] - delta)).astype(BF16)
        grad_keys = SCALE * dot(ds_ref[g], q_g, 1, 0)
        acc[g, :, :, :, 0] = grad_keys[0:prompt].reshape(2, nx, nz, 16, HEAD)
        own_grad[0, :, head_cols(g)] = grad_keys[prompt:]

    def query_gradient(g, weight):
        turned = dot(prompt_rows(g, 0), ds_ref[g, 0:prompt], 0, 0) + dot(
            own_v[0, :, head_cols(g)], ds_ref[g, prompt:], 0, 0
        )
        for j in range(QUERY_PER_KV):
            block = turned[:, j * TOKENS : (j + 1) * TOKENS]
            gq_v[:, query_cols(g, j)] = (block.T * weight).astype(BF16)

    loads[0].wait()
    loads[1].wait()
    for g in range(KEY_HEADS):
        kv[g, mc, mx, mz, 0] = shard_v[0, :, head_cols(g)]
        kv[g, mc, mx, mz, 1] = shard_v[1, :, head_cols(g)]
    pl.semaphore_wait(barrier, len(partners))
    start(gather_z())
    start(stat_copies(0))
    for load in loads[2:]:
        load.wait()
    own_part(0)
    own_part(1)
    arrive(gather_z())
    start(gather_x(0))
    start(gather_x(1))
    stat_next(0)
    own_part(2)
    x_to_c(0)
    own_part(3)
    stat_next(1)
    arrive(gather_c(0))
    forward(0)
    x_to_c(1)
    backward(0)
    stat_next(2)
    forward(1)
    backward(1)
    advantage = (reward - stat[in_group, 0:1] / (nz * nx * 2)).reshape(1, 1, 1, 1, 1, 128)
    before_c(0, advantage)
    arrive(gather_c(1))
    forward(2)
    stat_next(3)
    after_c(0, advantage)
    backward(2)
    before_c(1, advantage)
    forward(3)
    stat_next(4)
    after_c(1, advantage)
    backward(3)
    before_c(2, advantage)
    after_x(0)
    unit = 1.0 / stat[len(stages), 8:9]
    weight = (reward - stat[in_group, 0:1] / (nz * nx * 2)) * unit
    query_gradient(0, weight * SCALE)
    after_c(2, advantage)
    after_x(1)
    query_gradient(1, weight * SCALE)
    query_gradient(2, weight * SCALE)
    after_x(2)
    query_gradient(3, weight * SCALE)
    for g in range(KEY_HEADS):
        for i in range(2):
            go_v[i, :, head_cols(g)] = (own_grad[i, :, head_cols(g)] * weight).astype(BF16)
    stores = [
        pltpu.make_async_copy(src, dst, out_sem.at[i])
        for i, (src, dst) in enumerate(
            (
                (gq_v, gq_hbm),
                (go_v.at[0], gok_hbm),
                (go_v.at[1], gov_hbm),
                (gp_v.at[0], gpk_hbm),
                (gp_v.at[1], gpv_hbm),
            )
        )
    ]
    start(stores[0:3])
    for step in range(len(stages)):
        drain(stat_copies(step))
    drain(gather_z())
    for n in range(len(pieces)):
        drain(gather_x(n))
        drain(gather_c(n))
    after_z(0, unit)
    after_z(1, unit)
    for n in range(len(chunks)):
        drain(reduce_c(n))
        drain(reduce_x(n))
        if n + 1 < len(chunks):
            drain(reduce_z(n))
    after_z(2, unit)
    start(stores[3:5])
    drain(reduce_z(len(chunks) - 1))
    for store in stores:
        store.wait()


def store_kernel(*refs):
    sources, targets, holds = refs[0:5], refs[5:10], refs[10:15]
    in_sem, out_sem = refs[15:17]
    ins = [
        pltpu.make_async_copy(sources[i], holds[i], in_sem.at[i]) for i in range(5)
    ]
    outs = [
        pltpu.make_async_copy(holds[i], targets[i], out_sem.at[i]) for i in range(5)
    ]
    for copy in ins:
        copy.start()
    for i in (1, 2, 3, 4, 0):
        ins[i].wait()
        outs[i].start()
    for copy in outs:
        copy.wait()


def on_device(
    dims,
    queries,
    response_keys,
    response_values,
    prompt_key_rows,
    prompt_value_rows,
    upstream,
    rewards,
    lengths,
):
    nl, ny, nz, nx = dims
    kvh, rows = KEY_HEADS, QUERY_PER_KV * TOKENS
    prompt = nz * nx * 2 * 16
    joined = prompt + TOKENS
    wide, narrow = queries.shape[3], response_keys.shape[3]
    shard = prompt_key_rows.shape[1]
    vmem, sem = pltpu.VMEM, pltpu.SemaphoreType.DMA
    anywhere = pl.BlockSpec(memory_space=pl.ANY)
    scalar = pl.BlockSpec(memory_space=pltpu.SMEM)
    shapes = (
        jax.ShapeDtypeStruct((TOKENS, wide), BF16),
        jax.ShapeDtypeStruct((TOKENS, narrow), BF16),
        jax.ShapeDtypeStruct((TOKENS, narrow), BF16),
        jax.ShapeDtypeStruct((shard, narrow), F32),
        jax.ShapeDtypeStruct((shard, narrow), F32),
    )
    results = pl.pallas_call(
        functools.partial(kernel, dims),
        out_shape=shapes,
        in_specs=[anywhere] * 6 + [scalar] * 2,
        out_specs=[anywhere] * 5,
        scratch_shapes=[
            vmem((TOKENS, wide), BF16),
            vmem((2, TOKENS, narrow), BF16),
            vmem((2, shard, narrow), F32),
            vmem((TOKENS, wide), BF16),
            vmem((TOKENS, wide), BF16),
            vmem((2, TOKENS, narrow), BF16),
            vmem((2, shard, narrow), BF16),
            vmem((kvh, 2, nx, nz, 2, 16, HEAD), BF16),
            vmem((10, 16, 128), F32),
            vmem((5, 3, 16, 128), F32),
            vmem((2, TOKENS, narrow), F32),
            vmem((1, rows), F32),
            vmem((kvh, TOKENS, rows), F32),
            vmem((kvh, TOKENS, rows), F32),
            vmem((prompt, rows), F32),
            vmem((joined, rows), F32),
            vmem((joined, rows), F32),
            vmem((joined, rows), BF16),
            vmem((kvh, joined, rows), BF16),
            vmem((kvh, 2, nx, nz, 2, 16, HEAD), F32),
            vmem((kvh, nx, nz, 2, 16, HEAD), BF16),
            vmem((kvh, nx, nz, 2, 16, HEAD), BF16),
            vmem((kvh, nx, nz, 2, 16, HEAD), F32),
            vmem((kvh, nx, nz, 2, 16, HEAD), BF16),
            vmem((nx - 1, kvh, nz, 2, 16, HEAD), BF16),
            vmem((kvh, nz, 2, 16, HEAD), BF16),
            vmem((nz - 1, kvh, 2, 16, HEAD), BF16),
            sem((6,)),
            sem((5,)),
            sem((nz - 1,)),
            sem((nz - 1,)),
            sem((2, nx - 1)),
            sem((2, nx - 1)),
            sem((2,)),
            sem((2,)),
            sem((3,)),
            sem((3,)),
            sem((3, nx - 1)),
            sem((3, nx - 1)),
            sem((3, nz - 1)),
            sem((3, nz - 1)),
            sem((5, 3)),
            sem((5, 3)),
        ],
        compiler_params=pltpu.CompilerParams(
            collective_id=0,
            has_side_effects=True,
            vmem_limit_bytes=VMEM_LIMIT,
        ),
        cost_estimate=pl.CostEstimate(
            flops=1_400_000_000, bytes_accessed=3_000_000, transcendentals=1_400_000
        ),
    )(
        queries[0, 0],
        response_keys[0, 0],
        response_values[0, 0],
        prompt_key_rows[0],
        prompt_value_rows[0],
        upstream[0, 0],
        rewards,
        lengths,
    )
    gq, gok, gov, gpk, gpv = pl.pallas_call(
        store_kernel,
        out_shape=shapes,
        in_specs=[anywhere] * 5,
        out_specs=[anywhere] * 5,
        scratch_shapes=[vmem(x.shape, x.dtype) for x in shapes] + [sem((5,)), sem((5,))],
        compiler_params=pltpu.CompilerParams(vmem_limit_bytes=VMEM_LIMIT),
    )(*results)
    return gq[None, None], gok[None, None], gov[None, None], gpk[None], gpv[None]


def solution(mesh, dims=(4, 4, 4, 4)):
    four = P("group", "resp", None, None)
    three = P("group", "resp", None)
    two = P("group", "resp")
    return jax.shard_map(
        functools.partial(on_device, dims),
        mesh=mesh,
        in_specs=(four, four, four, three, three, four, two, two),
        out_specs=(four, four, four, three, three),
        check_vma=False,
    )
```

```python
import functools

import jax
import jax.numpy as jnp
from jax import lax
from jax.experimental import pallas as pl
from jax.experimental.pallas import tpu as pltpu
from jax.sharding import PartitionSpec as P

MESH = pl.DeviceIdType.MESH
KEY_HEADS = 4
QUERY_PER_KV = 4
HEAD = 128
TOKENS = 128
SCALE = HEAD ** (-0.5)
F32 = jnp.float32
BF16 = jnp.bfloat16
VMEM_LIMIT = 56 * 1024 * 1024


def dot(a, b, a_dim, b_dim):
    return lax.dot_general(
        a, b, (((a_dim,), (b_dim,)), ((), ())), preferred_element_type=F32
    )


def kernel(
    dims,
    q_hbm,
    ok_hbm,
    ov_hbm,
    pk_hbm,
    pv_hbm,
    up_hbm,
    reward_ref,
    length_ref,
    gq_hbm,
    gok_hbm,
    gov_hbm,
    gpk_hbm,
    gpv_hbm,
    gq_v,
    go_v,
    gp_v,
    q_v,
    up_v,
    own_v,
    shard_v,
    kv,
    stat,
    stat_in,
    own_grad,
    s_ref,
    e_ref,
    dp_ref,
    pb_ref,
    ds_ref,
    acc,
    cs,
    rc,
    part,
    xs,
    rx,
    zs,
    rz,
    in_sem,
    out_sem,
    gz_s,
    gz_r,
    gx_s,
    gx_r,
    gc_s,
    gc_r,
    sc_s,
    sc_r,
    sx_s,
    sx_r,
    sz_s,
    sz_r,
    t_s,
    t_r,
):
    nl, ny, nz, nx = dims
    prompt = nz * nx * 2 * 16
    rows = QUERY_PER_KV * TOKENS
    gi, ri = lax.axis_index("group"), lax.axis_index("resp")
    mc = lax.rem(ri, 2)
    mx = lax.rem(lax.div(ri, 2), nx)
    mz = lax.div(ri, 2 * nx)
    my = lax.rem(gi, ny)
    ml = lax.div(gi, ny)

    def device(c=mc, x=mx, z=mz, y=my, l=ml):
        return (l * ny + y, (z * nx + x) * 2 + c)

    def ahead(me, d, n):
        return lax.rem(me + d, n)

    def remote(src, dst, send, recv, to):
        return pltpu.make_async_remote_copy(
            src_ref=src,
            dst_ref=dst,
            send_sem=send,
            recv_sem=recv,
            device_id=to,
            device_id_type=MESH,
        )

    on_core = device(c=1 - mc)
    on_x = [device(x=ahead(mx, d, nx)) for d in range(1, nx)]
    on_z = [device(z=ahead(mz, d, nz)) for d in range(1, nz)]
    on_y = [device(y=ahead(my, d, ny)) for d in range(1, ny)]
    on_l = [device(l=ahead(ml, d, nl)) for d in range(1, nl)]
    partners = [on_core] + on_x + on_z + on_y + on_l
    barrier = pltpu.get_barrier_semaphore()
    for partner in partners:
        pl.semaphore_signal(barrier, inc=1, device_id=partner, device_id_type=MESH)

    loads = [
        pltpu.make_async_copy(src, dst, in_sem.at[i])
        for i, (src, dst) in enumerate(
            (
                (pk_hbm, shard_v.at[0]),
                (pv_hbm, shard_v.at[1]),
                (q_hbm, q_v),
                (ok_hbm, own_v.at[0]),
                (ov_hbm, own_v.at[1]),
                (up_hbm, up_v),
            )
        )
    ]
    for load in loads:
        load.start()

    reward = reward_ref[0, 0]
    length = length_ref[0, 0]
    stat[0, 0:8] = jnp.full((8, 128), reward, F32)
    stat[0, 8:16] = jnp.full((8, 128), length.astype(F32), F32)

    def start(copies):
        for copy in copies:
            copy.start()

    def arrive(copies):
        for copy in copies:
            copy.wait_recv()

    def drain(copies):
        for copy in copies:
            copy.wait_send()

    stages = (on_z, on_x, [on_core], on_y, on_l)

    def stat_copies(step):
        return [
            remote(
                stat.at[step],
                stat_in.at[step, d],
                t_s.at[step, d],
                t_r.at[step, d],
                to,
            )
            for d, to in enumerate(stages[step])
        ]

    def stat_sum(step):
        arrive(stat_copies(step))
        total = stat[step]
        for d in range(len(stages[step])):
            total = total + stat_in[step, d]
        stat[step + 1] = total

    def gather_z():
        mine = kv.at[:, mc, mx, mz]
        return [
            remote(mine, mine, gz_s.at[d], gz_r.at[d], to) for d, to in enumerate(on_z)
        ]

    def gather_x(half):
        mine = kv.at[2 * half : 2 * half + 2, mc, mx]
        return [
            remote(mine, mine, gx_s.at[half, d], gx_r.at[half, d], to)
            for d, to in enumerate(on_x)
        ]

    def gather_c(half):
        mine = kv.at[2 * half : 2 * half + 2, mc]
        return [remote(mine, mine, gc_s.at[half], gc_r.at[half], on_core)]

    chunks = (slice(0, 2), slice(2, 3), slice(3, 4))

    def reduce_c(n):
        return [
            remote(cs.at[chunks[n]], rc.at[chunks[n]], sc_s.at[n], sc_r.at[n], on_core)
        ]

    def reduce_x(n):
        return [
            remote(
                xs.at[chunks[n], ahead(mx, d + 1, nx)],
                rx.at[d, chunks[n]],
                sx_s.at[n, d],
                sx_r.at[n, d],
                to,
            )
            for d, to in enumerate(on_x)
        ]

    def reduce_z(n):
        return [
            remote(
                zs.at[chunks[n], ahead(mz, d + 1, nz)],
                rz.at[d, chunks[n]],
                sz_s.at[n, d],
                sz_r.at[n, d],
                to,
            )
            for d, to in enumerate(on_z)
        ]

    def before_c(n):
        cs[chunks[n]] = acc[chunks[n], 1 - mc].astype(BF16)
        start(reduce_c(n))

    def after_c(n):
        arrive(reduce_c(n))
        both = acc[chunks[n], mc] + rc[chunks[n]].astype(F32)
        part[chunks[n]] = both
        xs[chunks[n]] = both.astype(BF16)
        start(reduce_x(n))

    def after_x(n):
        arrive(reduce_x(n))
        both = part[chunks[n], mx]
        for d in range(nx - 1):
            both = both + rx[d, chunks[n]].astype(F32)
        part[chunks[n], 0] = both
        zs[chunks[n]] = both.astype(BF16)
        start(reduce_z(n))

    def after_z(n, scale):
        arrive(reduce_z(n))
        both = part[chunks[n], 0, mz]
        for d in range(nz - 1):
            both = both + rz[d, chunks[n]].astype(F32)
        for i, g in enumerate(range(chunks[n].start, chunks[n].stop)):
            gp_v[0, :, head_cols(g)] = both[i, 0] * scale
            gp_v[1, :, head_cols(g)] = both[i, 1] * scale

    def head_cols(g):
        return slice(g * HEAD, (g + 1) * HEAD)

    def query_cols(g, j):
        lower = (g * QUERY_PER_KV + j) * HEAD
        return slice(lower, lower + HEAD)

    def stacked(ref, g):
        return jnp.concatenate(
            [ref[:, query_cols(g, j)] for j in range(QUERY_PER_KV)], axis=0
        )

    def prompt_rows(g, i):
        return kv[g, :, :, :, i].reshape(prompt, HEAD)

    def own_part(g):
        key = lax.broadcasted_iota(jnp.int32, (TOKENS, rows), 0)
        step = lax.broadcasted_iota(jnp.int32, (TOKENS, rows), 1) & (TOKENS - 1)
        scores = dot(own_v[0, :, head_cols(g)], stacked(q_v, g), 1, 1)
        s_ref[g, prompt:] = jnp.where(key <= step, scores, -1e30)
        step = lax.broadcasted_iota(jnp.int32, (TOKENS, HEAD), 0)
        live = jnp.where(step < length, 1.0, 0.0)
        for j in range(QUERY_PER_KV):
            cols = query_cols(g, j)
            up_v[:, cols] = (up_v[:, cols].astype(F32) * live).astype(BF16)
        dp_ref[g, prompt:] = dot(own_v[1, :, head_cols(g)], stacked(up_v, g), 1, 1)

    def attend(g, advantage):
        q_g, grad_out = stacked(q_v, g), stacked(up_v, g)
        s_ref[g, 0:prompt] = dot(prompt_rows(g, 0), q_g, 1, 1)
        dp_ref[g, 0:prompt] = dot(prompt_rows(g, 1), grad_out, 1, 1)
        top = jnp.max(s_ref[g], axis=0, keepdims=True)
        e_ref[g] = jnp.exp((s_ref[g] - top) * SCALE)
        inverse = 1.0 / jnp.sum(e_ref[g], axis=0, keepdims=True)
        pb_ref[g] = (e_ref[g] * inverse).astype(BF16)
        grad_values = advantage * dot(pb_ref[g], grad_out, 1, 0)
        acc[g, :, :, :, 1] = grad_values[0:prompt].reshape(2, nx, nz, 16, HEAD)
        own_grad[1, :, head_cols(g)] = grad_values[prompt:]
        delta = jnp.sum(pb_ref[g].astype(F32) * dp_ref[g], axis=0, keepdims=True)
        ds_ref[g] = ((e_ref[g] * inverse) * (dp_ref[g] - delta)).astype(BF16)
        grad_keys = (advantage * SCALE) * dot(ds_ref[g], q_g, 1, 0)
        acc[g, :, :, :, 0] = grad_keys[0:prompt].reshape(2, nx, nz, 16, HEAD)
        own_grad[0, :, head_cols(g)] = grad_keys[prompt:]

    def query_gradient(g, weight):
        turned = dot(prompt_rows(g, 0), ds_ref[g, 0:prompt], 0, 0) + dot(
            own_v[0, :, head_cols(g)], ds_ref[g, prompt:], 0, 0
        )
        for j in range(QUERY_PER_KV):
            block = turned[:, j * TOKENS : (j + 1) * TOKENS]
            gq_v[:, query_cols(g, j)] = (block.T * weight).astype(BF16)

    loads[0].wait()
    loads[1].wait()
    for g in range(KEY_HEADS):
        kv[g, mc, mx, mz, 0] = shard_v[0, :, head_cols(g)]
        kv[g, mc, mx, mz, 1] = shard_v[1, :, head_cols(g)]
    pl.semaphore_wait(barrier, len(partners))
    start(gather_z())
    start(stat_copies(0))
    for load in loads[2:]:
        load.wait()
    own_part(0)
    own_part(1)
    arrive(gather_z())
    start(gather_x(0))
    start(gather_x(1))
    stat_sum(0)
    start(stat_copies(1))
    own_part(2)
    own_part(3)
    arrive(gather_x(0))
    start(gather_c(0))
    stat_sum(1)
    start(stat_copies(2))
    arrive(gather_x(1))
    start(gather_c(1))
    stat_sum(2)
    start(stat_copies(3))
    advantage = reward - stat[3, 0:1] / (nz * nx * 2)
    arrive(gather_c(0))
    attend(0, advantage)
    attend(1, advantage)
    before_c(0)
    arrive(gather_c(1))
    attend(2, advantage)
    before_c(1)
    after_c(0)
    stat_sum(3)
    start(stat_copies(4))
    attend(3, advantage)
    before_c(2)
    after_c(1)
    stat_sum(4)
    unit = 1.0 / stat[5, 8:9]
    weight = advantage * SCALE * unit
    query_gradient(0, weight)
    after_c(2)
    after_x(0)
    query_gradient(1, weight)
    after_x(1)
    query_gradient(2, weight)
    after_x(2)
    query_gradient(3, weight)
    for g in range(KEY_HEADS):
        for i in range(2):
            go_v[i, :, head_cols(g)] = (own_grad[i, :, head_cols(g)] * unit).astype(BF16)
    stores = [
        pltpu.make_async_copy(src, dst, out_sem.at[i])
        for i, (src, dst) in enumerate(
            (
                (gq_v, gq_hbm),
                (go_v.at[0], gok_hbm),
                (go_v.at[1], gov_hbm),
                (gp_v.at[0], gpk_hbm),
                (gp_v.at[1], gpv_hbm),
            )
        )
    ]
    start(stores[0:3])
    for step in range(len(stages)):
        drain(stat_copies(step))
    drain(gather_z())
    for half in range(2):
        drain(gather_x(half))
        drain(gather_c(half))
    after_z(0, unit)
    after_z(1, unit)
    for n in range(len(chunks)):
        drain(reduce_c(n))
        drain(reduce_x(n))
        if n + 1 < len(chunks):
            drain(reduce_z(n))
    after_z(2, unit)
    start(stores[3:5])
    drain(reduce_z(len(chunks) - 1))
    for store in stores:
        store.wait()


def store_kernel(*refs):
    sources, targets, holds = refs[0:5], refs[5:10], refs[10:15]
    in_sem, out_sem = refs[15:17]
    ins = [
        pltpu.make_async_copy(sources[i], holds[i], in_sem.at[i]) for i in range(5)
    ]
    outs = [
        pltpu.make_async_copy(holds[i], targets[i], out_sem.at[i]) for i in range(5)
    ]
    for copy in ins:
        copy.start()
    for i in (1, 2, 3, 4, 0):
        ins[i].wait()
        outs[i].start()
    for copy in outs:
        copy.wait()


def on_device(
    dims,
    queries,
    response_keys,
    response_values,
    prompt_key_rows,
    prompt_value_rows,
    upstream,
    rewards,
    lengths,
):
    nl, ny, nz, nx = dims
    kvh, rows = KEY_HEADS, QUERY_PER_KV * TOKENS
    prompt = nz * nx * 2 * 16
    joined = prompt + TOKENS
    wide, narrow = queries.shape[3], response_keys.shape[3]
    shard = prompt_key_rows.shape[1]
    most = max(dims) - 1
    vmem, sem = pltpu.VMEM, pltpu.SemaphoreType.DMA
    anywhere = pl.BlockSpec(memory_space=pl.ANY)
    scalar = pl.BlockSpec(memory_space=pltpu.SMEM)
    shapes = (
        jax.ShapeDtypeStruct((TOKENS, wide), BF16),
        jax.ShapeDtypeStruct((TOKENS, narrow), BF16),
        jax.ShapeDtypeStruct((TOKENS, narrow), BF16),
        jax.ShapeDtypeStruct((shard, narrow), F32),
        jax.ShapeDtypeStruct((shard, narrow), F32),
    )
    results = pl.pallas_call(
        functools.partial(kernel, dims),
        out_shape=shapes,
        in_specs=[anywhere] * 6 + [scalar] * 2,
        out_specs=[anywhere] * 5,
        scratch_shapes=[
            vmem((TOKENS, wide), BF16),
            vmem((2, TOKENS, narrow), BF16),
            vmem((2, shard, narrow), F32),
            vmem((TOKENS, wide), BF16),
            vmem((TOKENS, wide), BF16),
            vmem((2, TOKENS, narrow), BF16),
            vmem((2, shard, narrow), BF16),
            vmem((kvh, 2, nx, nz, 2, 16, HEAD), BF16),
            vmem((6, 16, 128), F32),
            vmem((5, most, 16, 128), F32),
            vmem((2, TOKENS, narrow), F32),
            vmem((kvh, joined, rows), F32),
            vmem((kvh, joined, rows), F32),
            vmem((kvh, joined, rows), F32),
            vmem((kvh, joined, rows), BF16),
            vmem((kvh, joined, rows), BF16),
            vmem((kvh, 2, nx, nz, 2, 16, HEAD), F32),
            vmem((kvh, nx, nz, 2, 16, HEAD), BF16),
            vmem((kvh, nx, nz, 2, 16, HEAD), BF16),
            vmem((kvh, nx, nz, 2, 16, HEAD), F32),
            vmem((kvh, nx, nz, 2, 16, HEAD), BF16),
            vmem((nx - 1, kvh, nz, 2, 16, HEAD), BF16),
            vmem((kvh, nz, 2, 16, HEAD), BF16),
            vmem((nz - 1, kvh, 2, 16, HEAD), BF16),
            sem((6,)),
            sem((5,)),
            sem((nz - 1,)),
            sem((nz - 1,)),
            sem((2, nx - 1)),
            sem((2, nx - 1)),
            sem((2,)),
            sem((2,)),
            sem((3,)),
            sem((3,)),
            sem((3, nx - 1)),
            sem((3, nx - 1)),
            sem((3, nz - 1)),
            sem((3, nz - 1)),
            sem((5, most)),
            sem((5, most)),
        ],
        compiler_params=pltpu.CompilerParams(
            collective_id=0,
            has_side_effects=True,
            vmem_limit_bytes=VMEM_LIMIT,
        ),
        cost_estimate=pl.CostEstimate(
            flops=1_400_000_000, bytes_accessed=3_000_000, transcendentals=1_400_000
        ),
    )(
        queries[0, 0],
        response_keys[0, 0],
        response_values[0, 0],
        prompt_key_rows[0],
        prompt_value_rows[0],
        upstream[0, 0],
        rewards,
        lengths,
    )
    gq, gok, gov, gpk, gpv = pl.pallas_call(
        store_kernel,
        out_shape=shapes,
        in_specs=[anywhere] * 5,
        out_specs=[anywhere] * 5,
        scratch_shapes=[vmem(x.shape, x.dtype) for x in shapes] + [sem((5,)), sem((5,))],
        compiler_params=pltpu.CompilerParams(vmem_limit_bytes=VMEM_LIMIT),
    )(*results)
    return gq[None, None], gok[None, None], gov[None, None], gpk[None], gpv[None]


def solution(mesh, dims=(4, 4, 4, 4)):
    four = P("group", "resp", None, None)
    three = P("group", "resp", None)
    two = P("group", "resp")
    return jax.shard_map(
        functools.partial(on_device, dims),
        mesh=mesh,
        in_specs=(four, four, four, three, three, four, two, two),
        out_specs=(four, four, four, three, three),
        check_vma=False,
    )
```

```python
import functools

import jax
import jax.numpy as jnp
from jax import lax
from jax.experimental import pallas as pl
from jax.experimental.pallas import tpu as pltpu
from jax.sharding import PartitionSpec as P

MESH = pl.DeviceIdType.MESH
KEY_HEADS = 4
QUERY_PER_KV = 4
HEAD = 128
TOKENS = 128
SCALE = HEAD ** (-0.5)
F32 = jnp.float32
BF16 = jnp.bfloat16
VMEM_LIMIT = 56 * 1024 * 1024


def dot(a, b, a_dim, b_dim):
    return lax.dot_general(
        a, b, (((a_dim,), (b_dim,)), ((), ())), preferred_element_type=F32
    )


def kernel(
    dims,
    q_hbm,
    ok_hbm,
    ov_hbm,
    pk_hbm,
    pv_hbm,
    up_hbm,
    reward_ref,
    length_ref,
    gq_hbm,
    gok_hbm,
    gov_hbm,
    gpk_hbm,
    gpv_hbm,
    gq_v,
    go_v,
    gp_v,
    q_v,
    up_v,
    own_v,
    shard_v,
    kv,
    stat,
    stat_in,
    own_grad,
    s_ref,
    e_ref,
    dp_ref,
    pb_ref,
    ds_ref,
    acc,
    cs,
    rc,
    part,
    xs,
    rx,
    zs,
    rz,
    in_sem,
    out_sem,
    gz_s,
    gz_r,
    gx_s,
    gx_r,
    gc_s,
    gc_r,
    sc_s,
    sc_r,
    sx_s,
    sx_r,
    sz_s,
    sz_r,
    t_s,
    t_r,
):
    nl, ny, nz, nx = dims
    prompt = nz * nx * 2 * 16
    rows = QUERY_PER_KV * TOKENS
    gi, ri = lax.axis_index("group"), lax.axis_index("resp")
    mc = lax.rem(ri, 2)
    mx = lax.rem(lax.div(ri, 2), nx)
    mz = lax.div(ri, 2 * nx)
    my = lax.rem(gi, ny)
    ml = lax.div(gi, ny)

    def device(c=mc, x=mx, z=mz, y=my, l=ml):
        return (l * ny + y, (z * nx + x) * 2 + c)

    def ahead(me, d, n):
        return lax.rem(me + d, n)

    def remote(src, dst, send, recv, to):
        return pltpu.make_async_remote_copy(
            src_ref=src,
            dst_ref=dst,
            send_sem=send,
            recv_sem=recv,
            device_id=to,
            device_id_type=MESH,
        )

    on_core = device(c=1 - mc)
    on_x = [device(x=ahead(mx, d, nx)) for d in range(1, nx)]
    on_z = [device(z=ahead(mz, d, nz)) for d in range(1, nz)]
    on_y = [device(y=ahead(my, d, ny)) for d in range(1, ny)]
    on_l = [device(l=ahead(ml, d, nl)) for d in range(1, nl)]
    partners = [on_core] + on_x + on_z + on_y + on_l
    barrier = pltpu.get_barrier_semaphore()
    for partner in partners:
        pl.semaphore_signal(barrier, inc=1, device_id=partner, device_id_type=MESH)

    loads = [
        pltpu.make_async_copy(src, dst, in_sem.at[i])
        for i, (src, dst) in enumerate(
            (
                (pk_hbm, shard_v.at[0]),
                (pv_hbm, shard_v.at[1]),
                (q_hbm, q_v),
                (ok_hbm, own_v.at[0]),
                (ov_hbm, own_v.at[1]),
                (up_hbm, up_v),
            )
        )
    ]
    for load in loads:
        load.start()

    reward = reward_ref[0, 0]
    length = length_ref[0, 0]
    stat[0, 0:8] = jnp.full((8, 128), reward, F32)
    stat[0, 8:16] = jnp.full((8, 128), length.astype(F32), F32)

    def start(copies):
        for copy in copies:
            copy.start()

    def arrive(copies):
        for copy in copies:
            copy.wait_recv()

    def drain(copies):
        for copy in copies:
            copy.wait_send()

    stages = (on_z, on_x, [on_core], on_y, on_l)

    def stat_copies(step):
        return [
            remote(
                stat.at[step],
                stat_in.at[step, d],
                t_s.at[step, d],
                t_r.at[step, d],
                to,
            )
            for d, to in enumerate(stages[step])
        ]

    def stat_sum(step):
        arrive(stat_copies(step))
        total = stat[step]
        for d in range(len(stages[step])):
            total = total + stat_in[step, d]
        stat[step + 1] = total

    def gather_z():
        mine = kv.at[:, mc, mx, mz]
        return [
            remote(mine, mine, gz_s.at[d], gz_r.at[d], to) for d, to in enumerate(on_z)
        ]

    def gather_x(half):
        mine = kv.at[2 * half : 2 * half + 2, mc, mx]
        return [
            remote(mine, mine, gx_s.at[half, d], gx_r.at[half, d], to)
            for d, to in enumerate(on_x)
        ]

    def gather_c(half):
        mine = kv.at[2 * half : 2 * half + 2, mc]
        return [remote(mine, mine, gc_s.at[half], gc_r.at[half], on_core)]

    chunks = (slice(0, 2), slice(2, 4))

    def reduce_c(n):
        return [
            remote(cs.at[chunks[n]], rc.at[chunks[n]], sc_s.at[n], sc_r.at[n], on_core)
        ]

    def reduce_x(n):
        return [
            remote(
                xs.at[chunks[n], ahead(mx, d + 1, nx)],
                rx.at[d, chunks[n]],
                sx_s.at[n, d],
                sx_r.at[n, d],
                to,
            )
            for d, to in enumerate(on_x)
        ]

    def reduce_z(n):
        return [
            remote(
                zs.at[chunks[n], ahead(mz, d + 1, nz)],
                rz.at[d, chunks[n]],
                sz_s.at[n, d],
                sz_r.at[n, d],
                to,
            )
            for d, to in enumerate(on_z)
        ]

    def before_c(n):
        cs[chunks[n]] = acc[chunks[n], 1 - mc].astype(BF16)
        start(reduce_c(n))

    def after_c(n):
        arrive(reduce_c(n))
        both = acc[chunks[n], mc] + rc[chunks[n]].astype(F32)
        part[chunks[n]] = both
        xs[chunks[n]] = both.astype(BF16)
        start(reduce_x(n))

    def after_x(n):
        arrive(reduce_x(n))
        both = part[chunks[n], mx]
        for d in range(nx - 1):
            both = both + rx[d, chunks[n]].astype(F32)
        part[chunks[n], 0] = both
        zs[chunks[n]] = both.astype(BF16)
        start(reduce_z(n))

    def after_z(n, scale):
        arrive(reduce_z(n))
        both = part[chunks[n], 0, mz]
        for d in range(nz - 1):
            both = both + rz[d, chunks[n]].astype(F32)
        for i, g in enumerate(range(chunks[n].start, chunks[n].stop)):
            gp_v[0, :, head_cols(g)] = both[i, 0] * scale
            gp_v[1, :, head_cols(g)] = both[i, 1] * scale

    def head_cols(g):
        return slice(g * HEAD, (g + 1) * HEAD)

    def query_cols(g, j):
        lower = (g * QUERY_PER_KV + j) * HEAD
        return slice(lower, lower + HEAD)

    def stacked(ref, g):
        return jnp.concatenate(
            [ref[:, query_cols(g, j)] for j in range(QUERY_PER_KV)], axis=0
        )

    def prompt_rows(g, i):
        return kv[g, :, :, :, i].reshape(prompt, HEAD)

    def own_part(g):
        key = lax.broadcasted_iota(jnp.int32, (TOKENS, rows), 0)
        step = lax.broadcasted_iota(jnp.int32, (TOKENS, rows), 1) & (TOKENS - 1)
        scores = dot(own_v[0, :, head_cols(g)], stacked(q_v, g), 1, 1)
        s_ref[g, prompt:] = jnp.where(key <= step, scores, -1e30)
        step = lax.broadcasted_iota(jnp.int32, (TOKENS, HEAD), 0)
        live = jnp.where(step < length, 1.0, 0.0)
        for j in range(QUERY_PER_KV):
            cols = query_cols(g, j)
            up_v[:, cols] = (up_v[:, cols].astype(F32) * live).astype(BF16)
        dp_ref[g, prompt:] = dot(own_v[1, :, head_cols(g)], stacked(up_v, g), 1, 1)

    def attend(g, advantage):
        q_g, grad_out = stacked(q_v, g), stacked(up_v, g)
        s_ref[g, 0:prompt] = dot(prompt_rows(g, 0), q_g, 1, 1)
        dp_ref[g, 0:prompt] = dot(prompt_rows(g, 1), grad_out, 1, 1)
        top = jnp.max(s_ref[g], axis=0, keepdims=True)
        e_ref[g] = jnp.exp((s_ref[g] - top) * SCALE)
        inverse = 1.0 / jnp.sum(e_ref[g], axis=0, keepdims=True)
        pb_ref[g] = (e_ref[g] * inverse).astype(BF16)
        grad_values = advantage * dot(pb_ref[g], grad_out, 1, 0)
        acc[g, :, :, :, 1] = grad_values[0:prompt].reshape(2, nx, nz, 16, HEAD)
        own_grad[1, :, head_cols(g)] = grad_values[prompt:]
        delta = jnp.sum(pb_ref[g].astype(F32) * dp_ref[g], axis=0, keepdims=True)
        ds_ref[g] = ((e_ref[g] * inverse) * (dp_ref[g] - delta)).astype(BF16)
        grad_keys = (advantage * SCALE) * dot(ds_ref[g], q_g, 1, 0)
        acc[g, :, :, :, 0] = grad_keys[0:prompt].reshape(2, nx, nz, 16, HEAD)
        own_grad[0, :, head_cols(g)] = grad_keys[prompt:]

    def query_gradient(g, weight):
        turned = dot(prompt_rows(g, 0), ds_ref[g, 0:prompt], 0, 0) + dot(
            own_v[0, :, head_cols(g)], ds_ref[g, prompt:], 0, 0
        )
        for j in range(QUERY_PER_KV):
            block = turned[:, j * TOKENS : (j + 1) * TOKENS]
            gq_v[:, query_cols(g, j)] = (block.T * weight).astype(BF16)

    loads[0].wait()
    loads[1].wait()
    for g in range(KEY_HEADS):
        kv[g, mc, mx, mz, 0] = shard_v[0, :, head_cols(g)]
        kv[g, mc, mx, mz, 1] = shard_v[1, :, head_cols(g)]
    pl.semaphore_wait(barrier, len(partners))
    start(gather_z())
    start(stat_copies(0))
    for load in loads[2:]:
        load.wait()
    own_part(0)
    own_part(1)
    arrive(gather_z())
    start(gather_x(0))
    start(gather_x(1))
    stat_sum(0)
    start(stat_copies(1))
    own_part(2)
    own_part(3)
    arrive(gather_x(0))
    start(gather_c(0))
    stat_sum(1)
    start(stat_copies(2))
    arrive(gather_x(1))
    start(gather_c(1))
    stat_sum(2)
    start(stat_copies(3))
    advantage = reward - stat[3, 0:1] / (nz * nx * 2)
    arrive(gather_c(0))
    attend(0, advantage)
    attend(1, advantage)
    before_c(0)
    arrive(gather_c(1))
    attend(2, advantage)
    after_c(0)
    stat_sum(3)
    start(stat_copies(4))
    attend(3, advantage)
    before_c(1)
    stat_sum(4)
    unit = 1.0 / stat[5, 8:9]
    weight = advantage * SCALE * unit
    query_gradient(0, weight)
    after_c(1)
    after_x(0)
    query_gradient(1, weight)
    query_gradient(2, weight)
    after_x(1)
    query_gradient(3, weight)
    for g in range(KEY_HEADS):
        for i in range(2):
            go_v[i, :, head_cols(g)] = (own_grad[i, :, head_cols(g)] * unit).astype(BF16)
    stores = [
        pltpu.make_async_copy(src, dst, out_sem.at[i])
        for i, (src, dst) in enumerate(
            (
                (gq_v, gq_hbm),
                (go_v.at[0], gok_hbm),
                (go_v.at[1], gov_hbm),
                (gp_v.at[0], gpk_hbm),
                (gp_v.at[1], gpv_hbm),
            )
        )
    ]
    start(stores[0:3])
    for step in range(len(stages)):
        drain(stat_copies(step))
    drain(gather_z())
    for half in range(2):
        drain(gather_x(half))
        drain(gather_c(half))
    after_z(0, unit)
    for n in range(len(chunks)):
        drain(reduce_c(n))
        drain(reduce_x(n))
        if n + 1 < len(chunks):
            drain(reduce_z(n))
    after_z(1, unit)
    start(stores[3:5])
    drain(reduce_z(len(chunks) - 1))
    for store in stores:
        store.wait()


def store_kernel(*refs):
    sources, targets, holds = refs[0:5], refs[5:10], refs[10:15]
    in_sem, out_sem = refs[15:17]
    ins = [
        pltpu.make_async_copy(sources[i], holds[i], in_sem.at[i]) for i in range(5)
    ]
    outs = [
        pltpu.make_async_copy(holds[i], targets[i], out_sem.at[i]) for i in range(5)
    ]
    for copy in ins:
        copy.start()
    for i in (1, 2, 3, 4, 0):
        ins[i].wait()
        outs[i].start()
    for copy in outs:
        copy.wait()


def on_device(
    dims,
    queries,
    response_keys,
    response_values,
    prompt_key_rows,
    prompt_value_rows,
    upstream,
    rewards,
    lengths,
):
    nl, ny, nz, nx = dims
    kvh, rows = KEY_HEADS, QUERY_PER_KV * TOKENS
    prompt = nz * nx * 2 * 16
    joined = prompt + TOKENS
    wide, narrow = queries.shape[3], response_keys.shape[3]
    shard = prompt_key_rows.shape[1]
    most = max(dims) - 1
    vmem, sem = pltpu.VMEM, pltpu.SemaphoreType.DMA
    anywhere = pl.BlockSpec(memory_space=pl.ANY)
    scalar = pl.BlockSpec(memory_space=pltpu.SMEM)
    shapes = (
        jax.ShapeDtypeStruct((TOKENS, wide), BF16),
        jax.ShapeDtypeStruct((TOKENS, narrow), BF16),
        jax.ShapeDtypeStruct((TOKENS, narrow), BF16),
        jax.ShapeDtypeStruct((shard, narrow), F32),
        jax.ShapeDtypeStruct((shard, narrow), F32),
    )
    results = pl.pallas_call(
        functools.partial(kernel, dims),
        out_shape=shapes,
        in_specs=[anywhere] * 6 + [scalar] * 2,
        out_specs=[anywhere] * 5,
        scratch_shapes=[
            vmem((TOKENS, wide), BF16),
            vmem((2, TOKENS, narrow), BF16),
            vmem((2, shard, narrow), F32),
            vmem((TOKENS, wide), BF16),
            vmem((TOKENS, wide), BF16),
            vmem((2, TOKENS, narrow), BF16),
            vmem((2, shard, narrow), BF16),
            vmem((kvh, 2, nx, nz, 2, 16, HEAD), BF16),
            vmem((6, 16, 128), F32),
            vmem((5, most, 16, 128), F32),
            vmem((2, TOKENS, narrow), F32),
            vmem((kvh, joined, rows), F32),
            vmem((kvh, joined, rows), F32),
            vmem((kvh, joined, rows), F32),
            vmem((kvh, joined, rows), BF16),
            vmem((kvh, joined, rows), BF16),
            vmem((kvh, 2, nx, nz, 2, 16, HEAD), F32),
            vmem((kvh, nx, nz, 2, 16, HEAD), BF16),
            vmem((kvh, nx, nz, 2, 16, HEAD), BF16),
            vmem((kvh, nx, nz, 2, 16, HEAD), F32),
            vmem((kvh, nx, nz, 2, 16, HEAD), BF16),
            vmem((nx - 1, kvh, nz, 2, 16, HEAD), BF16),
            vmem((kvh, nz, 2, 16, HEAD), BF16),
            vmem((nz - 1, kvh, 2, 16, HEAD), BF16),
            sem((6,)),
            sem((5,)),
            sem((nz - 1,)),
            sem((nz - 1,)),
            sem((2, nx - 1)),
            sem((2, nx - 1)),
            sem((2,)),
            sem((2,)),
            sem((2,)),
            sem((2,)),
            sem((2, nx - 1)),
            sem((2, nx - 1)),
            sem((2, nz - 1)),
            sem((2, nz - 1)),
            sem((5, most)),
            sem((5, most)),
        ],
        compiler_params=pltpu.CompilerParams(
            collective_id=0,
            has_side_effects=True,
            vmem_limit_bytes=VMEM_LIMIT,
        ),
        cost_estimate=pl.CostEstimate(
            flops=1_400_000_000, bytes_accessed=3_000_000, transcendentals=1_400_000
        ),
    )(
        queries[0, 0],
        response_keys[0, 0],
        response_values[0, 0],
        prompt_key_rows[0],
        prompt_value_rows[0],
        upstream[0, 0],
        rewards,
        lengths,
    )
    gq, gok, gov, gpk, gpv = pl.pallas_call(
        store_kernel,
        out_shape=shapes,
        in_specs=[anywhere] * 5,
        out_specs=[anywhere] * 5,
        scratch_shapes=[vmem(x.shape, x.dtype) for x in shapes] + [sem((5,)), sem((5,))],
        compiler_params=pltpu.CompilerParams(vmem_limit_bytes=VMEM_LIMIT),
    )(*results)
    return gq[None, None], gok[None, None], gov[None, None], gpk[None], gpv[None]


def solution(mesh, dims=(4, 4, 4, 4)):
    four = P("group", "resp", None, None)
    three = P("group", "resp", None)
    two = P("group", "resp")
    return jax.shard_map(
        functools.partial(on_device, dims),
        mesh=mesh,
        in_specs=(four, four, four, three, three, four, two, two),
        out_specs=(four, four, four, three, three),
        check_vma=False,
    )
```
